256 devices in a mesh: cube: 64 (over y, z_lo, x, core), panel: 4 (over z_hi).
Axes of the slice: x: 4, y: 4, z: 8 (z_hi: 4, z_lo: 2; z = z_hi * 2 + z_lo), core: 2. Of those that a mesh axis runs over, the one named last changes fastest.
Arguments:
- leaf_updates: float32 [32768, 4096], P(('cube', 'panel')), as said below
- extend_maps: int32 [14, 4096], replicated, may hold values from 0 to 4607, as said below
- front_diagonal: float32 [7, 4608], replicated, may hold values from 0.5 to 2
- pivot_order: int32 [512], replicated, may hold values from 0 to 511, each once
- coupling_rows: bfloat16 [65536, 4608], P(('cube', 'panel')), may hold values from -0.1796875 to 0.1796875
- coupling_owner: int32 [65536, 1], P(('cube', 'panel')), may hold values from 0 to 255; in each aligned block of 256 rows (0 to 255, 256 to 511, ...) at most 2 rows name the same one
- coupling_slot: int32 [65536], P(('cube', 'panel')), may hold values from 0 to 15
Outputs:
- root_factor: bfloat16 [4096, 512], P(('cube', 'panel'))
- root_update: float32 [4096, 4096], P(('cube', 'panel'))
The draws below stay inside these ranges and needn't reach their ends.
Inputs may be any that keep to these rules, and one draw needn't show every extreme that they name: leaf_updates: each of the 8 blocks of 4096 rows is symmetric positive definite. `extend_maps`: each row names distinct indices. For a child h of its parent (h = row parity) at merge level j, with g = 8 * 2 ** j, r = 4096 // (2 * g * 4) and k = 512 // (2 * g * 4): its indices fall in aligned blocks of 2 * r, block number s * 4 + p; the first r of a block name front indices of parent block (h * g + s) * 4 + p, the other r those of parent block ((1 - h) * g + s) * 4 + p, where parent block u holds pivots u * k to u * k + k - 1 and indices 512 + u * r to 512 + u * r + r - 1. `coupling_owner`: within the rows of one device, no owner is named by more than 2 rows.
All inputs are finite; a program needn't handle non-finite values.
Results may differ from the reference program's by a relative error of at most 0.0065.
Values may be sent and summed in bfloat16 or wider, within the bound.
A program may use at most 128 MiB of HBM per device.

```python
import math
import jax
import jax.numpy as jnp
import numpy as np
from jax import lax

U = 4096
K = 512
CAP = 2
F = 4608
QLEAF = 8
PANELS = 4
UDR = 16
M = 256
ROUTED = 65536
N_CUBE = 64
N_PANEL = 4


def draw_leaf_updates(key, part):
    key = jax.random.fold_in(key, 5)
    basis_key = jax.random.fold_in(key, 1)
    diag_key = jax.random.fold_in(key, 2)
    inner = U // 4
    basis = jax.random.normal(basis_key, (8, U, inner), jnp.float32)
    gram = jnp.einsum('lir,ljr->lij', basis, basis, precision=lax.Precision.HIGHEST) / inner
    diagonal = jnp.exp(jax.random.uniform(diag_key, (8, U), jnp.float32, -0.7, 0.7))
    gram = gram + diagonal[:, :, None] * jnp.eye(U, dtype=jnp.float32)[None, :, :]
    gram = gram + 0.05
    return gram.reshape(8 * U, U)


def draw_extend_maps(key, part):
    key = jax.random.fold_in(key, 11)
    level_rows = []
    for merge_level in range(3):
        kids = 8 // 2 ** merge_level
        child_group = QLEAF * 2 ** merge_level
        upd_rows = U // (2 * child_group * PANELS)
        piv_rows = K // (2 * child_group * PANELS)
        slot_count = upd_rows + piv_rows
        blocks = child_group * PANELS
        level_key = jax.random.fold_in(key, merge_level)
        many_keys = jax.random.split(level_key, kids * blocks * 2)
        chosen = jax.vmap(lambda one_key: jax.random.permutation(one_key, slot_count))(many_keys)[:, :upd_rows]
        chosen = chosen.reshape(kids, blocks, 2, upd_rows).astype(jnp.int32)
        child_side = (jnp.arange(kids, dtype=jnp.int32) % 2)[:, None, None, None]
        block_ids = jnp.arange(blocks, dtype=jnp.int32)[None, :, None, None]
        lower_pos = block_ids // PANELS
        panel_pos = block_ids % PANELS
        halves = jnp.arange(2, dtype=jnp.int32)[None, None, :, None]
        target_side = jnp.where(halves == 0, child_side, 1 - child_side)
        parent_block = (target_side * child_group + lower_pos) * PANELS + panel_pos
        indices = jnp.where(chosen < piv_rows, parent_block * piv_rows + chosen, K + parent_block * upd_rows + chosen - piv_rows)
        level_rows.append(indices.reshape(kids, U))
    return jnp.concatenate(level_rows, 0).astype(jnp.int32)


def plant(entries, stream_key, smallest, top_value):
    dims = entries.shape
    place = [jax.random.randint(jax.random.fold_in(stream_key, axis), (), 0, dims[axis]) for axis in range(len(dims))]
    entries = entries.at[tuple(place)].set(smallest)
    longest = dims.index(max(dims))
    place[longest] = (place[longest] + 1) % dims[longest]
    return entries.at[tuple(place)].set(top_value)


def levels(stream_key, shape, cuts, smallest, high):
    def one(axis_at, shards_of):
        steps = jax.random.uniform(jax.random.fold_in(jax.random.fold_in(stream_key, 6), axis_at), (shards_of,), jnp.float32, smallest / len(cuts), high / len(cuts))
        return jnp.repeat(jnp.exp(steps), shape[axis_at] // shards_of).reshape((-1,) + (1,) * (len(shape) - axis_at - 1))

    loudness = one(*cuts[0])
    for cut in cuts[1:]:
        loudness = loudness * one(*cut)
    return loudness


def routed_block(stream_key, own, number, rows, count, top, reach, skew):
    ranking = jax.random.permutation(stream_key, count)
    packed, usual = portions_of(count, rows * top, reach, skew, True), portions_of(count, rows * top, reach, skew, False)
    places = jnp.arange(count)

    def named(sizes, offset_by):
        used = int((sizes > 0).sum())
        fixed = max(1, used // 4)
        shifted = fixed + (places - fixed + offset_by * (used - fixed)) % max(1, count - fixed)
        return jnp.zeros((count,), jnp.int32).at[ranking[jnp.where(places < fixed, places, shifted)]].set(jnp.asarray(sizes, jnp.int32))

    sizes = jnp.where(number % 4 == 0, named(packed, number // 4), named(usual, number - number // 4 - 1))
    mixed = jax.random.permutation(jax.random.fold_in(own, 3), count)
    giver, sink = mixed[0:count // 2 * 2:2], mixed[1:count // 2 * 2:2]
    margin = jnp.minimum(sizes[giver] - 1, reach - sizes[sink]) // 2
    margin = jnp.where((giver == ranking[0]) | (sink == ranking[0]) | (sizes[sink] == 0), 0, jnp.maximum(margin, 0))
    shifted = jax.random.randint(jax.random.fold_in(own, 4), (count // 2,), 0, 1 << 20) % (margin + 1)
    sizes = sizes.at[giver].add(-shifted).at[sink].add(shifted)
    members = jnp.searchsorted(jnp.cumsum(sizes), jnp.arange(rows * top), side="right").astype(jnp.int32)
    grid = members.reshape(top, rows).T
    grid = grid[jax.random.permutation(jax.random.fold_in(own, 1), rows)]
    offset_by = jax.random.randint(jax.random.fold_in(own, 2), (rows, 1), 0, top)
    return jnp.take_along_axis(grid, (jnp.arange(top)[None, :] + offset_by) % top, axis=1)


def portions_of(number_of, total, limit, skew, full):
    portions = [(1 << 20) // math.isqrt(standing ** skew) + 1 for standing in range(1, number_of + 1)]
    largest = limit if full else min(limit, max(-(-total // number_of), total * portions[0] // sum(portions)))
    least = 1 if total - largest >= number_of - 1 else 0
    counts, surplus = [largest] + [least] * (number_of - 1), total - largest - least * (number_of - 1)
    while surplus > 0:
        free = [i for i in range(1, number_of) if counts[i] < largest] or [i for i in range(1, number_of) if counts[i] < limit]
        mass, remaining = sum([portions[i] for i in free]), surplus
        for i in free:
            extra = min(limit - counts[i], max(1, remaining * portions[i] // mass), surplus)
            counts[i] = counts[i] + extra
            surplus = surplus - extra
    return np.array(counts)


def scatter_about(key, dims, deviation, most, cuts=(), kind=jnp.bfloat16):
    loudness = levels(key, dims, cuts, -0.22, 0.18) if cuts else 1.0
    values = jax.random.normal(key, dims, jnp.float32) * deviation * loudness
    return jnp.minimum(jnp.maximum(values, -most), most).astype(kind)


def setup_inputs(seed: int = 0) -> dict:
    key_list = jax.random.split(jax.random.key(seed), 8)
    leaf_updates = draw_leaf_updates(jax.random.fold_in(key_list[7], 71), 0)
    extend_maps = draw_extend_maps(jax.random.fold_in(key_list[7], 71), 0)
    front_diagonal = jnp.clip(jnp.exp(jax.random.uniform(key_list[2], (7, F), jnp.float32, math.log(0.5), math.log(2.0))), 0.5, 2.0)
    pivot_order = jax.random.permutation(key_list[3], K).astype(jnp.int32)
    coupling_rows = scatter_about(key_list[4], (ROUTED, F), 0.03, 0.1796875, ((0, 256),))
    coupling_owner_keys = jax.random.split(jax.random.fold_in(key_list[5], 1), ROUTED // M)
    coupling_owner_turns = jax.random.permutation(jax.random.fold_in(key_list[5], 3), ROUTED // M)
    coupling_owner = jax.vmap(lambda own, number: routed_block(jax.random.fold_in(key_list[5], 2), own, number, M, N_CUBE * N_PANEL, 1, CAP, 2))(coupling_owner_keys, coupling_owner_turns).reshape((ROUTED, 1))
    coupling_slot = plant(jax.random.randint(key_list[6], (ROUTED,), 0, UDR), jax.random.fold_in(key_list[6], 1), 0, UDR - 1).astype(jnp.int32)
    return {"leaf_updates": leaf_updates, "extend_maps": extend_maps, "front_diagonal": front_diagonal, "pivot_order": pivot_order, "coupling_rows": coupling_rows, "coupling_owner": coupling_owner, "coupling_slot": coupling_slot}


def assemble(child_one, child_two, map_one, map_two, diagonal):
    front = jnp.zeros((F, F), jnp.float32)
    front = front.at[map_one[:, None], map_one[None, :]].add(child_one)
    front = front.at[map_two[:, None], map_two[None, :]].add(child_two)
    indices = jnp.arange(F, dtype=jnp.int32)
    return front.at[indices, indices].add(diagonal)

def eliminate(front, ordering):
    pivot_block = jnp.take(jnp.take(front[:K, :K], ordering, axis=0), ordering, axis=1)
    chol_lower = jnp.linalg.cholesky(pivot_block)
    coupled = jnp.take(front[K:, :K], ordering, axis=1)
    factor = lax.linalg.triangular_solve(chol_lower, coupled, left_side=False, lower=True, transpose_a=True).astype(jnp.bfloat16)
    product = lax.dot_general(factor.astype(jnp.float32), factor.astype(jnp.float32), (((1,), (1,)), ((), ())), preferred_element_type=jnp.float32)
    return (factor, front[K:, K:] - product)

def reference(leaf_updates, extend_maps, front_diagonal, pivot_order, coupling_rows, coupling_owner, coupling_slot):
    children = [leaf_updates[index * U:(index + 1) * U] for index in range(8)]
    natural_order = jnp.arange(K, dtype=jnp.int32)
    map_base = 0
    diag_base = 0
    factor = None
    for merge_level in range(3):
        updates = []
        for front_at in range(len(children) // 2):
            front = assemble(children[2 * front_at], children[2 * front_at + 1], extend_maps[map_base + 2 * front_at], extend_maps[map_base + 2 * front_at + 1], front_diagonal[diag_base + front_at])
            ordering = natural_order
            if merge_level == 2:
                rows_at = K + coupling_owner[:, 0] * UDR + coupling_slot
                front = front.at[rows_at].add(coupling_rows.astype(jnp.float32))
                ordering = pivot_order
            factor, update = eliminate(front, ordering)
            updates.append(update)
        map_base += len(children)
        diag_base += len(children) // 2
        children = updates
    return (factor, children[0])
```

```python
import functools
import jax
import jax.numpy as jnp
from jax import lax
from jax.experimental import pallas as pl
from jax.experimental.pallas import tpu as pltpu
from jax.sharding import PartitionSpec as P

CAP = 2
K = 512
U = 4096
PANELS = 4
f32, bf16, i32 = jnp.float32, jnp.bfloat16, jnp.int32
VMEM = pl.BlockSpec(memory_space=pltpu.VMEM)


def split(x):
    hi = x.astype(bf16)
    return hi, (x - hi.astype(f32)).astype(bf16)

def mm(x, y, dims):
    xh, xl = split(x); yh, yl = split(y)
    d = functools.partial(lax.dot_general, dimension_numbers=(dims, ((), ())), preferred_element_type=f32)
    return d(xh, yh) + (d(xh, yl) + d(xl, yh))

def diag_inverse(V, ahead=2):
    V = list(V)
    lane = lax.broadcasted_iota(jnp.int32, (8, 128), 1)
    sub = lax.broadcasted_iota(jnp.int32, (8, 128), 0)
    below = [sub > i for i in range(8)]
    scale = []
    for g in range(8):
        p0, j0 = 2 * g, 16 * g
        win = [q for q in range(p0, min(p0 + 2 + ahead, 16))]
        B = {(k, q): jnp.broadcast_to(V[q][:, j0+k:j0+k+1], (8, 128)) for k in range(16) for q in win}
        dinv = [None, None]
        for i in range(16):
            s, ii = divmod(i, 8)
            ps = p0 + s
            j = j0 + i
            inv = 1.0 / jnp.broadcast_to(B[i, ps][ii:ii+1, :], (8, 128))
            dinv[s] = inv if ii == 0 else jnp.where(below[ii-1], inv, dinv[s])
            at = lane == j
            row = jnp.where(at, 1.0, jnp.broadcast_to(V[ps][ii:ii+1, :], (8, 128)))
            splats = {k: jnp.broadcast_to(B[k, ps][ii:ii+1, :], (8, 128)) for k in range(i+1, 16)}
            for q in win:
                if q < ps or (q == ps and ii == 7): continue
                m = B[i, q] * inv
                if q == ps:
                    m = jnp.where(below[ii], m, 0.0)
                    z = jnp.where(at & below[ii], 0.0, V[q])
                else:
                    z = jnp.where(at, 0.0, V[q])
                V[q] = z - m * row
                for k in range(i+1, 16):
                    B[k, q] = B[k, q] - m * splats[k]
        scale += dinv
        rest = range(p0 + 2 + ahead, 16)
        if len(rest):
            G, Q = [], []
            for s in range(2):
                r = sub + (j0 + 8 * s)
                v = V[p0 + s]
                Q.append(v * dinv[s])
                inwin = (lane >= j0) & (lane < j0 + 16)
                G.append(jnp.where(inwin, jnp.where(lane < r, v, jnp.where(lane == r, 1.0, 0.0)), v))
            Gc, Qc = jnp.concatenate(G, 0), jnp.concatenate(Q, 0)
            gh, gl = split(Gc); qh, ql = split(Qc)
            upd = lax.dot_general(jnp.concatenate([qh, qh, ql], 0), jnp.concatenate([gh, gl, gh], 0),
                                  (((0,), (0,)), ((), ())), preferred_element_type=f32)
            zw = (lane >= j0) & (lane < j0 + 16)
            for q in rest:
                V[q] = jnp.where(zw, 0.0, V[q]) - upd[8*q:8*q+8]
    out = []
    for p in range(16):
        r = sub + 8 * p
        s = jnp.sqrt(scale[p])
        out.append(jnp.where(lane < r, V[p] * s, jnp.where(lane == r, s, 0.0)))
    return out


def place(level):
    group = 16 << level
    cube_at = lax.axis_index("cube")
    position = lax.rem(cube_at, group)
    return group, position, cube_at // group, position // (group // 2)


def assemble_kernel(level, *refs):
    maps, diag, mine, other = refs[:4]
    extra = refs[4] if level == 2 else None
    piv_out, coupled_out, upd_out, map_row, diag_row = refs[-5:]
    group, position, front_at, side = place(level)
    panel_at = lax.axis_index("panel")
    r = U // (group * PANELS)
    k = K // (group * PANELS)
    map_base = (0, 8, 12)[level]
    diag_base = (0, 4, 6)[level]
    block = lax.rem(position, group // 2) * PANELS + panel_at
    parent = position * PANELS + panel_at
    map_row[0:1, :] = maps[pl.ds(map_base + 2 * front_at + side, 1), :]
    map_row[1:2, :] = maps[pl.ds(map_base + 2 * front_at + 1 - side, 1), :]
    diag_row[0:1, :] = diag[pl.ds(diag_base + front_at, 1), :]
    lane = lax.broadcasted_iota(i32, (1, 128), 1)
    height = 16 + r

    def row_choice(half):
        start = block * (2 * r)
        tile = map_row[half:half + 1, pl.ds(pl.multiple_of(start // 128 * 128, 128), 128)]
        shift = lax.rem(128 - lax.rem(start + half * r, 128), 128)
        t = pltpu.roll(jnp.broadcast_to(tile, (8, 128)), shift, 1)[:1, :r]
        slot = jnp.where(t < K, t - parent * k, 16 + t - K - parent * r)
        rows = lax.broadcasted_iota(i32, (height, r), 0)
        return (rows == slot).astype(f32).astype(bf16)

    sel = (row_choice(0), row_choice(1))
    sides = (side, 1 - side)
    spread = lax.broadcasted_iota(i32, (128, 256), 0)
    piv_acc = [None, None]
    out_rows = lax.broadcasted_iota(i32, (height, 128), 0)
    upd_row_id = parent * r + out_rows - 16
    piv_row_id = parent * k + out_rows
    for c in range(16):
        xs, ss = [], []
        for which, ref in enumerate((mine, other)):
            x = ref[:, c * 256:(c + 1) * 256]
            hi, lo = split(x)
            pick = lambda y: jnp.dot(sel[which], y, preferred_element_type=f32).astype(bf16)
            xs.append(jnp.concatenate([pick(hi), pick(lo)], axis=0))
            m = map_row[which:which + 1, c * 256:(c + 1) * 256]
            onehots = [
                spread == m - (K + s * (U // 2) + c * 128) for s in sides
            ] + [spread == m - (s * (K // 2) + c // 8 * 128) for s in sides]
            ss.append(jnp.concatenate([o.astype(f32).astype(bf16) for o in onehots], axis=0))
        res = lax.dot_general(
            jnp.concatenate(xs, axis=1), jnp.concatenate(ss, axis=1),
            (((1,), (1,)), ((), ())), preferred_element_type=f32,
        )
        res = res[:height] + res[height:]
        upd_col = side * (U // 2) + c * 128 + lane
        d = diag_row[0:1, pl.ds(pl.multiple_of(K + side * (U // 2) + c * 128, 128), 128)]
        own = res[:, :128] + jnp.where(upd_row_id == upd_col, d, 0.0)
        for at, tile in ((side, own), (1 - side, res[:, 128:256])):
            cols = pl.ds(pl.multiple_of(at * (U // 2) + c * 128, 128), 128)
            value = tile[16:]
            if extra is not None:
                value += extra[:, pl.ds(pl.multiple_of(K + at * (U // 2) + c * 128, 128), 128)]
            upd_out[:, cols] = value
        for n in range(2):
            part = res[:, 256 + n * 128:384 + n * 128]
            piv_acc[n] = part if c % 8 == 0 else piv_acc[n] + part
        if c % 8 == 7:
            half = c // 8
            col = side * (K // 2) + half * 128 + lane
            d = diag_row[0:1, pl.ds(pl.multiple_of(side * (K // 2) + half * 128, 128), 128)]
            piv_acc[0] += jnp.where((piv_row_id == col) & (out_rows < 16), d, 0.0)
            for n, at in enumerate((side, 1 - side)):
                cols = pl.ds(pl.multiple_of(at * (K // 2) + half * 128, 128), 128)
                value = piv_acc[n][16:]
                if extra is not None:
                    value += extra[:, cols]
                coupled_out[:, cols] = value
                piv_out[pl.ds(2 * at + half, k, stride=4), :] = piv_acc[n][:k]


def assemble(level, maps, diag, mine, other, extra):
    r = mine.shape[0]
    k = r // 8
    ins = (maps, diag, mine, other) + ((extra,) if level == 2 else ())
    return pl.pallas_call(
        functools.partial(assemble_kernel, level),
        out_shape=(
            jax.ShapeDtypeStruct((4 * k, 128), f32),
            jax.ShapeDtypeStruct((r, K), f32),
            jax.ShapeDtypeStruct((r, U), f32),
        ),
        in_specs=[VMEM] * len(ins),
        out_specs=(VMEM,) * 3,
        scratch_shapes=[pltpu.VMEM((8, U), i32), pltpu.VMEM((8, U + K), f32)],
        compiler_params=pltpu.CompilerParams(vmem_limit_bytes=40 * 2**20),
        name="assemble%d" % level,
    )(*ins)


def factor_kernel(level, *refs):
    pivots, coupled = refs[:2]
    out, w = refs[-2:]
    r = coupled.shape[0]
    n = K
    ct = coupled[...]
    if level == 2:
        order = refs[2]
        move = (lax.broadcasted_iota(i32, (n, n), 0) == order[...]).astype(f32).astype(bf16)
        ch, cl = split(ct)
        ct = jnp.dot(ch, move, preferred_element_type=f32) + jnp.dot(cl, move, preferred_element_type=f32)
        a = jnp.concatenate([pivots[pl.ds(c, n, stride=4), :] for c in range(4)], axis=1)
        ah, al = split(a)
        for part, source in enumerate((ah, al)):
            cols = jnp.dot(source, move, preferred_element_type=f32).astype(bf16)
            both = lax.dot_general(move, cols, (((0,), (0,)), ((), ())), preferred_element_type=f32)
            if part == 0:
                w[:, :n] = both
            else:
                w[:, :n] += both
    else:
        for c in range(4):
            w[:, c * 128:(c + 1) * 128] = pivots[pl.ds(c, n, stride=4), :]
    if r < 128:
        ct = jnp.concatenate([ct, jnp.zeros((128 - r, n), f32)], axis=0)
    w[:, n:] = ct.T
    blocks = n // 128
    for b in range(blocks):
        lo = b * 128
        rows = [w[lo + 8 * p: lo + 8 * p + 8, lo:lo + 128] for p in range(16)]
        inverse = jnp.concatenate(diag_inverse(rows), axis=0)
        solved = mm(inverse, w[lo:lo + 128, lo + 128:], ((1,), (0,)))
        for later in range(b + 1, blocks):
            off = (later - b - 1) * 128
            w[later * 128:(later + 1) * 128, later * 128:] -= mm(
                solved[:, off:off + 128], solved[:, off:], ((0,), (0,))
            )
        out[:, lo:lo + 128] = solved[:, n - lo - 128:].T[:r].astype(bf16)


def make_factor(level, pivots, coupled, order):
    r = coupled.shape[0]
    ins = (pivots, coupled) + ((order,) if level == 2 else ())
    return pl.pallas_call(
        functools.partial(factor_kernel, level),
        out_shape=jax.ShapeDtypeStruct((r, K), bf16),
        in_specs=[VMEM] * len(ins),
        out_specs=VMEM,
        scratch_shapes=[pltpu.VMEM((K, K + 128), f32)],
        compiler_params=pltpu.CompilerParams(vmem_limit_bytes=32 * 2**20),
        name="factor%d" % level,
    )(*ins)


def gather_kernel(ysize, x_ref, out, send_sem, recv_sem, local_sem):
    cube_at = lax.axis_index("cube")
    zh = lax.axis_index("panel")
    core = lax.rem(cube_at, 2)
    x = lax.rem(cube_at // 2, 4)
    zl = lax.rem(cube_at // 8, 2)
    yfull = cube_at // 16
    y = lax.rem(yfull, ysize)
    ybase = yfull - y

    def target(y, zl, x, core, zh):
        return {"cube": (ybase + y) * 16 + zl * 8 + x * 2 + core, "panel": zh}

    def shifted(v, d, size):
        return lax.rem(v + d, size)

    z_peers = [
        target(y, shifted(zl, a, 2), x, core, shifted(zh, b, 4))
        for a in range(2) for b in range(4) if a + b
    ]
    x_peers = [target(y, zl, shifted(x, d, 4), core, zh) for d in range(1, 4)]
    y_peers = [target(shifted(y, d, ysize), zl, x, core, zh) for d in range(1, ysize)]
    core_peers = [target(y, zl, x, 1 - core, zh)]
    stages = [
        (z_peers, out.at[y, zl, x, core, zh]),
        (x_peers, out.at[y, :, x, core]),
        (y_peers, out.at[y, :, :, core]),
        (core_peers, out.at[:, :, :, core]),
    ]
    everyone = z_peers + x_peers + y_peers + core_peers
    keep = pltpu.make_async_copy(x_ref, out.at[y, zl, x, core, zh], local_sem)
    keep.start()
    barrier = pltpu.get_barrier_semaphore()
    for peer in everyone:
        pl.semaphore_signal(barrier, inc=1, device_id=peer, device_id_type=pl.DeviceIdType.MESH)
    pl.semaphore_wait(barrier, len(everyone))
    keep.wait()
    number = 0
    sent = []
    for peers, part in stages:
        copies = []
        for peer in peers:
            copies.append(pltpu.make_async_remote_copy(
                src_ref=part, dst_ref=part, send_sem=send_sem.at[number], recv_sem=recv_sem.at[number],
                device_id=peer, device_id_type=pl.DeviceIdType.MESH,
            ))
            number += 1
        for copy in copies:
            copy.start()
        for copy in copies:
            copy.wait_recv()
        sent += copies
    for copy in sent:
        copy.wait_send()


def gather(level, piece, ident):
    ysize = 1 << level
    rows, cols = piece.shape
    count = 7 + 3 + ysize - 1 + 1
    out = pl.pallas_call(
        functools.partial(gather_kernel, ysize),
        out_shape=jax.ShapeDtypeStruct((ysize, 2, 4, 2, 4, rows, cols), piece.dtype),
        in_specs=[VMEM],
        out_specs=VMEM,
        scratch_shapes=[
            pltpu.SemaphoreType.DMA((count,)), pltpu.SemaphoreType.DMA((count,)),
            pltpu.SemaphoreType.DMA(()),
        ],
        compiler_params=pltpu.CompilerParams(
            collective_id=ident, has_side_effects=True, vmem_limit_bytes=32 * 2**20
        ),
        name="gather%d" % ident,
    )(piece)
    return out.reshape(-1, cols)


def from_partner(shard, stride):
    return lax.ppermute(shard, "cube", [(i, i ^ 1 << stride) for i in range(64)])


def route_rows(coupling_rows, coupling_owner, coupling_slot):
    cubes, panels, root_rows = 64, PANELS, 16
    owners = coupling_owner[:, 0]
    owner_count = cubes * panels
    owner_hits = (owners[:, None] == jnp.arange(owner_count, dtype=i32)[None, :]).astype(i32)
    earlier = jnp.sum((jnp.cumsum(owner_hits, axis=0) - owner_hits) * owner_hits, axis=1)
    target = owners * CAP + earlier
    row_width = coupling_rows.shape[1]
    choose = (target[None, :] == jnp.arange(owner_count * CAP, dtype=i32)[:, None]).astype(bf16)
    marks = (coupling_slot[:, None] == jnp.arange(root_rows, dtype=i32)[None, :]).astype(bf16)
    outgoing = jnp.dot(choose, coupling_rows, preferred_element_type=f32).astype(bf16)
    labels = jnp.dot(choose, marks, preferred_element_type=f32).astype(bf16)
    outgoing = outgoing.reshape(cubes, panels, CAP, row_width)
    labels = labels.reshape(cubes, panels, CAP, root_rows)

    def spread(v):
        v = lax.all_to_all(v, "cube", split_axis=0, concat_axis=0, tiled=True)
        return lax.all_to_all(v, "panel", split_axis=1, concat_axis=1, tiled=True)

    return jnp.einsum("abcr,abcf->rf", spread(labels), spread(outgoing), preferred_element_type=f32)


def body(leaf_updates, extend_maps, front_diagonal, pivot_order, coupling_rows, coupling_owner, coupling_slot):
    assembly = route_rows(coupling_rows, coupling_owner, coupling_slot)
    children = leaf_updates
    order = pivot_order.reshape(1, K)
    for level in range(3):
        r = children.shape[0] // 2
        incoming = from_partner(children[r:], 3 + level)
        piece, coupled, update_rows = assemble(
            level, extend_maps, front_diagonal, children[:r], incoming, assembly
        )
        pivots = gather(level, piece, 2 * level)
        factor = make_factor(level, pivots, coupled, order)
        collected = gather(level, factor, 2 * level + 1)
        product = lax.dot_general(
            factor, collected, (((1,), (1,)), ((), ())), preferred_element_type=f32
        )
        children = update_rows - product
    return (factor, children)


def solution(mesh):
    return jax.shard_map(
        body,
        mesh=mesh,
        in_specs=(
            P(("cube", "panel"), None), P(), P(), P(),
            P(("cube", "panel"), None), P(("cube", "panel"), None), P(("cube", "panel")),
        ),
        out_specs=(P(("cube", "panel"), None), P(("cube", "panel"), None)),
        check_vma=False,
    )
```

```python
import functools
import jax
import jax.numpy as jnp
from jax import lax
from jax.experimental import pallas as pl
from jax.experimental.pallas import tpu as pltpu
from jax.sharding import PartitionSpec as P

CAP = 2
K = 512
U = 4096
PANELS = 4
f32, bf16, i32 = jnp.float32, jnp.bfloat16, jnp.int32
VMEM = pl.BlockSpec(memory_space=pltpu.VMEM)


def split(x):
    hi = x.astype(bf16)
    return hi, (x - hi.astype(f32)).astype(bf16)

def mm(x, y, dims):
    xh, xl = split(x); yh, yl = split(y)
    d = functools.partial(lax.dot_general, dimension_numbers=(dims, ((), ())), preferred_element_type=f32)
    return d(xh, yh) + (d(xh, yl) + d(xl, yh))

def diag_inverse(V, ahead=2):
    V = list(V)
    lane = lax.broadcasted_iota(jnp.int32, (8, 128), 1)
    sub = lax.broadcasted_iota(jnp.int32, (8, 128), 0)
    below = [sub > i for i in range(8)]
    scale = []
    for g in range(8):
        p0, j0 = 2 * g, 16 * g
        win = [q for q in range(p0, min(p0 + 2 + ahead, 16))]
        B = {(k, q): jnp.broadcast_to(V[q][:, j0+k:j0+k+1], (8, 128)) for k in range(16) for q in win}
        dinv = [None, None]
        for i in range(16):
            s, ii = divmod(i, 8)
            ps = p0 + s
            j = j0 + i
            inv = 1.0 / jnp.broadcast_to(B[i, ps][ii:ii+1, :], (8, 128))
            dinv[s] = inv if ii == 0 else jnp.where(below[ii-1], inv, dinv[s])
            at = lane == j
            row = jnp.where(at, 1.0, jnp.broadcast_to(V[ps][ii:ii+1, :], (8, 128)))
            splats = {k: jnp.broadcast_to(B[k, ps][ii:ii+1, :], (8, 128)) for k in range(i+1, 16)}
            for q in win:
                if q < ps or (q == ps and ii == 7): continue
                m = B[i, q] * inv
                if q == ps:
                    m = jnp.where(below[ii], m, 0.0)
                    z = jnp.where(at & below[ii], 0.0, V[q])
                else:
                    z = jnp.where(at, 0.0, V[q])
                V[q] = z - m * row
                for k in range(i+1, 16):
                    B[k, q] = B[k, q] - m * splats[k]
        scale += dinv
        rest = range(p0 + 2 + ahead, 16)
        if len(rest):
            G, Q = [], []
            for s in range(2):
                r = sub + (j0 + 8 * s)
                v = V[p0 + s]
                Q.append(v * dinv[s])
                inwin = (lane >= j0) & (lane < j0 + 16)
                G.append(jnp.where(inwin, jnp.where(lane < r, v, jnp.where(lane == r, 1.0, 0.0)), v))
            Gc, Qc = jnp.concatenate(G, 0), jnp.concatenate(Q, 0)
            gh, gl = split(Gc); qh, ql = split(Qc)
            upd = lax.dot_general(jnp.concatenate([qh, qh, ql], 0), jnp.concatenate([gh, gl, gh], 0),
                                  (((0,), (0,)), ((), ())), preferred_element_type=f32)
            zw = (lane >= j0) & (lane < j0 + 16)
            for q in rest:
                V[q] = jnp.where(zw, 0.0, V[q]) - upd[8*q:8*q+8]
    out = []
    for p in range(16):
        r = sub + 8 * p
        s = jnp.sqrt(scale[p])
        out.append(jnp.where(lane < r, V[p] * s, jnp.where(lane == r, s, 0.0)))
    return out


def place(level):
    group = 16 << level
    cube_at = lax.axis_index("cube")
    position = lax.rem(cube_at, group)
    return group, position, cube_at // group, position // (group // 2)


def assemble_kernel(level, *refs):
    maps, diag, mine, other = refs[:4]
    extra = refs[4] if level == 2 else None
    piv_out, coupled_out, upd_out, map_row, diag_row = refs[-5:]
    group, position, front_at, side = place(level)
    panel_at = lax.axis_index("panel")
    r = U // (group * PANELS)
    k = K // (group * PANELS)
    map_base = (0, 8, 12)[level]
    diag_base = (0, 4, 6)[level]
    block = lax.rem(position, group // 2) * PANELS + panel_at
    parent = position * PANELS + panel_at
    map_row[0:1, :] = maps[pl.ds(map_base + 2 * front_at + side, 1), :]
    map_row[1:2, :] = maps[pl.ds(map_base + 2 * front_at + 1 - side, 1), :]
    diag_row[0:1, :] = diag[pl.ds(diag_base + front_at, 1), :]
    lane = lax.broadcasted_iota(i32, (1, 128), 1)
    height = 16 + r

    def row_choice(half):
        start = block * (2 * r)
        tile = map_row[half:half + 1, pl.ds(pl.multiple_of(start // 128 * 128, 128), 128)]
        shift = lax.rem(128 - lax.rem(start + half * r, 128), 128)
        t = pltpu.roll(jnp.broadcast_to(tile, (8, 128)), shift, 1)[:1, :r]
        slot = jnp.where(t < K, t - parent * k, 16 + t - K - parent * r)
        rows = lax.broadcasted_iota(i32, (height, r), 0)
        return (rows == slot).astype(f32).astype(bf16)

    sel = (row_choice(0), row_choice(1))
    sides = (side, 1 - side)
    spread = lax.broadcasted_iota(i32, (128, 256), 0)
    piv_acc = [None, None]
    out_rows = lax.broadcasted_iota(i32, (height, 128), 0)
    upd_row_id = parent * r + out_rows - 16
    piv_row_id = parent * k + out_rows
    for c in range(16):
        xs, ss = [], []
        for which, ref in enumerate((mine, other)):
            x = ref[:, c * 256:(c + 1) * 256]
            hi, lo = split(x)
            pick = lambda y: jnp.dot(sel[which], y, preferred_element_type=f32).astype(bf16)
            xs.append(jnp.concatenate([pick(hi), pick(lo)], axis=0))
            m = map_row[which:which + 1, c * 256:(c + 1) * 256]
            onehots = [
                spread == m - (K + s * (U // 2) + c * 128) for s in sides
            ] + [spread == m - (s * (K // 2) + c // 8 * 128) for s in sides]
            ss.append(jnp.concatenate([o.astype(f32).astype(bf16) for o in onehots], axis=0))
        res = lax.dot_general(
            jnp.concatenate(xs, axis=1), jnp.concatenate(ss, axis=1),
            (((1,), (1,)), ((), ())), preferred_element_type=f32,
        )
        res = res[:height] + res[height:]
        upd_col = side * (U // 2) + c * 128 + lane
        d = diag_row[0:1, pl.ds(pl.multiple_of(K + side * (U // 2) + c * 128, 128), 128)]
        own = res[:, :128] + jnp.where(upd_row_id == upd_col, d, 0.0)
        for at, tile in ((side, own), (1 - side, res[:, 128:256])):
            cols = pl.ds(pl.multiple_of(at * (U // 2) + c * 128, 128), 128)
            value = tile[16:]
            if extra is not None:
                value += extra[:, pl.ds(pl.multiple_of(K + at * (U // 2) + c * 128, 128), 128)]
            upd_out[:, cols] = value
        for n in range(2):
            part = res[:, 256 + n * 128:384 + n * 128]
            piv_acc[n] = part if c % 8 == 0 else piv_acc[n] + part
        if c % 8 == 7:
            half = c // 8
            col = side * (K // 2) + half * 128 + lane
            d = diag_row[0:1, pl.ds(pl.multiple_of(side * (K // 2) + half * 128, 128), 128)]
            piv_acc[0] += jnp.where((piv_row_id == col) & (out_rows < 16), d, 0.0)
            for n, at in enumerate((side, 1 - side)):
                cols = pl.ds(pl.multiple_of(at * (K // 2) + half * 128, 128), 128)
                value = piv_acc[n][16:]
                if extra is not None:
                    value += extra[:, cols]
                coupled_out[:, cols] = value
                piv_out[pl.ds(2 * at + half, k, stride=4), :] = piv_acc[n][:k]


def assemble(level, maps, diag, mine, other, extra):
    r = mine.shape[0]
    k = r // 8
    ins = (maps, diag, mine, other) + ((extra,) if level == 2 else ())
    return pl.pallas_call(
        functools.partial(assemble_kernel, level),
        out_shape=(
            jax.ShapeDtypeStruct((4 * k, 128), f32),
            jax.ShapeDtypeStruct((r, K), f32),
            jax.ShapeDtypeStruct((r, U), f32),
        ),
        in_specs=[VMEM] * len(ins),
        out_specs=(VMEM,) * 3,
        scratch_shapes=[pltpu.VMEM((8, U), i32), pltpu.VMEM((8, U + K), f32)],
        compiler_params=pltpu.CompilerParams(vmem_limit_bytes=40 * 2**20),
        cost_estimate=pl.CostEstimate(flops=2 * 10**9, bytes_accessed=4 * 10**6, transcendentals=0),
        name="assemble%d" % level,
    )(*ins)


def factor_kernel(level, *refs):
    pivots, coupled = refs[:2]
    out, w = refs[-2:]
    r = coupled.shape[0]
    n = K
    ct = coupled[...]
    if level == 2:
        order = refs[2]
        move = (lax.broadcasted_iota(i32, (n, n), 0) == order[...]).astype(f32).astype(bf16)
        ch, cl = split(ct)
        ct = jnp.dot(ch, move, preferred_element_type=f32) + jnp.dot(cl, move, preferred_element_type=f32)
        a = jnp.concatenate([pivots[pl.ds(c, n, stride=4), :] for c in range(4)], axis=1)
        ah, al = split(a)
        for part, source in enumerate((ah, al)):
            cols = jnp.dot(source, move, preferred_element_type=f32).astype(bf16)
            both = lax.dot_general(move, cols, (((0,), (0,)), ((), ())), preferred_element_type=f32)
            if part == 0:
                w[:, :n] = both
            else:
                w[:, :n] += both
    else:
        for c in range(4):
            w[:, c * 128:(c + 1) * 128] = pivots[pl.ds(c, n, stride=4), :]
    if r < 128:
        ct = jnp.concatenate([ct, jnp.zeros((128 - r, n), f32)], axis=0)
    w[:, n:] = ct.T
    blocks = n // 128
    for b in range(blocks):
        lo = b * 128
        rows = [w[lo + 8 * p: lo + 8 * p + 8, lo:lo + 128] for p in range(16)]
        inverse = jnp.concatenate(diag_inverse(rows), axis=0)
        solved = mm(inverse, w[lo:lo + 128, lo + 128:], ((1,), (0,)))
        for later in range(b + 1, blocks):
            off = (later - b - 1) * 128
            w[later * 128:(later + 1) * 128, later * 128:] -= mm(
                solved[:, off:off + 128], solved[:, off:], ((0,), (0,))
            )
        out[:, lo:lo + 128] = solved[:, n - lo - 128:].T[:r].astype(bf16)


def make_factor(level, pivots, coupled, order):
    r = coupled.shape[0]
    ins = (pivots, coupled) + ((order,) if level == 2 else ())
    return pl.pallas_call(
        functools.partial(factor_kernel, level),
        out_shape=jax.ShapeDtypeStruct((r, K), bf16),
        in_specs=[VMEM] * len(ins),
        out_specs=VMEM,
        scratch_shapes=[pltpu.VMEM((K, K + 128), f32)],
        compiler_params=pltpu.CompilerParams(vmem_limit_bytes=32 * 2**20),
        cost_estimate=pl.CostEstimate(flops=10**10, bytes_accessed=40 * 10**6, transcendentals=0),
        name="factor%d" % level,
    )(*ins)


def gather_kernel(ysize, x_ref, out, send_sem, recv_sem, local_sem):
    cube_at = lax.axis_index("cube")
    zh = lax.axis_index("panel")
    core = lax.rem(cube_at, 2)
    x = lax.rem(cube_at // 2, 4)
    zl = lax.rem(cube_at // 8, 2)
    yfull = cube_at // 16
    y = lax.rem(yfull, ysize)
    ybase = yfull - y

    def target(y, zl, x, core, zh):
        return {"cube": (ybase + y) * 16 + zl * 8 + x * 2 + core, "panel": zh}

    def shifted(v, d, size):
        return lax.rem(v + d, size)

    z_peers = [
        target(y, shifted(zl, a, 2), x, core, shifted(zh, b, 4))
        for a in range(2) for b in range(4) if a + b
    ]
    x_peers = [target(y, zl, shifted(x, d, 4), core, zh) for d in range(1, 4)]
    y_peers = [target(shifted(y, d, ysize), zl, x, core, zh) for d in range(1, ysize)]
    core_peers = [target(y, zl, x, 1 - core, zh)]
    stages = [
        (z_peers, out.at[y, zl, x, core, zh]),
        (x_peers, out.at[y, :, x, core]),
        (y_peers, out.at[y, :, :, core]),
        (core_peers, out.at[:, :, :, core]),
    ]
    everyone = z_peers + x_peers + y_peers + core_peers
    keep = pltpu.make_async_copy(x_ref, out.at[y, zl, x, core, zh], local_sem)
    keep.start()
    barrier = pltpu.get_barrier_semaphore()
    for peer in everyone:
        pl.semaphore_signal(barrier, inc=1, device_id=peer, device_id_type=pl.DeviceIdType.MESH)
    pl.semaphore_wait(barrier, len(everyone))
    keep.wait()
    number = 0
    sent = []
    for peers, part in stages:
        copies = []
        for peer in peers:
            copies.append(pltpu.make_async_remote_copy(
                src_ref=part, dst_ref=part, send_sem=send_sem.at[number], recv_sem=recv_sem.at[number],
                device_id=peer, device_id_type=pl.DeviceIdType.MESH,
            ))
            number += 1
        for copy in copies:
            copy.start()
        for copy in copies:
            copy.wait_recv()
        sent += copies
    for copy in sent:
        copy.wait_send()


def gather(level, piece, ident):
    ysize = 1 << level
    rows, cols = piece.shape
    count = 7 + 3 + ysize - 1 + 1
    out = pl.pallas_call(
        functools.partial(gather_kernel, ysize),
        out_shape=jax.ShapeDtypeStruct((ysize, 2, 4, 2, 4, rows, cols), piece.dtype),
        in_specs=[VMEM],
        out_specs=VMEM,
        scratch_shapes=[
            pltpu.SemaphoreType.DMA((count,)), pltpu.SemaphoreType.DMA((count,)),
            pltpu.SemaphoreType.DMA(()),
        ],
        compiler_params=pltpu.CompilerParams(
            collective_id=ident, has_side_effects=True, vmem_limit_bytes=32 * 2**20
        ),
        cost_estimate=pl.CostEstimate(flops=10**10, bytes_accessed=60 * 10**6, transcendentals=0),
        name="gather%d" % ident,
    )(piece)
    return out.reshape(-1, cols)


def from_partner(shard, stride):
    return lax.ppermute(shard, "cube", [(i, i ^ 1 << stride) for i in range(64)])


def plane_of(owner):
    cube, zh = owner // PANELS, lax.rem(owner, PANELS)
    cls = cube // 16 * 8 + lax.rem(cube, 8)
    return cls, lax.rem(cube // 8, 2) * PANELS + zh


def route_plane(coupling_rows, coupling_owner, coupling_slot):
    cls, z = plane_of(coupling_owner[:, 0])
    m = coupling_rows.shape[0]
    hits = (cls[:, None] == jnp.arange(32, dtype=i32)[None, :]).astype(bf16)
    before = (jnp.arange(m)[:, None] > jnp.arange(m)[None, :]).astype(bf16)
    earlier = jnp.dot(before, hits, preferred_element_type=f32)
    earlier = jnp.sum(earlier * hits.astype(f32), axis=1).astype(i32)
    target = cls * 16 + earlier
    choose = (target[None, :] == jnp.arange(512, dtype=i32)[:, None]).astype(bf16)
    marks = (z * 16 + coupling_slot)[:, None] == jnp.arange(128, dtype=i32)[None, :]
    payload = jnp.concatenate([coupling_rows, marks.astype(bf16)], axis=1)
    outgoing = jnp.dot(choose, payload, preferred_element_type=f32).astype(bf16)
    outgoing = outgoing.reshape(32, 16, -1)
    groups = [[y * 16 + zl * 8 + xc for y in range(4) for xc in range(8)] for zl in range(2)]
    return lax.all_to_all(outgoing, "cube", 0, 0, axis_index_groups=groups, tiled=True)


def route_column(got):
    got = got.reshape(512, -1)
    sums = lax.dot_general(
        got[:, U + K:], got[:, :U + K], (((0,), (0,)), ((), ())), preferred_element_type=f32
    ).astype(bf16).reshape(8, 16, U + K)
    groups = [
        [(y * 16 + zl * 8 + xc) * PANELS + zh for zl in range(2) for zh in range(PANELS)]
        for y in range(4) for xc in range(8)
    ]
    return lax.all_to_all(sums, ("cube", "panel"), 0, 0, axis_index_groups=groups, tiled=True)


def body(leaf_updates, extend_maps, front_diagonal, pivot_order, coupling_rows, coupling_owner, coupling_slot):
    routed = route_plane(coupling_rows, coupling_owner, coupling_slot)
    assembly = None
    children = leaf_updates
    order = pivot_order.reshape(1, K)
    for level in range(3):
        r = children.shape[0] // 2
        incoming = from_partner(children[r:], 3 + level)
        if level == 2:
            assembly = jnp.sum(routed.astype(f32), axis=0)
        piece, coupled, update_rows = assemble(
            level, extend_maps, front_diagonal, children[:r], incoming, assembly
        )
        pivots = gather(level, piece, 2 * level)
        factor = make_factor(level, pivots, coupled, order)
        if level == 0:
            routed, factor = lax.optimization_barrier((routed, factor))
            routed = route_column(routed)
        collected = gather(level, factor, 2 * level + 1)
        product = lax.dot_general(
            factor, collected, (((1,), (1,)), ((), ())), preferred_element_type=f32
        )
        children = update_rows - product
    return (factor, children)


def solution(mesh):
    return jax.shard_map(
        body,
        mesh=mesh,
        in_specs=(
            P(("cube", "panel"), None), P(), P(), P(),
            P(("cube", "panel"), None), P(("cube", "panel"), None), P(("cube", "panel")),
        ),
        out_specs=(P(("cube", "panel"), None), P(("cube", "panel"), None)),
        check_vma=False,
    )
```

```python
import functools
import jax
import jax.numpy as jnp
from jax import lax
from jax.experimental import pallas as pl
from jax.experimental.pallas import tpu as pltpu
from jax.sharding import PartitionSpec as P

CAP = 2
K = 512
U = 4096
PANELS = 4
f32, bf16, i32 = jnp.float32, jnp.bfloat16, jnp.int32
VMEM = pl.BlockSpec(memory_space=pltpu.VMEM)


def split(x):
    hi = x.astype(bf16)
    return hi, (x - hi.astype(f32)).astype(bf16)

def mm(x, y, dims):
    xh, xl = split(x); yh, yl = split(y)
    d = functools.partial(lax.dot_general, dimension_numbers=(dims, ((), ())), preferred_element_type=f32)
    return d(xh, yh) + (d(xh, yl) + d(xl, yh))

def diag_inverse(V, ahead=2):
    V = list(V)
    lane = lax.broadcasted_iota(jnp.int32, (8, 128), 1)
    sub = lax.broadcasted_iota(jnp.int32, (8, 128), 0)
    below = [sub > i for i in range(8)]
    scale = []
    for g in range(8):
        p0, j0 = 2 * g, 16 * g
        win = [q for q in range(p0, min(p0 + 2 + ahead, 16))]
        B = {(k, q): jnp.broadcast_to(V[q][:, j0+k:j0+k+1], (8, 128)) for k in range(16) for q in win}
        dinv = [None, None]
        for i in range(16):
            s, ii = divmod(i, 8)
            ps = p0 + s
            j = j0 + i
            inv = 1.0 / jnp.broadcast_to(B[i, ps][ii:ii+1, :], (8, 128))
            dinv[s] = inv if ii == 0 else jnp.where(below[ii-1], inv, dinv[s])
            at = lane == j
            row = jnp.where(at, 1.0, jnp.broadcast_to(V[ps][ii:ii+1, :], (8, 128)))
            splats = {k: jnp.broadcast_to(B[k, ps][ii:ii+1, :], (8, 128)) for k in range(i+1, 16)}
            for q in win:
                if q < ps or (q == ps and ii == 7): continue
                m = B[i, q] * inv
                if q == ps:
                    m = jnp.where(below[ii], m, 0.0)
                    z = jnp.where(at & below[ii], 0.0, V[q])
                else:
                    z = jnp.where(at, 0.0, V[q])
                V[q] = z - m * row
                for k in range(i+1, 16):
                    B[k, q] = B[k, q] - m * splats[k]
        scale += dinv
        rest = range(p0 + 2 + ahead, 16)
        if len(rest):
            G, Q = [], []
            for s in range(2):
                r = sub + (j0 + 8 * s)
                v = V[p0 + s]
                Q.append(v * dinv[s])
                inwin = (lane >= j0) & (lane < j0 + 16)
                G.append(jnp.where(inwin, jnp.where(lane < r, v, jnp.where(lane == r, 1.0, 0.0)), v))
            Gc, Qc = jnp.concatenate(G, 0), jnp.concatenate(Q, 0)
            gh, gl = split(Gc); qh, ql = split(Qc)
            upd = lax.dot_general(jnp.concatenate([qh, qh, ql], 0), jnp.concatenate([gh, gl, gh], 0),
                                  (((0,), (0,)), ((), ())), preferred_element_type=f32)
            zw = (lane >= j0) & (lane < j0 + 16)
            for q in rest:
                V[q] = jnp.where(zw, 0.0, V[q]) - upd[8*q:8*q+8]
    out = []
    for p in range(16):
        r = sub + 8 * p
        s = jnp.sqrt(scale[p])
        out.append(jnp.where(lane < r, V[p] * s, jnp.where(lane == r, s, 0.0)))
    return out


def place(level):
    group = 16 << level
    cube_at = lax.axis_index("cube")
    position = lax.rem(cube_at, group)
    return group, position, cube_at // group, position // (group // 2)


def assemble_kernel(level, *refs):
    maps, diag, mine, other = refs[:4]
    extra = refs[4] if level == 2 else None
    piv_out, coupled_out, upd_out, map_row, diag_row = refs[-5:]
    group, position, front_at, side = place(level)
    panel_at = lax.axis_index("panel")
    r = U // (group * PANELS)
    k = K // (group * PANELS)
    map_base = (0, 8, 12)[level]
    diag_base = (0, 4, 6)[level]
    block = lax.rem(position, group // 2) * PANELS + panel_at
    parent = position * PANELS + panel_at
    map_row[0:1, :] = maps[pl.ds(map_base + 2 * front_at + side, 1), :]
    map_row[1:2, :] = maps[pl.ds(map_base + 2 * front_at + 1 - side, 1), :]
    diag_row[0:1, :] = diag[pl.ds(diag_base + front_at, 1), :]
    lane = lax.broadcasted_iota(i32, (1, 128), 1)
    height = 16 + r

    def row_choice(half):
        start = block * (2 * r)
        tile = map_row[half:half + 1, pl.ds(pl.multiple_of(start // 128 * 128, 128), 128)]
        shift = lax.rem(128 - lax.rem(start + half * r, 128), 128)
        t = pltpu.roll(jnp.broadcast_to(tile, (8, 128)), shift, 1)[:1, :r]
        slot = jnp.where(t < K, t - parent * k, 16 + t - K - parent * r)
        rows = lax.broadcasted_iota(i32, (height, r), 0)
        return (rows == slot).astype(f32).astype(bf16)

    sel = (row_choice(0), row_choice(1))
    sides = (side, 1 - side)
    spread = lax.broadcasted_iota(i32, (128, 256), 0)
    piv_acc = [None, None]
    out_rows = lax.broadcasted_iota(i32, (height, 128), 0)
    upd_row_id = parent * r + out_rows - 16
    piv_row_id = parent * k + out_rows
    for c in range(16):
        xs, ss = [], []
        for which, ref in enumerate((mine, other)):
            x = ref[:, c * 256:(c + 1) * 256]
            hi, lo = split(x)
            pick = lambda y: jnp.dot(sel[which], y, preferred_element_type=f32).astype(bf16)
            xs.append(jnp.concatenate([pick(hi), pick(lo)], axis=0))
            m = map_row[which:which + 1, c * 256:(c + 1) * 256]
            onehots = [
                spread == m - (K + s * (U // 2) + c * 128) for s in sides
            ] + [spread == m - (s * (K // 2) + c // 8 * 128) for s in sides]
            ss.append(jnp.concatenate([o.astype(f32).astype(bf16) for o in onehots], axis=0))
        res = lax.dot_general(
            jnp.concatenate(xs, axis=1), jnp.concatenate(ss, axis=1),
            (((1,), (1,)), ((), ())), preferred_element_type=f32,
        )
        res = res[:height] + res[height:]
        upd_col = side * (U // 2) + c * 128 + lane
        d = diag_row[0:1, pl.ds(pl.multiple_of(K + side * (U // 2) + c * 128, 128), 128)]
        own = res[:, :128] + jnp.where(upd_row_id == upd_col, d, 0.0)
        for at, tile in ((side, own), (1 - side, res[:, 128:256])):
            cols = pl.ds(pl.multiple_of(at * (U // 2) + c * 128, 128), 128)
            value = tile[16:]
            if extra is not None:
                value += extra[:, pl.ds(pl.multiple_of(K + at * (U // 2) + c * 128, 128), 128)]
            upd_out[:, cols] = value
        for n in range(2):
            part = res[:, 256 + n * 128:384 + n * 128]
            piv_acc[n] = part if c % 8 == 0 else piv_acc[n] + part
        if c % 8 == 7:
            half = c // 8
            col = side * (K // 2) + half * 128 + lane
            d = diag_row[0:1, pl.ds(pl.multiple_of(side * (K // 2) + half * 128, 128), 128)]
            piv_acc[0] += jnp.where((piv_row_id == col) & (out_rows < 16), d, 0.0)
            for n, at in enumerate((side, 1 - side)):
                cols = pl.ds(pl.multiple_of(at * (K // 2) + half * 128, 128), 128)
                value = piv_acc[n][16:]
                if extra is not None:
                    value += extra[:, cols]
                coupled_out[:, cols] = value
                piv_out[pl.ds(2 * at + half, k, stride=4), :] = piv_acc[n][:k]


def assemble(level, maps, diag, mine, other, extra):
    r = mine.shape[0]
    k = r // 8
    ins = (maps, diag, mine, other) + ((extra,) if level == 2 else ())
    return pl.pallas_call(
        functools.partial(assemble_kernel, level),
        out_shape=(
            jax.ShapeDtypeStruct((4 * k, 128), f32),
            jax.ShapeDtypeStruct((r, K), f32),
            jax.ShapeDtypeStruct((r, U), f32),
        ),
        in_specs=[VMEM] * len(ins),
        out_specs=(VMEM,) * 3,
        scratch_shapes=[pltpu.VMEM((8, U), i32), pltpu.VMEM((8, U + K), f32)],
        compiler_params=pltpu.CompilerParams(vmem_limit_bytes=40 * 2**20),
        cost_estimate=pl.CostEstimate(flops=2 * 10**9, bytes_accessed=4 * 10**6, transcendentals=0),
        name="assemble%d" % level,
    )(*ins)


def factor_kernel(level, *refs):
    pivots, coupled = refs[:2]
    out, w = refs[-2:]
    r = coupled.shape[0]
    n = K
    ct = coupled[...]
    if level == 2:
        order = refs[2]
        move = (lax.broadcasted_iota(i32, (n, n), 0) == order[...]).astype(f32).astype(bf16)
        ch, cl = split(ct)
        ct = jnp.dot(ch, move, preferred_element_type=f32) + jnp.dot(cl, move, preferred_element_type=f32)
        a = jnp.concatenate([pivots[pl.ds(c, n, stride=4), :] for c in range(4)], axis=1)
        ah, al = split(a)
        for part, source in enumerate((ah, al)):
            cols = jnp.dot(source, move, preferred_element_type=f32).astype(bf16)
            both = lax.dot_general(move, cols, (((0,), (0,)), ((), ())), preferred_element_type=f32)
            if part == 0:
                w[:, :n] = both
            else:
                w[:, :n] += both
    else:
        for c in range(4):
            w[:, c * 128:(c + 1) * 128] = pivots[pl.ds(c, n, stride=4), :]
    if r < 128:
        ct = jnp.concatenate([ct, jnp.zeros((128 - r, n), f32)], axis=0)
    w[:, n:] = ct.T
    blocks = n // 128
    for b in range(blocks):
        lo = b * 128
        rows = [w[lo + 8 * p: lo + 8 * p + 8, lo:lo + 128] for p in range(16)]
        inverse = jnp.concatenate(diag_inverse(rows), axis=0)
        solved = mm(inverse, w[lo:lo + 128, lo + 128:], ((1,), (0,)))
        for later in range(b + 1, blocks):
            off = (later - b - 1) * 128
            w[later * 128:(later + 1) * 128, later * 128:] -= mm(
                solved[:, off:off + 128], solved[:, off:], ((0,), (0,))
            )
        out[:, lo:lo + 128] = solved[:, n - lo - 128:].T[:r].astype(bf16)


def make_factor(level, pivots, coupled, order):
    r = coupled.shape[0]
    ins = (pivots, coupled) + ((order,) if level == 2 else ())
    return pl.pallas_call(
        functools.partial(factor_kernel, level),
        out_shape=jax.ShapeDtypeStruct((r, K), bf16),
        in_specs=[VMEM] * len(ins),
        out_specs=VMEM,
        scratch_shapes=[pltpu.VMEM((K, K + 128), f32)],
        compiler_params=pltpu.CompilerParams(vmem_limit_bytes=32 * 2**20),
        cost_estimate=pl.CostEstimate(flops=10**10, bytes_accessed=40 * 10**6, transcendentals=0),
        name="factor%d" % level,
    )(*ins)


def gather_kernel(ysize, x_ref, out, send_sem, recv_sem, local_sem):
    cube_at = lax.axis_index("cube")
    zh = lax.axis_index("panel")
    core = lax.rem(cube_at, 2)
    x = lax.rem(cube_at // 2, 4)
    zl = lax.rem(cube_at // 8, 2)
    yfull = cube_at // 16
    y = lax.rem(yfull, ysize)
    ybase = yfull - y

    def target(y, zl, x, core, zh):
        return {"cube": (ybase + y) * 16 + zl * 8 + x * 2 + core, "panel": zh}

    def shifted(v, d, size):
        return lax.rem(v + d, size)

    z_peers = [
        target(y, shifted(zl, a, 2), x, core, shifted(zh, b, 4))
        for a in range(2) for b in range(4) if a + b
    ]
    x_peers = [target(y, zl, shifted(x, d, 4), core, zh) for d in range(1, 4)]
    y_peers = [target(shifted(y, d, ysize), zl, x, core, zh) for d in range(1, ysize)]
    core_peers = [target(y, zl, x, 1 - core, zh)]
    stages = [
        (z_peers, out.at[y, zl, x, core, zh]),
        (x_peers, out.at[y, :, x, core]),
        (y_peers, out.at[y, :, :, core]),
        (core_peers, out.at[:, :, :, core]),
    ]
    everyone = z_peers + x_peers + y_peers + core_peers
    keep = pltpu.make_async_copy(x_ref, out.at[y, zl, x, core, zh], local_sem)
    keep.start()
    barrier = pltpu.get_barrier_semaphore()
    for peer in everyone:
        pl.semaphore_signal(barrier, inc=1, device_id=peer, device_id_type=pl.DeviceIdType.MESH)
    pl.semaphore_wait(barrier, len(everyone))
    keep.wait()
    number = 0
    sent = []
    for peers, part in stages:
        copies = []
        for peer in peers:
            copies.append(pltpu.make_async_remote_copy(
                src_ref=part, dst_ref=part, send_sem=send_sem.at[number], recv_sem=recv_sem.at[number],
                device_id=peer, device_id_type=pl.DeviceIdType.MESH,
            ))
            number += 1
        for copy in copies:
            copy.start()
        for copy in copies:
            copy.wait_recv()
        sent += copies
    for copy in sent:
        copy.wait_send()


def gather(level, piece, ident):
    ysize = 1 << level
    rows, cols = piece.shape
    count = 7 + 3 + ysize - 1 + 1
    out = pl.pallas_call(
        functools.partial(gather_kernel, ysize),
        out_shape=jax.ShapeDtypeStruct((ysize, 2, 4, 2, 4, rows, cols), piece.dtype),
        in_specs=[VMEM],
        out_specs=VMEM,
        scratch_shapes=[
            pltpu.SemaphoreType.DMA((count,)), pltpu.SemaphoreType.DMA((count,)),
            pltpu.SemaphoreType.DMA(()),
        ],
        compiler_params=pltpu.CompilerParams(
            collective_id=ident, has_side_effects=True, vmem_limit_bytes=32 * 2**20
        ),
        cost_estimate=pl.CostEstimate(flops=10**10, bytes_accessed=60 * 10**6, transcendentals=0),
        name="gather%d" % ident,
    )(piece)
    return out.reshape(-1, cols)


def update_kernel(ysize, f_ref, upd_ref, out, fi, fj, prod, got, send_sem, recv_sem):
    r = f_ref.shape[0]
    cube_at = lax.axis_index("cube")
    zh = lax.axis_index("panel")
    w = lax.rem(cube_at, 8)
    zl = lax.rem(cube_at // 8, 2)
    yfull = cube_at // 16
    y = lax.rem(yfull, ysize)
    ybase = yfull - y

    def target(y, zl, w, zh):
        return {"cube": (ybase + y) * 16 + zl * 8 + w, "panel": zh}

    mine = (y * 2 + zl) * PANELS + zh
    v_peers = [
        target(lax.rem(y + a, ysize), lax.rem(zl + b, 2), w, lax.rem(zh + c, 4))
        for a in range(ysize) for b in range(2) for c in range(4) if a + b + c
    ]
    w_places = [lax.rem(w + d, 8) for d in range(1, 8)]
    w_peers = [target(y, zl, place, zh) for place in w_places]
    barrier = pltpu.get_barrier_semaphore()
    for peer in v_peers + w_peers:
        pl.semaphore_signal(barrier, inc=1, device_id=peer, device_id_type=pl.DeviceIdType.MESH)
    fi[pl.ds(w, 1)] = f_ref[...][None]
    fj[pl.ds(mine, 1)] = f_ref[...][None]
    pl.semaphore_wait(barrier, len(v_peers) + len(w_peers))
    copies = []

    def send(src, dst, peer):
        copy = pltpu.make_async_remote_copy(
            src_ref=src, dst_ref=dst, send_sem=send_sem.at[len(copies)], recv_sem=recv_sem.at[len(copies)],
            device_id=peer, device_id_type=pl.DeviceIdType.MESH,
        )
        copy.start()
        copies.append(copy)

    for peer in v_peers:
        send(fj.at[mine], fj.at[mine], peer)
    for peer in w_peers:
        send(fi.at[w], fi.at[w], peer)
    for copy in copies:
        copy.wait_recv()
    right = fj[...].reshape(-1, K)
    prod[...] = lax.dot_general(
        fi[...].reshape(-1, K), right, (((1,), (1,)), ((), ())), preferred_element_type=f32
    ).reshape(8, r, 512)
    first = len(copies)
    for place, peer in zip(w_places, w_peers):
        send(prod.at[place], got.at[w], peer)
    got[pl.ds(w, 1)] = prod[pl.ds(w, 1)]
    for copy in copies[first:]:
        copy.wait_recv()
    wide = PANELS * r
    for block in range(2 * ysize):
        parts = [got[q, :, block * wide:(block + 1) * wide] for q in range(8)]
        lo = block * 8 * wide
        out[:, lo:lo + 8 * wide] = upd_ref[:, lo:lo + 8 * wide] - jnp.concatenate(parts, axis=1)
    for copy in copies:
        copy.wait_send()


def update(level, factor, update_rows, ident):
    ysize = 1 << level
    r = factor.shape[0]
    count = 8 * ysize - 1 + 7 + 7
    return pl.pallas_call(
        functools.partial(update_kernel, ysize),
        out_shape=jax.ShapeDtypeStruct((r, U), f32),
        in_specs=[VMEM] * 2,
        out_specs=VMEM,
        scratch_shapes=[
            pltpu.VMEM((8, r, K), bf16), pltpu.VMEM((8 * ysize, r, K), bf16),
            pltpu.VMEM((8, r, 512), f32), pltpu.VMEM((8, r, 512), f32),
            pltpu.SemaphoreType.DMA((count,)), pltpu.SemaphoreType.DMA((count,)),
        ],
        compiler_params=pltpu.CompilerParams(
            collective_id=ident, has_side_effects=True, vmem_limit_bytes=32 * 2**20
        ),
        cost_estimate=pl.CostEstimate(flops=10**10, bytes_accessed=60 * 10**6, transcendentals=0),
        name="update%d" % level,
    )(factor, update_rows)


def from_partner(shard, stride):
    return lax.ppermute(shard, "cube", [(i, i ^ 1 << stride) for i in range(64)])


def plane_of(owner):
    cube, zh = owner // PANELS, lax.rem(owner, PANELS)
    cls = cube // 16 * 8 + lax.rem(cube, 8)
    return cls, lax.rem(cube // 8, 2) * PANELS + zh


def route_plane(coupling_rows, coupling_owner, coupling_slot):
    cls, z = plane_of(coupling_owner[:, 0])
    m = coupling_rows.shape[0]
    hits = (cls[:, None] == jnp.arange(32, dtype=i32)[None, :]).astype(bf16)
    before = (jnp.arange(m)[:, None] > jnp.arange(m)[None, :]).astype(bf16)
    earlier = jnp.dot(before, hits, preferred_element_type=f32)
    earlier = jnp.sum(earlier * hits.astype(f32), axis=1).astype(i32)
    target = cls * 16 + earlier
    choose = (target[None, :] == jnp.arange(512, dtype=i32)[:, None]).astype(bf16)
    marks = (z * 16 + coupling_slot)[:, None] == jnp.arange(128, dtype=i32)[None, :]
    payload = jnp.concatenate([coupling_rows, marks.astype(bf16)], axis=1)
    outgoing = jnp.dot(choose, payload, preferred_element_type=f32).astype(bf16)
    outgoing = outgoing.reshape(32, 16, -1)
    groups = [[y * 16 + zl * 8 + xc for y in range(4) for xc in range(8)] for zl in range(2)]
    return lax.all_to_all(outgoing, "cube", 0, 0, axis_index_groups=groups, tiled=True)


def route_column(got):
    got = got.reshape(512, -1)
    sums = lax.dot_general(
        got[:, U + K:], got[:, :U + K], (((0,), (0,)), ((), ())), preferred_element_type=f32
    ).astype(bf16).reshape(8, 16, U + K)
    groups = [
        [(y * 16 + zl * 8 + xc) * PANELS + zh for zl in range(2) for zh in range(PANELS)]
        for y in range(4) for xc in range(8)
    ]
    return lax.all_to_all(sums, ("cube", "panel"), 0, 0, axis_index_groups=groups, tiled=True)


def body(leaf_updates, extend_maps, front_diagonal, pivot_order, coupling_rows, coupling_owner, coupling_slot):
    routed = route_plane(coupling_rows, coupling_owner, coupling_slot)
    assembly = None
    children = leaf_updates
    order = pivot_order.reshape(1, K)
    for level in range(3):
        r = children.shape[0] // 2
        incoming = from_partner(children[r:], 3 + level)
        if level == 2:
            assembly = jnp.sum(routed.astype(f32), axis=0)
        piece, coupled, update_rows = assemble(
            level, extend_maps, front_diagonal, children[:r], incoming, assembly
        )
        pivots = gather(level, piece, 2 * level)
        factor = make_factor(level, pivots, coupled, order)
        if level == 0:
            routed, factor = lax.optimization_barrier((routed, factor))
            routed = route_column(routed)
        children = update(level, factor, update_rows, 2 * level + 1)
    return (factor, children)


def solution(mesh):
    return jax.shard_map(
        body,
        mesh=mesh,
        in_specs=(
            P(("cube", "panel"), None), P(), P(), P(),
            P(("cube", "panel"), None), P(("cube", "panel"), None), P(("cube", "panel")),
        ),
        out_specs=(P(("cube", "panel"), None), P(("cube", "panel"), None)),
        check_vma=False,
    )
```

```python
import functools
import jax
import jax.numpy as jnp
from jax import lax
from jax.experimental import pallas as pl
from jax.experimental.pallas import tpu as pltpu
from jax.sharding import PartitionSpec as P

CAP = 2
K = 512
U = 4096
PANELS = 4
f32, bf16, i32 = jnp.float32, jnp.bfloat16, jnp.int32
VMEM = pl.BlockSpec(memory_space=pltpu.VMEM)


def split(x):
    hi = x.astype(bf16)
    return hi, (x - hi.astype(f32)).astype(bf16)

def mm(x, y, dims):
    xh, xl = split(x); yh, yl = split(y)
    d = functools.partial(lax.dot_general, dimension_numbers=(dims, ((), ())), preferred_element_type=f32)
    return d(xh, yh) + (d(xh, yl) + d(xl, yh))

def diag_inverse(V, ahead=2):
    V = list(V)
    lane = lax.broadcasted_iota(jnp.int32, (8, 128), 1)
    sub = lax.broadcasted_iota(jnp.int32, (8, 128), 0)
    below = [sub > i for i in range(8)]
    scale = []
    for g in range(8):
        p0, j0 = 2 * g, 16 * g
        win = [q for q in range(p0, min(p0 + 2 + ahead, 16))]
        B = {(k, q): jnp.broadcast_to(V[q][:, j0+k:j0+k+1], (8, 128)) for k in range(16) for q in win}
        dinv = [None, None]
        for i in range(16):
            s, ii = divmod(i, 8)
            ps = p0 + s
            j = j0 + i
            inv = 1.0 / jnp.broadcast_to(B[i, ps][ii:ii+1, :], (8, 128))
            dinv[s] = inv if ii == 0 else jnp.where(below[ii-1], inv, dinv[s])
            at = lane == j
            row = jnp.where(at, 1.0, jnp.broadcast_to(V[ps][ii:ii+1, :], (8, 128)))
            splats = {k: jnp.broadcast_to(B[k, ps][ii:ii+1, :], (8, 128)) for k in range(i+1, 16)}
            for q in win:
                if q < ps or (q == ps and ii == 7): continue
                m = B[i, q] * inv
                if q == ps:
                    m = jnp.where(below[ii], m, 0.0)
                    z = jnp.where(at & below[ii], 0.0, V[q])
                else:
                    z = jnp.where(at, 0.0, V[q])
                V[q] = z - m * row
                for k in range(i+1, 16):
                    B[k, q] = B[k, q] - m * splats[k]
        scale += dinv
        rest = range(p0 + 2 + ahead, 16)
        if len(rest):
            G, Q = [], []
            for s in range(2):
                r = sub + (j0 + 8 * s)
                v = V[p0 + s]
                Q.append(v * dinv[s])
                inwin = (lane >= j0) & (lane < j0 + 16)
                G.append(jnp.where(inwin, jnp.where(lane < r, v, jnp.where(lane == r, 1.0, 0.0)), v))
            Gc, Qc = jnp.concatenate(G, 0), jnp.concatenate(Q, 0)
            gh, gl = split(Gc); qh, ql = split(Qc)
            upd = lax.dot_general(jnp.concatenate([qh, qh, ql], 0), jnp.concatenate([gh, gl, gh], 0),
                                  (((0,), (0,)), ((), ())), preferred_element_type=f32)
            zw = (lane >= j0) & (lane < j0 + 16)
            for q in rest:
                V[q] = jnp.where(zw, 0.0, V[q]) - upd[8*q:8*q+8]
    out = []
    for p in range(16):
        r = sub + 8 * p
        s = jnp.sqrt(scale[p])
        out.append(jnp.where(lane < r, V[p] * s, jnp.where(lane == r, s, 0.0)))
    return out


def place(level):
    group = 16 << level
    cube_at = lax.axis_index("cube")
    position = lax.rem(cube_at, group)
    return group, position, cube_at // group, position // (group // 2)


def assemble_kernel(level, *refs):
    maps, diag, mine, other = refs[:4]
    extra = refs[4] if level == 2 else None
    piv_out, coupled_out, upd_out, map_row, diag_row = refs[-5:]
    group, position, front_at, side = place(level)
    panel_at = lax.axis_index("panel")
    r = U // (group * PANELS)
    k = K // (group * PANELS)
    map_base = (0, 8, 12)[level]
    diag_base = (0, 4, 6)[level]
    block = lax.rem(position, group // 2) * PANELS + panel_at
    parent = position * PANELS + panel_at
    map_row[0:1, :] = maps[pl.ds(map_base + 2 * front_at + side, 1), :]
    map_row[1:2, :] = maps[pl.ds(map_base + 2 * front_at + 1 - side, 1), :]
    diag_row[0:1, :] = diag[pl.ds(diag_base + front_at, 1), :]
    lane = lax.broadcasted_iota(i32, (1, 128), 1)
    height = 16 + r

    def row_choice(half):
        start = block * (2 * r)
        tile = map_row[half:half + 1, pl.ds(pl.multiple_of(start // 128 * 128, 128), 128)]
        shift = lax.rem(128 - lax.rem(start + half * r, 128), 128)
        t = pltpu.roll(jnp.broadcast_to(tile, (8, 128)), shift, 1)[:1, :r]
        slot = jnp.where(t < K, t - parent * k, 16 + t - K - parent * r)
        rows = lax.broadcasted_iota(i32, (height, r), 0)
        return (rows == slot).astype(f32).astype(bf16)

    sel = (row_choice(0), row_choice(1))
    sides = (side, 1 - side)
    spread = lax.broadcasted_iota(i32, (128, 256), 0)
    piv_acc = [None, None]
    out_rows = lax.broadcasted_iota(i32, (height, 128), 0)
    upd_row_id = parent * r + out_rows - 16
    piv_row_id = parent * k + out_rows
    for c in range(16):
        xs, ss = [], []
        for which, ref in enumerate((mine, other)):
            x = ref[:, c * 256:(c + 1) * 256]
            hi, lo = split(x)
            pick = lambda y: jnp.dot(sel[which], y, preferred_element_type=f32).astype(bf16)
            xs.append(jnp.concatenate([pick(hi), pick(lo)], axis=0))
            m = map_row[which:which + 1, c * 256:(c + 1) * 256]
            onehots = [
                spread == m - (K + s * (U // 2) + c * 128) for s in sides
            ] + [spread == m - (s * (K // 2) + c // 8 * 128) for s in sides]
            ss.append(jnp.concatenate([o.astype(f32).astype(bf16) for o in onehots], axis=0))
        res = lax.dot_general(
            jnp.concatenate(xs, axis=1), jnp.concatenate(ss, axis=1),
            (((1,), (1,)), ((), ())), preferred_element_type=f32,
        )
        res = res[:height] + res[height:]
        upd_col = side * (U // 2) + c * 128 + lane
        d = diag_row[0:1, pl.ds(pl.multiple_of(K + side * (U // 2) + c * 128, 128), 128)]
        own = res[:, :128] + jnp.where(upd_row_id == upd_col, d, 0.0)
        for at, tile in ((side, own), (1 - side, res[:, 128:256])):
            cols = pl.ds(pl.multiple_of(at * (U // 2) + c * 128, 128), 128)
            value = tile[16:]
            if extra is not None:
                value += extra[:, pl.ds(pl.multiple_of(K + at * (U // 2) + c * 128, 128), 128)]
            upd_out[:, cols] = value
        for n in range(2):
            part = res[:, 256 + n * 128:384 + n * 128]
            piv_acc[n] = part if c % 8 == 0 else piv_acc[n] + part
        if c % 8 == 7:
            half = c // 8
            col = side * (K // 2) + half * 128 + lane
            d = diag_row[0:1, pl.ds(pl.multiple_of(side * (K // 2) + half * 128, 128), 128)]
            piv_acc[0] += jnp.where((piv_row_id == col) & (out_rows < 16), d, 0.0)
            for n, at in enumerate((side, 1 - side)):
                cols = pl.ds(pl.multiple_of(at * (K // 2) + half * 128, 128), 128)
                value = piv_acc[n][16:]
                if extra is not None:
                    value += extra[:, cols]
                coupled_out[:, cols] = value
                piv_out[pl.ds(2 * at + half, k, stride=4), :] = piv_acc[n][:k]


def assemble(level, maps, diag, mine, other, extra):
    r = mine.shape[0]
    k = r // 8
    ins = (maps, diag, mine, other) + ((extra,) if level == 2 else ())
    return pl.pallas_call(
        functools.partial(assemble_kernel, level),
        out_shape=(
            jax.ShapeDtypeStruct((4 * k, 128), f32),
            jax.ShapeDtypeStruct((r, K), f32),
            jax.ShapeDtypeStruct((r, U), f32),
        ),
        in_specs=[VMEM] * len(ins),
        out_specs=(VMEM,) * 3,
        scratch_shapes=[pltpu.VMEM((8, U), i32), pltpu.VMEM((8, U + K), f32)],
        compiler_params=pltpu.CompilerParams(vmem_limit_bytes=40 * 2**20),
        cost_estimate=pl.CostEstimate(flops=2 * 10**9, bytes_accessed=4 * 10**6, transcendentals=0),
        name="assemble%d" % level,
    )(*ins)


def level_kernel(level, *refs):
    last = level == 2
    ysize = 1 << level
    piece, coupled, upd = refs[:3]
    order = refs[3] if last else None
    outs, scratch = refs[3 + last:5 + last], refs[5 + last:]
    own_out, second_out = outs
    a, w, fi, fj, prod, got, upd_in, send_sem, recv_sem = scratch
    r = coupled.shape[0]
    half = prod.shape[2]
    n = K
    cube_at = lax.axis_index("cube")
    zh = lax.axis_index("panel")
    place = lax.rem(cube_at, 8)
    core = lax.rem(cube_at, 2)
    x = lax.rem(cube_at // 2, 4)
    zl = lax.rem(cube_at // 8, 2)
    yfull = cube_at // 16
    y = lax.rem(yfull, ysize)
    ybase = yfull - y
    mine = (y * 2 + zl) * PANELS + zh

    def target(y, zl, w, zh):
        return {"cube": (ybase + y) * 16 + zl * 8 + w, "panel": zh}

    def turned(a, b, c):
        return target(lax.rem(y + a, ysize), lax.rem(zl + b, 2), place, lax.rem(zh + c, 4))

    z_peers = [turned(0, b, c) for b in range(2) for c in range(4) if b + c]
    v_peers = z_peers + [turned(d, b, c) for d in range(1, ysize) for b in range(2) for c in range(4)]
    w_places = [lax.rem(place + d, 8) for d in range(1, 8)]
    w_peers = [target(y, zl, q, zh) for q in w_places]
    cross_places, cross_peers = [], []
    if not last:
        bit = 1 << level
        across = yfull + bit - 2 * bit * lax.rem(yfull // bit, 2)
        cross_places = [place] + w_places
        cross_peers = [{"cube": across * 16 + zl * 8 + q, "panel": zh} for q in cross_places]
    everyone = v_peers + w_peers + cross_peers
    barrier = pltpu.get_barrier_semaphore()
    for peer in everyone:
        pl.semaphore_signal(barrier, inc=1, device_id=peer, device_id_type=pl.DeviceIdType.MESH)
    a[pl.ds(y, 1), pl.ds(zl, 1), pl.ds(x, 1), pl.ds(core, 1), pl.ds(zh, 1)] = piece[...][None, None, None, None, None]
    pl.semaphore_wait(barrier, len(everyone))
    copies = []

    def send(src, dst, peer):
        copy = pltpu.make_async_remote_copy(
            src_ref=src, dst_ref=dst, send_sem=send_sem.at[len(copies)], recv_sem=recv_sem.at[len(copies)],
            device_id=peer, device_id_type=pl.DeviceIdType.MESH,
        )
        copy.start()
        copies.append(copy)
        return copy

    early = None
    stages = [
        (z_peers, a.at[y, zl, x, core, zh]),
        ([target(y, zl, lax.rem(x + d, 4) * 2 + core, zh) for d in range(1, 4)], a.at[y, :, x, core]),
        ([turned(d, 0, 0) for d in range(1, ysize)], a.at[y, :, :, core]),
        ([target(y, zl, x * 2 + 1 - core, zh)], a.at[:, :, :, core]),
    ]
    for number, (peers, part) in enumerate(stages):
        started = [send(part, part, peer) for peer in peers]
        if number == 0 and not last:
            early = send(upd.at[half:], upd_in, cross_peers[0])
        for copy in started:
            copy.wait_recv()

    flat = a.reshape(4 * n, 128)
    ct = coupled[...]
    if last:
        move = (lax.broadcasted_iota(i32, (n, n), 0) == order[...]).astype(f32).astype(bf16)
        ch, cl = split(ct)
        ct = jnp.dot(ch, move, preferred_element_type=f32) + jnp.dot(cl, move, preferred_element_type=f32)
        full = jnp.concatenate([flat[pl.ds(c, n, stride=4), :] for c in range(4)], axis=1)
        for part, source in enumerate(split(full)):
            cols = jnp.dot(source, move, preferred_element_type=f32).astype(bf16)
            both = lax.dot_general(move, cols, (((0,), (0,)), ((), ())), preferred_element_type=f32)
            if part == 0:
                w[:, :n] = both
            else:
                w[:, :n] += both
    else:
        for c in range(4):
            w[:, c * 128:(c + 1) * 128] = flat[pl.ds(c, n, stride=4), :]
    if r < 128:
        ct = jnp.concatenate([ct, jnp.zeros((128 - r, n), f32)], axis=0)
    w[:, n:] = ct.T
    blocks = n // 128
    factors = [[], []]

    def spread(lo, hi, group):
        for peer in v_peers:
            group.append(send(fj.at[lo:hi, mine], fj.at[lo:hi, mine], peer))
        for peer in w_peers:
            group.append(send(fi.at[lo:hi, place], fi.at[lo:hi, place], peer))

    for b in range(blocks):
        lo = b * 128
        rows = [w[lo + 8 * p: lo + 8 * p + 8, lo:lo + 128] for p in range(16)]
        inverse = jnp.concatenate(diag_inverse(rows), axis=0)
        solved = mm(inverse, w[lo:lo + 128, lo + 128:], ((1,), (0,)))
        for later in range(b + 1, blocks):
            off = (later - b - 1) * 128
            w[later * 128:(later + 1) * 128, later * 128:] -= mm(
                solved[:, off:off + 128], solved[:, off:], ((0,), (0,))
            )
        f = solved[:, n - lo - 128:].T[:r].astype(bf16)
        if last:
            second_out[:, lo:lo + 128] = f
        fi[b, pl.ds(place, 1)] = f[None]
        fj[b, pl.ds(mine, 1)] = f[None]
        if b == blocks - 2:
            spread(0, blocks - 1, factors[0])
        if b == blocks - 1:
            spread(blocks - 1, blocks, factors[1])

    def block_product(lo, hi):
        left = jnp.concatenate([fi[b].reshape(8 * r, 128) for b in range(lo, hi)], axis=1)
        right = jnp.concatenate([fj[b].reshape(512, 128) for b in range(lo, hi)], axis=1)
        return lax.dot_general(left, right, (((1,), (1,)), ((), ())), preferred_element_type=f32)

    for copy in factors[0]:
        copy.wait_recv()
    product = block_product(0, blocks - 1)
    for copy in factors[1]:
        copy.wait_recv()
    product = (product + block_product(blocks - 1, blocks)).reshape(8, r, 512)
    for part in range(r // half):
        prod[part] = product[:, part * half:(part + 1) * half]
    back = [send(prod.at[0, q], got.at[0, place], peer) for q, peer in zip(w_places, w_peers)]
    back += [send(prod.at[1, q], got.at[1, place], peer) for q, peer in zip(cross_places, cross_peers)]
    got[0, pl.ds(place, 1)] = prod[0, pl.ds(place, 1)]
    if early is not None:
        early.wait_recv()
    for copy in back:
        copy.wait_recv()
    wide = PANELS * r
    for part in range(r // half):
        source = upd_in if part else upd
        out = second_out if part else own_out
        for block in range(2 * ysize):
            parts = [got[part, q, :, block * wide:(block + 1) * wide] for q in range(8)]
            lo = block * 8 * wide
            out[:, lo:lo + 8 * wide] = source[:half, lo:lo + 8 * wide] - jnp.concatenate(parts, axis=1)
    for copy in copies:
        copy.wait_send()


def eliminate(level, piece, coupled, update_rows, order):
    last = level == 2
    ysize = 1 << level
    r = coupled.shape[0]
    half = r if last else r // 2
    ins = (piece, coupled, update_rows) + ((order,) if last else ())
    second = jax.ShapeDtypeStruct((r, K), bf16) if last else jax.ShapeDtypeStruct((half, U), f32)
    v = 8 * ysize
    count = 7 + 3 + ysize - 1 + 1 + 2 * (v - 1 + 7) + 7 + (0 if last else 9)
    return pl.pallas_call(
        functools.partial(level_kernel, level),
        out_shape=(jax.ShapeDtypeStruct((half, U), f32), second),
        in_specs=[VMEM] * len(ins),
        out_specs=(VMEM, VMEM),
        scratch_shapes=[
            pltpu.VMEM((ysize, 2, 4, 2, 4) + piece.shape, f32),
            pltpu.VMEM((K, K + 128), f32),
            pltpu.VMEM((4, 8, r, 128), bf16),
            pltpu.VMEM((4, v, r, 128), bf16),
            pltpu.VMEM((r // half, 8, half, 512), f32),
            pltpu.VMEM((r // half, 8, half, 512), f32),
            pltpu.VMEM((half, U), f32),
            pltpu.SemaphoreType.DMA((count,)), pltpu.SemaphoreType.DMA((count,)),
        ],
        compiler_params=pltpu.CompilerParams(
            collective_id=level, has_side_effects=True, vmem_limit_bytes=40 * 2**20
        ),
        cost_estimate=pl.CostEstimate(flops=3 * 10**10, bytes_accessed=150 * 10**6, transcendentals=0),
        name="level%d" % level,
    )(*ins)


def from_partner(shard, stride):
    return lax.ppermute(shard, "cube", [(i, i ^ 1 << stride) for i in range(64)])


def plane_of(owner):
    cube, zh = owner // PANELS, lax.rem(owner, PANELS)
    cls = cube // 16 * 8 + lax.rem(cube, 8)
    return cls, lax.rem(cube // 8, 2) * PANELS + zh


def route_plane(coupling_rows, coupling_owner, coupling_slot):
    cls, z = plane_of(coupling_owner[:, 0])
    m = coupling_rows.shape[0]
    hits = (cls[:, None] == jnp.arange(32, dtype=i32)[None, :]).astype(bf16)
    before = (jnp.arange(m)[:, None] > jnp.arange(m)[None, :]).astype(bf16)
    earlier = jnp.dot(before, hits, preferred_element_type=f32)
    earlier = jnp.sum(earlier * hits.astype(f32), axis=1).astype(i32)
    target = cls * 16 + earlier
    choose = (target[None, :] == jnp.arange(512, dtype=i32)[:, None]).astype(bf16)
    marks = (z * 16 + coupling_slot)[:, None] == jnp.arange(128, dtype=i32)[None, :]
    payload = jnp.concatenate([coupling_rows, marks.astype(bf16)], axis=1)
    outgoing = jnp.dot(choose, payload, preferred_element_type=f32).astype(bf16)
    outgoing = outgoing.reshape(32, 16, -1)
    groups = [[y * 16 + zl * 8 + xc for y in range(4) for xc in range(8)] for zl in range(2)]
    return lax.all_to_all(outgoing, "cube", 0, 0, axis_index_groups=groups, tiled=True)


def route_column(got):
    got = got.reshape(512, -1)
    sums = lax.dot_general(
        got[:, U + K:], got[:, :U + K], (((0,), (0,)), ((), ())), preferred_element_type=f32
    ).astype(bf16).reshape(8, 16, U + K)
    groups = [
        [(y * 16 + zl * 8 + xc) * PANELS + zh for zl in range(2) for zh in range(PANELS)]
        for y in range(4) for xc in range(8)
    ]
    return lax.all_to_all(sums, ("cube", "panel"), 0, 0, axis_index_groups=groups, tiled=True)


def body(leaf_updates, extend_maps, front_diagonal, pivot_order, coupling_rows, coupling_owner, coupling_slot):
    routed = route_plane(coupling_rows, coupling_owner, coupling_slot)
    assembly = None
    r = leaf_updates.shape[0] // 2
    own, incoming = leaf_updates[:r], from_partner(leaf_updates[r:], 3)
    order = pivot_order.reshape(1, K)
    for level in range(3):
        if level == 2:
            assembly = jnp.sum(routed.astype(f32), axis=0)
        piece, coupled, update_rows = assemble(
            level, extend_maps, front_diagonal, own, incoming, assembly
        )
        own, incoming = eliminate(level, piece, coupled, update_rows, order)
        if level == 0:
            routed, own = lax.optimization_barrier((routed, own))
            routed = route_column(routed)
    return (incoming, own)


def solution(mesh):
    return jax.shard_map(
        body,
        mesh=mesh,
        in_specs=(
            P(("cube", "panel"), None), P(), P(), P(),
            P(("cube", "panel"), None), P(("cube", "panel"), None), P(("cube", "panel")),
        ),
        out_specs=(P(("cube", "panel"), None), P(("cube", "panel"), None)),
        check_vma=False,
    )
```

```python
import functools
import jax
import jax.numpy as jnp
from jax import lax
from jax.experimental import pallas as pl
from jax.experimental.pallas import tpu as pltpu
from jax.sharding import PartitionSpec as P

CAP = 2
K = 512
U = 4096
PANELS = 4
f32, bf16, i32 = jnp.float32, jnp.bfloat16, jnp.int32
VMEM = pl.BlockSpec(memory_space=pltpu.VMEM)


def split(x):
    hi = x.astype(bf16)
    return hi, (x - hi.astype(f32)).astype(bf16)

def mm(x, y, dims):
    xh, xl = split(x); yh, yl = split(y)
    d = functools.partial(lax.dot_general, dimension_numbers=(dims, ((), ())), preferred_element_type=f32)
    return d(xh, yh) + (d(xh, yl) + d(xl, yh))

def diag_inverse(V, ahead=2):
    V = list(V)
    lane = lax.broadcasted_iota(jnp.int32, (8, 128), 1)
    sub = lax.broadcasted_iota(jnp.int32, (8, 128), 0)
    below = [sub > i for i in range(8)]
    scale = []
    for g in range(8):
        p0, j0 = 2 * g, 16 * g
        win = [q for q in range(p0, min(p0 + 2 + ahead, 16))]
        B = {(k, q): jnp.broadcast_to(V[q][:, j0+k:j0+k+1], (8, 128)) for k in range(16) for q in win}
        dinv = [None, None]
        for i in range(16):
            s, ii = divmod(i, 8)
            ps = p0 + s
            j = j0 + i
            inv = 1.0 / jnp.broadcast_to(B[i, ps][ii:ii+1, :], (8, 128))
            dinv[s] = inv if ii == 0 else jnp.where(below[ii-1], inv, dinv[s])
            at = lane == j
            row = jnp.where(at, 1.0, jnp.broadcast_to(V[ps][ii:ii+1, :], (8, 128)))
            splats = {k: jnp.broadcast_to(B[k, ps][ii:ii+1, :], (8, 128)) for k in range(i+1, 16)}
            for q in win:
                if q < ps or (q == ps and ii == 7): continue
                m = B[i, q] * inv
                if q == ps:
                    m = jnp.where(below[ii], m, 0.0)
                    z = jnp.where(at & below[ii], 0.0, V[q])
                else:
                    z = jnp.where(at, 0.0, V[q])
                V[q] = z - m * row
                for k in range(i+1, 16):
                    B[k, q] = B[k, q] - m * splats[k]
        scale += dinv
        rest = range(p0 + 2 + ahead, 16)
        if len(rest):
            G, Q = [], []
            for s in range(2):
                r = sub + (j0 + 8 * s)
                v = V[p0 + s]
                Q.append(v * dinv[s])
                inwin = (lane >= j0) & (lane < j0 + 16)
                G.append(jnp.where(inwin, jnp.where(lane < r, v, jnp.where(lane == r, 1.0, 0.0)), v))
            Gc, Qc = jnp.concatenate(G, 0), jnp.concatenate(Q, 0)
            gh, gl = split(Gc); qh, ql = split(Qc)
            upd = lax.dot_general(jnp.concatenate([qh, qh, ql], 0), jnp.concatenate([gh, gl, gh], 0),
                                  (((0,), (0,)), ((), ())), preferred_element_type=f32)
            zw = (lane >= j0) & (lane < j0 + 16)
            for q in rest:
                V[q] = jnp.where(zw, 0.0, V[q]) - upd[8*q:8*q+8]
    out = []
    for p in range(16):
        r = sub + 8 * p
        s = jnp.sqrt(scale[p])
        out.append(jnp.where(lane < r, V[p] * s, jnp.where(lane == r, s, 0.0)))
    return out


def place(level):
    group = 16 << level
    cube_at = lax.axis_index("cube")
    position = lax.rem(cube_at, group)
    return group, position, cube_at // group, position // (group // 2)


def assemble_kernel(level, *refs):
    maps, diag, mine, other = refs[:4]
    extra = refs[4] if level == 2 else None
    piv_out, coupled_out, upd_out, map_row, diag_row = refs[-5:]
    group, position, front_at, side = place(level)
    panel_at = lax.axis_index("panel")
    r = U // (group * PANELS)
    k = K // (group * PANELS)
    map_base = (0, 8, 12)[level]
    diag_base = (0, 4, 6)[level]
    block = lax.rem(position, group // 2) * PANELS + panel_at
    parent = position * PANELS + panel_at
    map_row[0:1, :] = maps[pl.ds(map_base + 2 * front_at + side, 1), :]
    map_row[1:2, :] = maps[pl.ds(map_base + 2 * front_at + 1 - side, 1), :]
    diag_row[0:1, :] = diag[pl.ds(diag_base + front_at, 1), :]
    lane = lax.broadcasted_iota(i32, (1, 128), 1)
    height = 16 + r

    def row_choice(half):
        start = block * (2 * r)
        tile = map_row[half:half + 1, pl.ds(pl.multiple_of(start // 128 * 128, 128), 128)]
        shift = lax.rem(128 - lax.rem(start + half * r, 128), 128)
        t = pltpu.roll(jnp.broadcast_to(tile, (8, 128)), shift, 1)[:1, :r]
        slot = jnp.where(t < K, t - parent * k, 16 + t - K - parent * r)
        rows = lax.broadcasted_iota(i32, (height, r), 0)
        return (rows == slot).astype(f32).astype(bf16)

    sel = (row_choice(0), row_choice(1))
    sides = (side, 1 - side)
    spread = lax.broadcasted_iota(i32, (128, 256), 0)
    piv_acc = [None, None]
    out_rows = lax.broadcasted_iota(i32, (height, 128), 0)
    upd_row_id = parent * r + out_rows - 16
    piv_row_id = parent * k + out_rows
    for c in range(16):
        xs, ss = [], []
        for which, ref in enumerate((mine, other)):
            x = ref[:, c * 256:(c + 1) * 256]
            hi, lo = (x, jnp.zeros_like(x)) if x.dtype == bf16 else split(x)
            pick = lambda y: jnp.dot(sel[which], y, preferred_element_type=f32).astype(bf16)
            xs.append(jnp.concatenate([pick(hi), pick(lo)], axis=0))
            m = map_row[which:which + 1, c * 256:(c + 1) * 256]
            onehots = [
                spread == m - (K + s * (U // 2) + c * 128) for s in sides
            ] + [spread == m - (s * (K // 2) + c // 8 * 128) for s in sides]
            ss.append(jnp.concatenate([o.astype(f32).astype(bf16) for o in onehots], axis=0))
        res = lax.dot_general(
            jnp.concatenate(xs, axis=1), jnp.concatenate(ss, axis=1),
            (((1,), (1,)), ((), ())), preferred_element_type=f32,
        )
        res = res[:height] + res[height:]
        upd_col = side * (U // 2) + c * 128 + lane
        d = diag_row[0:1, pl.ds(pl.multiple_of(K + side * (U // 2) + c * 128, 128), 128)]
        own = res[:, :128] + jnp.where(upd_row_id == upd_col, d, 0.0)
        for at, tile in ((side, own), (1 - side, res[:, 128:256])):
            cols = pl.ds(pl.multiple_of(at * (U // 2) + c * 128, 128), 128)
            value = tile[16:]
            if extra is not None:
                value += extra[:, pl.ds(pl.multiple_of(K + at * (U // 2) + c * 128, 128), 128)]
            upd_out[:, cols] = value
        for n in range(2):
            part = res[:, 256 + n * 128:384 + n * 128]
            piv_acc[n] = part if c % 8 == 0 else piv_acc[n] + part
        if c % 8 == 7:
            half = c // 8
            col = side * (K // 2) + half * 128 + lane
            d = diag_row[0:1, pl.ds(pl.multiple_of(side * (K // 2) + half * 128, 128), 128)]
            piv_acc[0] += jnp.where((piv_row_id == col) & (out_rows < 16), d, 0.0)
            for n, at in enumerate((side, 1 - side)):
                cols = pl.ds(pl.multiple_of(at * (K // 2) + half * 128, 128), 128)
                value = piv_acc[n][16:]
                if extra is not None:
                    value += extra[:, cols]
                coupled_out[:, cols] = value
                piv_out[pl.ds(2 * at + half, k, stride=4), :] = piv_acc[n][:k]


def assemble(level, maps, diag, mine, other, extra):
    r = mine.shape[0]
    k = r // 8
    ins = (maps, diag, mine, other) + ((extra,) if level == 2 else ())
    return pl.pallas_call(
        functools.partial(assemble_kernel, level),
        out_shape=(
            jax.ShapeDtypeStruct((4 * k, 128), f32),
            jax.ShapeDtypeStruct((r, K), f32),
            jax.ShapeDtypeStruct((r, U), f32),
        ),
        in_specs=[VMEM] * len(ins),
        out_specs=(VMEM,) * 3,
        scratch_shapes=[pltpu.VMEM((8, U), i32), pltpu.VMEM((8, U + K), f32)],
        compiler_params=pltpu.CompilerParams(vmem_limit_bytes=40 * 2**20),
        cost_estimate=pl.CostEstimate(flops=2 * 10**9, bytes_accessed=4 * 10**6, transcendentals=0),
        name="assemble%d" % level,
    )(*ins)


def level_kernel(level, *refs):
    last = level == 2
    ysize = 1 << level
    piece, coupled, upd = refs[:3]
    order = refs[3] if last else None
    outs, scratch = refs[3 + last:5 + last], refs[5 + last:]
    own_out, second_out = outs
    a, w, fi, fj, prod, got, upd_in, send_sem, recv_sem = scratch
    r = coupled.shape[0]
    half = prod.shape[2]
    n = K
    cube_at = lax.axis_index("cube")
    zh = lax.axis_index("panel")
    place = lax.rem(cube_at, 8)
    core = lax.rem(cube_at, 2)
    x = lax.rem(cube_at // 2, 4)
    zl = lax.rem(cube_at // 8, 2)
    yfull = cube_at // 16
    y = lax.rem(yfull, ysize)
    ybase = yfull - y
    mine = (y * 2 + zl) * PANELS + zh

    def target(y, zl, w, zh):
        return {"cube": (ybase + y) * 16 + zl * 8 + w, "panel": zh}

    def turned(a, b, c):
        return target(lax.rem(y + a, ysize), lax.rem(zl + b, 2), place, lax.rem(zh + c, 4))

    z_peers = [turned(0, b, c) for b in range(2) for c in range(4) if b + c]
    v_peers = z_peers + [turned(d, b, c) for d in range(1, ysize) for b in range(2) for c in range(4)]
    w_places = [lax.rem(place + d, 8) for d in range(1, 8)]
    w_peers = [target(y, zl, q, zh) for q in w_places]
    cross_places, cross_peers = [], []
    if not last:
        bit = 1 << level
        across = yfull + bit - 2 * bit * lax.rem(yfull // bit, 2)
        cross_places = [place] + w_places
        cross_peers = [{"cube": across * 16 + zl * 8 + q, "panel": zh} for q in cross_places]
    everyone = v_peers + w_peers + cross_peers
    barrier = pltpu.get_barrier_semaphore()
    for peer in everyone:
        pl.semaphore_signal(barrier, inc=1, device_id=peer, device_id_type=pl.DeviceIdType.MESH)
    a[pl.ds(y, 1), pl.ds(zl, 1), pl.ds(x, 1), pl.ds(core, 1), pl.ds(zh, 1)] = piece[...][None, None, None, None, None]
    own = coupled[...]
    if last:
        move = (lax.broadcasted_iota(i32, (n, n), 0) == order[...]).astype(f32).astype(bf16)
        ch, cl = split(own)
        own = jnp.dot(ch, move, preferred_element_type=f32) + jnp.dot(cl, move, preferred_element_type=f32)
    own_rows = own.astype(bf16)[None]
    fi[pl.ds(place, 1)] = own_rows
    fj[pl.ds(mine, 1)] = own_rows
    pl.semaphore_wait(barrier, len(everyone))
    copies = []

    def send(src, dst, peer):
        copy = pltpu.make_async_remote_copy(
            src_ref=src, dst_ref=dst, send_sem=send_sem.at[len(copies)], recv_sem=recv_sem.at[len(copies)],
            device_id=peer, device_id_type=pl.DeviceIdType.MESH,
        )
        copy.start()
        copies.append(copy)
        return copy

    early = None
    stages = [
        (z_peers, a.at[y, zl, x, core, zh]),
        ([target(y, zl, lax.rem(x + d, 4) * 2 + core, zh) for d in range(1, 4)], a.at[y, :, x, core]),
        ([turned(d, 0, 0) for d in range(1, ysize)], a.at[y, :, :, core]),
        ([target(y, zl, x * 2 + 1 - core, zh)], a.at[:, :, :, core]),
    ]
    gathered = []
    for number, (peers, part) in enumerate(stages):
        started = [send(part, part, peer) for peer in peers]
        if number == 0 and not last:
            early = send(upd.at[half:], upd_in, cross_peers[0])
        if number == 1:
            gathered += [send(fj.at[mine], fj.at[mine], peer) for peer in v_peers]
        if number == 2:
            gathered += [send(fi.at[place], fi.at[place], peer) for peer in w_peers]
        for copy in started:
            copy.wait_recv()

    flat = a.reshape(4 * n, 128)
    if last:
        full = jnp.concatenate([flat[pl.ds(c, n, stride=4), :] for c in range(4)], axis=1)
        for part, source in enumerate(split(full)):
            cols = jnp.dot(source, move, preferred_element_type=f32).astype(bf16)
            both = lax.dot_general(move, cols, (((0,), (0,)), ((), ())), preferred_element_type=f32)
            if part == 0:
                w[:, :n] = both
            else:
                w[:, :n] += both
        w[:, n:] = jnp.concatenate([own, jnp.zeros((128 - r, n), f32)], axis=0).T
    else:
        for c in range(4):
            w[:, c * 128:(c + 1) * 128] = flat[pl.ds(c, n, stride=4), :]
    blocks = n // 128
    width = w.shape[1]
    first, second = ((0,), (0,)), ((1,), (0,))
    for b in range(blocks):
        lo, hi = b * 128, b * 128 + 128
        rows = [w[lo + 8 * p: lo + 8 * p + 8, lo:hi] for p in range(16)]
        inverse = jnp.concatenate(diag_inverse(rows), axis=0)
        if hi < width:
            solved = mm(inverse, w[lo:hi, hi:], second)
        for later in range(b + 1, blocks):
            off = (later - b - 1) * 128
            w[later * 128:later * 128 + 128, later * 128:] -= mm(solved[:, off:off + 128], solved[:, off:], first)
        if last:
            second_out[:, lo:hi] = solved[:, n - hi:].T[:r].astype(bf16)
        done = inverse
        if b:
            done = jnp.concatenate([mm(inverse, w[lo:hi, :lo], second), inverse], axis=1)
            w[lo:hi, :lo] = done[:, :lo]
        w[lo:hi, lo:hi] = inverse
        for later in range(b + 1, blocks):
            off = (later - b - 1) * 128
            part = mm(solved[:, off:off + 128], done, first)
            if b:
                w[later * 128:later * 128 + 128, :lo] -= part[:, :lo]
            w[later * 128:later * 128 + 128, lo:hi] = -part[:, lo:]

    for copy in gathered:
        copy.wait_recv()
    both = jnp.concatenate([fi[...].reshape(8 * r, n), fj[...].reshape(512, n)], axis=0)
    across_rows = ((1,), (1,))
    factors = []
    for b in range(blocks):
        hi = b * 128 + 128
        parts = [
            lax.dot_general(both[:, :hi], part, (across_rows, ((), ())), preferred_element_type=f32)
            for part in split(w[hi - 128:hi, :hi])
        ]
        factors.append((parts[0] + parts[1]).astype(bf16))
    factors = jnp.concatenate(factors, axis=1)
    product = lax.dot_general(
        factors[:8 * r], factors[8 * r:], (across_rows, ((), ())), preferred_element_type=f32
    ).astype(bf16).reshape(8, r, 512)
    for part in range(r // half):
        prod[part] = product[:, part * half:(part + 1) * half]
    back = [send(prod.at[0, q], got.at[0, place], peer) for q, peer in zip(w_places, w_peers)]
    back += [send(prod.at[1, q], got.at[1, place], peer) for q, peer in zip(cross_places, cross_peers)]
    got[0, pl.ds(place, 1)] = prod[0, pl.ds(place, 1)]
    if early is not None:
        early.wait_recv()
    for copy in back:
        copy.wait_recv()
    wide = PANELS * r
    for part in range(r // half):
        source = upd_in if part else upd
        out = second_out if part else own_out
        for block in range(2 * ysize):
            parts = [got[part, q, :, block * wide:(block + 1) * wide].astype(f32) for q in range(8)]
            lo = block * 8 * wide
            out[:, lo:lo + 8 * wide] = source[:half, lo:lo + 8 * wide] - jnp.concatenate(parts, axis=1)
    for copy in copies:
        copy.wait_send()


def eliminate(level, piece, coupled, update_rows, order):
    last = level == 2
    ysize = 1 << level
    r = coupled.shape[0]
    half = r if last else r // 2
    ins = (piece, coupled, update_rows) + ((order,) if last else ())
    second = jax.ShapeDtypeStruct((r, K), bf16) if last else jax.ShapeDtypeStruct((half, U), f32)
    v = 8 * ysize
    count = 7 + 3 + ysize - 1 + 1 + (v - 1 + 7) + 7 + (0 if last else 9)
    return pl.pallas_call(
        functools.partial(level_kernel, level),
        out_shape=(jax.ShapeDtypeStruct((half, U), f32), second),
        in_specs=[VMEM] * len(ins),
        out_specs=(VMEM, VMEM),
        scratch_shapes=[
            pltpu.VMEM((ysize, 2, 4, 2, 4) + piece.shape, f32),
            pltpu.VMEM((K, K + (128 if last else 0)), f32),
            pltpu.VMEM((8, r, K), bf16),
            pltpu.VMEM((v, r, K), bf16),
            pltpu.VMEM((r // half, 8, half, 512), bf16),
            pltpu.VMEM((r // half, 8, half, 512), bf16),
            pltpu.VMEM((half, U), f32),
            pltpu.SemaphoreType.DMA((count,)), pltpu.SemaphoreType.DMA((count,)),
        ],
        compiler_params=pltpu.CompilerParams(
            collective_id=level, has_side_effects=True, vmem_limit_bytes=40 * 2**20
        ),
        cost_estimate=pl.CostEstimate(flops=3 * 10**10, bytes_accessed=150 * 10**6, transcendentals=0),
        name="level%d" % level,
    )(*ins)


def from_partner(shard, stride):
    return lax.ppermute(shard, "cube", [(i, i ^ 1 << stride) for i in range(64)])


def plane_of(owner):
    cube, zh = owner // PANELS, lax.rem(owner, PANELS)
    cls = cube // 16 * 8 + lax.rem(cube, 8)
    return cls, lax.rem(cube // 8, 2) * PANELS + zh


def route_plane(coupling_rows, coupling_owner, coupling_slot):
    cls, z = plane_of(coupling_owner[:, 0])
    m = coupling_rows.shape[0]
    hits = (cls[:, None] == jnp.arange(32, dtype=i32)[None, :]).astype(bf16)
    before = (jnp.arange(m)[:, None] > jnp.arange(m)[None, :]).astype(bf16)
    earlier = jnp.dot(before, hits, preferred_element_type=f32)
    earlier = jnp.sum(earlier * hits.astype(f32), axis=1).astype(i32)
    target = cls * 16 + earlier
    choose = (target[None, :] == jnp.arange(512, dtype=i32)[:, None]).astype(bf16)
    marks = (z * 16 + coupling_slot)[:, None] == jnp.arange(128, dtype=i32)[None, :]
    payload = jnp.concatenate([coupling_rows, marks.astype(bf16)], axis=1)
    outgoing = jnp.dot(choose, payload, preferred_element_type=f32).astype(bf16)
    outgoing = outgoing.reshape(32, 16, -1)
    groups = [[y * 16 + zl * 8 + xc for y in range(4) for xc in range(8)] for zl in range(2)]
    return lax.all_to_all(outgoing, "cube", 0, 0, axis_index_groups=groups, tiled=True)


def route_column(got):
    got = got.reshape(512, -1)
    sums = lax.dot_general(
        got[:, U + K:], got[:, :U + K], (((0,), (0,)), ((), ())), preferred_element_type=f32
    ).astype(bf16).reshape(8, 16, U + K)
    groups = [
        [(y * 16 + zl * 8 + xc) * PANELS + zh for zl in range(2) for zh in range(PANELS)]
        for y in range(4) for xc in range(8)
    ]
    return lax.all_to_all(sums, ("cube", "panel"), 0, 0, axis_index_groups=groups, tiled=True)


def body(leaf_updates, extend_maps, front_diagonal, pivot_order, coupling_rows, coupling_owner, coupling_slot):
    routed = route_plane(coupling_rows, coupling_owner, coupling_slot)
    assembly = None
    r = leaf_updates.shape[0] // 2
    own, incoming = leaf_updates[:r], from_partner(leaf_updates[r:].astype(bf16), 3)
    order = pivot_order.reshape(1, K)
    for level in range(3):
        if level == 2:
            assembly = jnp.sum(routed.astype(f32), axis=0)
        piece, coupled, update_rows = assemble(
            level, extend_maps, front_diagonal, own, incoming, assembly
        )
        own, incoming = eliminate(level, piece, coupled, update_rows, order)
        if level == 0:
            routed, own = lax.optimization_barrier((routed, own))
            routed = route_column(routed)
    return (incoming, own)


def solution(mesh):
    return jax.shard_map(
        body,
        mesh=mesh,
        in_specs=(
            P(("cube", "panel"), None), P(), P(), P(),
            P(("cube", "panel"), None), P(("cube", "panel"), None), P(("cube", "panel")),
        ),
        out_specs=(P(("cube", "panel"), None), P(("cube", "panel"), None)),
        check_vma=False,
    )
```

```python
import functools
import jax
import jax.numpy as jnp
from jax import lax
from jax.experimental import pallas as pl
from jax.experimental.pallas import tpu as pltpu
from jax.sharding import PartitionSpec as P

CAP = 2
K = 512
U = 4096
PANELS = 4
f32, bf16, i32 = jnp.float32, jnp.bfloat16, jnp.int32
VMEM = pl.BlockSpec(memory_space=pltpu.VMEM)


def split(x):
    hi = x.astype(bf16)
    return hi, (x - hi.astype(f32)).astype(bf16)

def mm(x, y, dims):
    xh, xl = split(x); yh, yl = split(y)
    d = functools.partial(lax.dot_general, dimension_numbers=(dims, ((), ())), preferred_element_type=f32)
    return d(xh, yh) + (d(xh, yl) + d(xl, yh))

def diag_inverse(V, ahead=2):
    V = list(V)
    lane = lax.broadcasted_iota(jnp.int32, (8, 128), 1)
    sub = lax.broadcasted_iota(jnp.int32, (8, 128), 0)
    below = [sub > i for i in range(8)]
    scale = []
    for g in range(8):
        p0, j0 = 2 * g, 16 * g
        win = [q for q in range(p0, min(p0 + 2 + ahead, 16))]
        B = {(k, q): jnp.broadcast_to(V[q][:, j0+k:j0+k+1], (8, 128)) for k in range(16) for q in win}
        dinv = [None, None]
        for i in range(16):
            s, ii = divmod(i, 8)
            ps = p0 + s
            j = j0 + i
            inv = 1.0 / jnp.broadcast_to(B[i, ps][ii:ii+1, :], (8, 128))
            dinv[s] = inv if ii == 0 else jnp.where(below[ii-1], inv, dinv[s])
            at = lane == j
            row = jnp.where(at, 1.0, jnp.broadcast_to(V[ps][ii:ii+1, :], (8, 128)))
            splats = {k: jnp.broadcast_to(B[k, ps][ii:ii+1, :], (8, 128)) for k in range(i+1, 16)}
            for q in win:
                if q < ps or (q == ps and ii == 7): continue
                m = B[i, q] * inv
                if q == ps:
                    m = jnp.where(below[ii], m, 0.0)
                    z = jnp.where(at & below[ii], 0.0, V[q])
                else:
                    z = jnp.where(at, 0.0, V[q])
                V[q] = z - m * row
                for k in range(i+1, 16):
                    B[k, q] = B[k, q] - m * splats[k]
        scale += dinv
        rest = range(p0 + 2 + ahead, 16)
        if len(rest):
            G, Q = [], []
            for s in range(2):
                r = sub + (j0 + 8 * s)
                v = V[p0 + s]
                Q.append(v * dinv[s])
                inwin = (lane >= j0) & (lane < j0 + 16)
                G.append(jnp.where(inwin, jnp.where(lane < r, v, jnp.where(lane == r, 1.0, 0.0)), v))
            Gc, Qc = jnp.concatenate(G, 0), jnp.concatenate(Q, 0)
            gh, gl = split(Gc); qh, ql = split(Qc)
            upd = lax.dot_general(jnp.concatenate([qh, qh, ql], 0), jnp.concatenate([gh, gl, gh], 0),
                                  (((0,), (0,)), ((), ())), preferred_element_type=f32)
            zw = (lane >= j0) & (lane < j0 + 16)
            for q in rest:
                V[q] = jnp.where(zw, 0.0, V[q]) - upd[8*q:8*q+8]
    out = []
    for p in range(16):
        r = sub + 8 * p
        s = jnp.sqrt(scale[p])
        out.append(jnp.where(lane < r, V[p] * s, jnp.where(lane == r, s, 0.0)))
    return out


def place(level):
    group = 16 << level
    cube_at = lax.axis_index("cube")
    position = lax.rem(cube_at, group)
    return group, position, cube_at // group, position // (group // 2)


def assemble_kernel(level, *refs):
    maps, diag, mine, other = refs[:4]
    extra = refs[4] if level == 2 else None
    piv_out, coupled_out, upd_out, map_row, diag_row = refs[-5:]
    group, position, front_at, side = place(level)
    panel_at = lax.axis_index("panel")
    r = U // (group * PANELS)
    k = K // (group * PANELS)
    map_base = (0, 8, 12)[level]
    diag_base = (0, 4, 6)[level]
    block = lax.rem(position, group // 2) * PANELS + panel_at
    parent = position * PANELS + panel_at
    map_row[0:1, :] = maps[pl.ds(map_base + 2 * front_at + side, 1), :]
    map_row[1:2, :] = maps[pl.ds(map_base + 2 * front_at + 1 - side, 1), :]
    diag_row[0:1, :] = diag[pl.ds(diag_base + front_at, 1), :]
    lane = lax.broadcasted_iota(i32, (1, 128), 1)
    height = 16 + r

    def row_choice(half):
        start = block * (2 * r)
        tile = map_row[half:half + 1, pl.ds(pl.multiple_of(start // 128 * 128, 128), 128)]
        shift = lax.rem(128 - lax.rem(start + half * r, 128), 128)
        t = pltpu.roll(jnp.broadcast_to(tile, (8, 128)), shift, 1)[:1, :r]
        slot = jnp.where(t < K, t - parent * k, 16 + t - K - parent * r)
        rows = lax.broadcasted_iota(i32, (height, r), 0)
        return (rows == slot).astype(f32).astype(bf16)

    sel = (row_choice(0), row_choice(1))
    sides = (side, 1 - side)
    spread = lax.broadcasted_iota(i32, (128, 256), 0)
    piv_acc = [None, None]
    out_rows = lax.broadcasted_iota(i32, (height, 128), 0)
    upd_row_id = parent * r + out_rows - 16
    piv_row_id = parent * k + out_rows
    for c in range(16):
        xs, ss = [], []
        for which, ref in enumerate((mine, other)):
            x = ref[:, c * 256:(c + 1) * 256]
            hi, lo = (x, jnp.zeros_like(x)) if x.dtype == bf16 else split(x)
            pick = lambda y: jnp.dot(sel[which], y, preferred_element_type=f32).astype(bf16)
            xs.append(jnp.concatenate([pick(hi), pick(lo)], axis=0))
            m = map_row[which:which + 1, c * 256:(c + 1) * 256]
            onehots = [
                spread == m - (K + s * (U // 2) + c * 128) for s in sides
            ] + [spread == m - (s * (K // 2) + c // 8 * 128) for s in sides]
            ss.append(jnp.concatenate([o.astype(f32).astype(bf16) for o in onehots], axis=0))
        res = lax.dot_general(
            jnp.concatenate(xs, axis=1), jnp.concatenate(ss, axis=1),
            (((1,), (1,)), ((), ())), preferred_element_type=f32,
        )
        res = res[:height] + res[height:]
        upd_col = side * (U // 2) + c * 128 + lane
        d = diag_row[0:1, pl.ds(pl.multiple_of(K + side * (U // 2) + c * 128, 128), 128)]
        own = res[:, :128] + jnp.where(upd_row_id == upd_col, d, 0.0)
        for at, tile in ((side, own), (1 - side, res[:, 128:256])):
            cols = pl.ds(pl.multiple_of(at * (U // 2) + c * 128, 128), 128)
            value = tile[16:]
            if extra is not None:
                value += extra[:, pl.ds(pl.multiple_of(K + at * (U // 2) + c * 128, 128), 128)]
            upd_out[:, cols] = value
        for n in range(2):
            part = res[:, 256 + n * 128:384 + n * 128]
            piv_acc[n] = part if c % 8 == 0 else piv_acc[n] + part
        if c % 8 == 7:
            half = c // 8
            col = side * (K // 2) + half * 128 + lane
            d = diag_row[0:1, pl.ds(pl.multiple_of(side * (K // 2) + half * 128, 128), 128)]
            piv_acc[0] += jnp.where((piv_row_id == col) & (out_rows < 16), d, 0.0)
            for n, at in enumerate((side, 1 - side)):
                cols = pl.ds(pl.multiple_of(at * (K // 2) + half * 128, 128), 128)
                value = piv_acc[n][16:]
                if extra is not None:
                    value += extra[:, cols]
                coupled_out[:, cols] = value
                piv_out[pl.ds(2 * at + half, k, stride=4), :] = piv_acc[n][:k]


def assemble(level, maps, diag, mine, other, extra):
    r = mine.shape[0]
    k = r // 8
    ins = (maps, diag, mine, other) + ((extra,) if level == 2 else ())
    return pl.pallas_call(
        functools.partial(assemble_kernel, level),
        out_shape=(
            jax.ShapeDtypeStruct((4 * k, 128), f32),
            jax.ShapeDtypeStruct((r, K), f32),
            jax.ShapeDtypeStruct((r, U), f32),
        ),
        in_specs=[VMEM] * len(ins),
        out_specs=(VMEM,) * 3,
        scratch_shapes=[pltpu.VMEM((8, U), i32), pltpu.VMEM((8, U + K), f32)],
        compiler_params=pltpu.CompilerParams(vmem_limit_bytes=40 * 2**20),
        cost_estimate=pl.CostEstimate(flops=2 * 10**9, bytes_accessed=4 * 10**6, transcendentals=0),
        name="assemble%d" % level,
    )(*ins)


def level_kernel(level, *refs):
    last = level == 2
    ysize = 1 << level
    piece, coupled, upd = refs[:3]
    if last:
        order, own_out, second_out = refs[3:6]
        a, w, fi, fj, prod, got, upd_in, send_sem, recv_sem = refs[6:]
    else:
        routed, own_out, second_out, routed_out = refs[3:7]
        a, w, fi, fj, prod, got, upd_in, send_sem, recv_sem, landing = refs[7:]
    r = coupled.shape[0]
    half = prod.shape[2]
    n = K
    cube_at = lax.axis_index("cube")
    zh = lax.axis_index("panel")
    place = lax.rem(cube_at, 8)
    core = lax.rem(cube_at, 2)
    x = lax.rem(cube_at // 2, 4)
    zl = lax.rem(cube_at // 8, 2)
    yfull = cube_at // 16
    y = lax.rem(yfull, ysize)
    ybase = yfull - y
    mine = (y * 2 + zl) * PANELS + zh

    def target(y, zl, w, zh):
        return {"cube": (ybase + y) * 16 + zl * 8 + w, "panel": zh}

    def turned(a, b, c):
        return target(lax.rem(y + a, ysize), lax.rem(zl + b, 2), place, lax.rem(zh + c, 4))

    z_peers = [turned(0, b, c) for b in range(2) for c in range(4) if b + c]
    v_peers = z_peers + [turned(d, b, c) for d in range(1, ysize) for b in range(2) for c in range(4)]
    w_places = [lax.rem(place + d, 8) for d in range(1, 8)]
    w_peers = [target(y, zl, q, zh) for q in w_places]
    cross_places, cross_peers = [], []
    if not last:
        bit = 1 << level
        across = yfull + bit - 2 * bit * lax.rem(yfull // bit, 2)
        cross_places = [place] + w_places
        cross_peers = [{"cube": across * 16 + zl * 8 + q, "panel": zh} for q in cross_places]
    plane_places, plane_peers = [], []
    if level == 0:
        for dy in range(4):
            for q in [place] + w_places if dy else w_places:
                to_y = lax.rem(yfull + dy, 4)
                plane_places.append(to_y * 8 + q)
                plane_peers.append({"cube": to_y * 16 + zl * 8 + q, "panel": zh})
    everyone = v_peers + (plane_peers if level == 0 else w_peers + cross_peers)
    barrier = pltpu.get_barrier_semaphore()
    for peer in everyone:
        pl.semaphore_signal(barrier, inc=1, device_id=peer, device_id_type=pl.DeviceIdType.MESH)
    a[pl.ds(y, 1), pl.ds(zl, 1), pl.ds(x, 1), pl.ds(core, 1), pl.ds(zh, 1)] = piece[...][None, None, None, None, None]
    own = coupled[...]
    if last:
        move = (lax.broadcasted_iota(i32, (n, n), 0) == order[...]).astype(f32).astype(bf16)
        ch, cl = split(own)
        own = jnp.dot(ch, move, preferred_element_type=f32) + jnp.dot(cl, move, preferred_element_type=f32)
    own_rows = own.astype(bf16)[None]
    fi[pl.ds(place, 1)] = own_rows
    fj[pl.ds(mine, 1)] = own_rows
    pl.semaphore_wait(barrier, len(everyone))
    copies = []

    def send(src, dst, peer):
        copy = pltpu.make_async_remote_copy(
            src_ref=src, dst_ref=dst, send_sem=send_sem.at[len(copies)], recv_sem=recv_sem.at[len(copies)],
            device_id=peer, device_id_type=pl.DeviceIdType.MESH,
        )
        copy.start()
        copies.append(copy)
        return copy

    early = None
    stages = [
        (z_peers, a.at[y, zl, x, core, zh]),
        ([target(y, zl, lax.rem(x + d, 4) * 2 + core, zh) for d in range(1, 4)], a.at[y, :, x, core]),
        ([turned(d, 0, 0) for d in range(1, ysize)], a.at[y, :, :, core]),
        ([target(y, zl, x * 2 + 1 - core, zh)], a.at[:, :, :, core]),
    ]
    gathered = []
    for number, (peers, part) in enumerate(stages):
        started = [send(part, part, peer) for peer in peers]
        if number == 0 and not last:
            early = send(upd.at[half:], upd_in, cross_peers[0])
        if number == 1:
            gathered += [send(fj.at[mine], fj.at[mine], peer) for peer in v_peers]
        if number == 2:
            gathered += [send(fi.at[place], fi.at[place], peer) for peer in w_peers]
        for copy in started:
            copy.wait_recv()

    if level == 0:
        spot = yfull * 8 + place
        coupling = [send(routed.at[q], landing.at[spot], peer) for q, peer in zip(plane_places, plane_peers)]
    elif level == 1:
        spot = zl * PANELS + zh
        turns = [(b, c) for b in range(2) for c in range(4) if b + c]
        coupling = [
            send(routed.at[lax.rem(zl + b, 2) * PANELS + lax.rem(zh + c, 4)], landing.at[spot], peer)
            for (b, c), peer in zip(turns, z_peers)
        ]
    if not last:
        landing[pl.ds(spot, 1)] = routed[pl.ds(spot, 1)]
    flat = a.reshape(4 * n, 128)
    if last:
        full = jnp.concatenate([flat[pl.ds(c, n, stride=4), :] for c in range(4)], axis=1)
        for part, source in enumerate(split(full)):
            cols = jnp.dot(source, move, preferred_element_type=f32).astype(bf16)
            both = lax.dot_general(move, cols, (((0,), (0,)), ((), ())), preferred_element_type=f32)
            if part == 0:
                w[:, :n] = both
            else:
                w[:, :n] += both
        w[:, n:] = jnp.concatenate([own, jnp.zeros((128 - r, n), f32)], axis=0).T
    else:
        for c in range(4):
            w[:, c * 128:(c + 1) * 128] = flat[pl.ds(c, n, stride=4), :]
    blocks = n // 128
    width = w.shape[1]
    first, second = ((0,), (0,)), ((1,), (0,))
    for b in range(blocks):
        lo, hi = b * 128, b * 128 + 128
        rows = [w[lo + 8 * p: lo + 8 * p + 8, lo:hi] for p in range(16)]
        inverse = jnp.concatenate(diag_inverse(rows), axis=0)
        if hi < width:
            solved = mm(inverse, w[lo:hi, hi:], second)
        for later in range(b + 1, blocks):
            off = (later - b - 1) * 128
            w[later * 128:later * 128 + 128, later * 128:] -= mm(solved[:, off:off + 128], solved[:, off:], first)
        if last:
            second_out[:, lo:hi] = solved[:, n - hi:].T[:r].astype(bf16)
        done = inverse
        if b:
            done = jnp.concatenate([mm(inverse, w[lo:hi, :lo], second), inverse], axis=1)
            w[lo:hi, :lo] = done[:, :lo]
        w[lo:hi, lo:hi] = inverse
        for later in range(b + 1, blocks):
            off = (later - b - 1) * 128
            part = mm(solved[:, off:off + 128], done, first)
            if b:
                w[later * 128:later * 128 + 128, :lo] -= part[:, :lo]
            w[later * 128:later * 128 + 128, lo:hi] = -part[:, lo:]

    for copy in gathered:
        copy.wait_recv()
    both = jnp.concatenate([fi[...].reshape(8 * r, n), fj[...].reshape(512, n)], axis=0)
    across_rows = ((1,), (1,))
    factors = []
    for b in range(blocks):
        hi = b * 128 + 128
        parts = [
            lax.dot_general(both[:, :hi], part, (across_rows, ((), ())), preferred_element_type=f32)
            for part in split(w[hi - 128:hi, :hi])
        ]
        factors.append((parts[0] + parts[1]).astype(bf16))
    factors = jnp.concatenate(factors, axis=1)
    product = lax.dot_general(
        factors[:8 * r], factors[8 * r:], (across_rows, ((), ())), preferred_element_type=f32
    ).astype(bf16).reshape(8, r, 512)
    for part in range(r // half):
        prod[part] = product[:, part * half:(part + 1) * half]
    back = [send(prod.at[0, q], got.at[0, place], peer) for q, peer in zip(w_places, w_peers)]
    back += [send(prod.at[1, q], got.at[1, place], peer) for q, peer in zip(cross_places, cross_peers)]
    got[0, pl.ds(place, 1)] = prod[0, pl.ds(place, 1)]
    if early is not None:
        early.wait_recv()
    for copy in back:
        copy.wait_recv()
    wide = PANELS * r
    for part in range(r // half):
        source = upd_in if part else upd
        out = second_out if part else own_out
        for block in range(2 * ysize):
            parts = [got[part, q, :, block * wide:(block + 1) * wide].astype(f32) for q in range(8)]
            lo = block * 8 * wide
            out[:, lo:lo + 8 * wide] = source[:half, lo:lo + 8 * wide] - jnp.concatenate(parts, axis=1)
    if not last:
        for copy in coupling:
            copy.wait_recv()
    if level == 0:
        marks = landing[:, :, U + K:].reshape(512, 128)
        for c in range(9):
            rows = landing[:, :, c * 512:(c + 1) * 512].reshape(512, 512)
            sums = lax.dot_general(marks, rows, (((0,), (0,)), ((), ())), preferred_element_type=f32)
            routed_out[:, :, c * 512:(c + 1) * 512] = sums.astype(bf16).reshape(8, 16, 512)
    elif level == 1:
        total = landing[0].astype(f32)
        for q in range(1, 8):
            total = total + landing[q].astype(f32)
        routed_out[...] = total
    for copy in copies:
        copy.wait_send()


def eliminate(level, piece, coupled, update_rows, extra):
    last = level == 2
    ysize = 1 << level
    r = coupled.shape[0]
    half = r if last else r // 2
    ins = (piece, coupled, update_rows, extra)
    second = jax.ShapeDtypeStruct((r, K), bf16) if last else jax.ShapeDtypeStruct((half, U), f32)
    v = 8 * ysize
    count = 7 + 3 + ysize - 1 + 1 + (v - 1 + 7) + 7 + (31 + 9, 7 + 9, 0)[level]
    outs = (jax.ShapeDtypeStruct((half, U), f32), second)
    if level == 0:
        outs += (jax.ShapeDtypeStruct((8, 16, U + K), bf16),)
    elif level == 1:
        outs += (jax.ShapeDtypeStruct((16, U + K), f32),)
    return pl.pallas_call(
        functools.partial(level_kernel, level),
        out_shape=outs,
        in_specs=[VMEM] * len(ins),
        out_specs=(VMEM,) * len(outs),
        scratch_shapes=[
            pltpu.VMEM((ysize, 2, 4, 2, 4) + piece.shape, f32),
            pltpu.VMEM((K, K + (128 if last else 0)), f32),
            pltpu.VMEM((8, r, K), bf16),
            pltpu.VMEM((v, r, K), bf16),
            pltpu.VMEM((r // half, 8, half, 512), bf16),
            pltpu.VMEM((r // half, 8, half, 512), bf16),
            pltpu.VMEM((half, U), f32),
            pltpu.SemaphoreType.DMA((count,)), pltpu.SemaphoreType.DMA((count,)),
        ] + ([] if last else [pltpu.VMEM(extra.shape, bf16)]),
        compiler_params=pltpu.CompilerParams(
            collective_id=level, has_side_effects=True, vmem_limit_bytes=48 * 2**20
        ),
        cost_estimate=pl.CostEstimate(flops=3 * 10**10, bytes_accessed=150 * 10**6, transcendentals=0),
        name="level%d" % level,
    )(*ins)


def from_partner(shard, stride):
    return lax.ppermute(shard, "cube", [(i, i ^ 1 << stride) for i in range(64)])


def plane_of(owner):
    cube, zh = owner // PANELS, lax.rem(owner, PANELS)
    cls = cube // 16 * 8 + lax.rem(cube, 8)
    return cls, lax.rem(cube // 8, 2) * PANELS + zh


def route_plane(coupling_rows, coupling_owner, coupling_slot):
    cls, z = plane_of(coupling_owner[:, 0])
    m = coupling_rows.shape[0]
    hits = (cls[:, None] == jnp.arange(32, dtype=i32)[None, :]).astype(bf16)
    before = (jnp.arange(m)[:, None] > jnp.arange(m)[None, :]).astype(bf16)
    earlier = jnp.dot(before, hits, preferred_element_type=f32)
    earlier = jnp.sum(earlier * hits.astype(f32), axis=1).astype(i32)
    target = cls * 16 + earlier
    choose = (target[None, :] == jnp.arange(512, dtype=i32)[:, None]).astype(bf16)
    marks = (z * 16 + coupling_slot)[:, None] == jnp.arange(128, dtype=i32)[None, :]
    payload = jnp.concatenate([coupling_rows, marks.astype(bf16)], axis=1)
    outgoing = jnp.dot(choose, payload, preferred_element_type=f32).astype(bf16)
    outgoing = outgoing.reshape(32, 16, -1)
    return outgoing


def body(leaf_updates, extend_maps, front_diagonal, pivot_order, coupling_rows, coupling_owner, coupling_slot):
    r = leaf_updates.shape[0] // 2
    own, incoming = leaf_updates[:r], from_partner(leaf_updates[r:].astype(bf16), 3)
    extra = route_plane(coupling_rows, coupling_owner, coupling_slot)
    for level in range(3):
        piece, coupled, update_rows = assemble(
            level, extend_maps, front_diagonal, own, incoming, extra
        )
        if level == 2:
            extra = pivot_order.reshape(1, K)
        own, incoming, *rest = eliminate(level, piece, coupled, update_rows, extra)
        extra = rest[0] if rest else None
    return (incoming, own)


def solution(mesh):
    return jax.shard_map(
        body,
        mesh=mesh,
        in_specs=(
            P(("cube", "panel"), None), P(), P(), P(),
            P(("cube", "panel"), None), P(("cube", "panel"), None), P(("cube", "panel")),
        ),
        out_specs=(P(("cube", "panel"), None), P(("cube", "panel"), None)),
        check_vma=False,
    )
```

```python
import functools
import jax
import jax.numpy as jnp
from jax import lax
from jax.experimental import pallas as pl
from jax.experimental.pallas import tpu as pltpu
from jax.sharding import PartitionSpec as P

CAP = 2
K = 512
U = 4096
PANELS = 4
f32, bf16, i32 = jnp.float32, jnp.bfloat16, jnp.int32
VMEM = pl.BlockSpec(memory_space=pltpu.VMEM)


def split(x):
    hi = x.astype(bf16)
    return hi, (x - hi.astype(f32)).astype(bf16)

def mm(x, y, dims):
    xh, xl = split(x); yh, yl = split(y)
    d = functools.partial(lax.dot_general, dimension_numbers=(dims, ((), ())), preferred_element_type=f32)
    return d(xh, yh) + (d(xh, yl) + d(xl, yh))

def diag_inverse(V, ahead=2):
    V = list(V)
    lane = lax.broadcasted_iota(jnp.int32, (8, 128), 1)
    sub = lax.broadcasted_iota(jnp.int32, (8, 128), 0)
    below = [sub > i for i in range(8)]
    scale = []
    for g in range(8):
        p0, j0 = 2 * g, 16 * g
        win = [q for q in range(p0, min(p0 + 2 + ahead, 16))]
        B = {(k, q): jnp.broadcast_to(V[q][:, j0+k:j0+k+1], (8, 128)) for k in range(16) for q in win}
        dinv = [None, None]
        for i in range(16):
            s, ii = divmod(i, 8)
            ps = p0 + s
            j = j0 + i
            inv = 1.0 / jnp.broadcast_to(B[i, ps][ii:ii+1, :], (8, 128))
            dinv[s] = inv if ii == 0 else jnp.where(below[ii-1], inv, dinv[s])
            at = lane == j
            row = jnp.where(at, 1.0, jnp.broadcast_to(V[ps][ii:ii+1, :], (8, 128)))
            splats = {k: jnp.broadcast_to(B[k, ps][ii:ii+1, :], (8, 128)) for k in range(i+1, 16)}
            for q in win:
                if q < ps or (q == ps and ii == 7): continue
                m = B[i, q] * inv
                if q == ps:
                    m = jnp.where(below[ii], m, 0.0)
                    z = jnp.where(at & below[ii], 0.0, V[q])
                else:
                    z = jnp.where(at, 0.0, V[q])
                V[q] = z - m * row
                for k in range(i+1, 16):
                    B[k, q] = B[k, q] - m * splats[k]
        scale += dinv
        rest = range(p0 + 2 + ahead, 16)
        if len(rest):
            G, Q = [], []
            for s in range(2):
                r = sub + (j0 + 8 * s)
                v = V[p0 + s]
                Q.append(v * dinv[s])
                inwin = (lane >= j0) & (lane < j0 + 16)
                G.append(jnp.where(inwin, jnp.where(lane < r, v, jnp.where(lane == r, 1.0, 0.0)), v))
            Gc, Qc = jnp.concatenate(G, 0), jnp.concatenate(Q, 0)
            gh, gl = split(Gc); qh, ql = split(Qc)
            upd = lax.dot_general(jnp.concatenate([qh, qh, ql], 0), jnp.concatenate([gh, gl, gh], 0),
                                  (((0,), (0,)), ((), ())), preferred_element_type=f32)
            zw = (lane >= j0) & (lane < j0 + 16)
            for q in rest:
                V[q] = jnp.where(zw, 0.0, V[q]) - upd[8*q:8*q+8]
    out = []
    for p in range(16):
        r = sub + 8 * p
        s = jnp.sqrt(scale[p])
        out.append(jnp.where(lane < r, V[p] * s, jnp.where(lane == r, s, 0.0)))
    return out


PART = 2304
PLANE_TURNS = (
    2, 8, 6, 24, 10, 30, 14, 26, 4, 16, 12, 18, 28, 22, 20, 1, 3, 9, 7, 25, 11, 31, 15, 27, 5, 17, 13, 19, 29, 23, 21,
)


def place(level):
    group = 16 << level
    cube_at = lax.axis_index("cube")
    position = lax.rem(cube_at, group)
    return group, position, cube_at // group, position // (group // 2)


def assemble_kernel(level, *refs):
    maps, diag, mine, other = refs[:4]
    extra = refs[4] if level == 2 else None
    piv_out, coupled_out, upd_out, map_row, diag_row = refs[-5:]
    group, position, front_at, side = place(level)
    panel_at = lax.axis_index("panel")
    r = U // (group * PANELS)
    k = K // (group * PANELS)
    map_base = (0, 8, 12)[level]
    diag_base = (0, 4, 6)[level]
    block = lax.rem(position, group // 2) * PANELS + panel_at
    parent = position * PANELS + panel_at
    map_row[0:1, :] = maps[pl.ds(map_base + 2 * front_at + side, 1), :]
    map_row[1:2, :] = maps[pl.ds(map_base + 2 * front_at + 1 - side, 1), :]
    diag_row[0:1, :] = diag[pl.ds(diag_base + front_at, 1), :]
    lane = lax.broadcasted_iota(i32, (1, 128), 1)
    height = 16 + r

    def row_choice(half):
        start = block * (2 * r)
        tile = map_row[half:half + 1, pl.ds(pl.multiple_of(start // 128 * 128, 128), 128)]
        shift = lax.rem(128 - lax.rem(start + half * r, 128), 128)
        t = pltpu.roll(jnp.broadcast_to(tile, (8, 128)), shift, 1)[:1, :r]
        slot = jnp.where(t < K, t - parent * k, 16 + t - K - parent * r)
        rows = lax.broadcasted_iota(i32, (height, r), 0)
        return (rows == slot).astype(f32).astype(bf16)

    sel = (row_choice(0), row_choice(1))
    sides = (side, 1 - side)
    spread = lax.broadcasted_iota(i32, (128, 256), 0)
    piv_acc = [None, None]
    out_rows = lax.broadcasted_iota(i32, (height, 128), 0)
    upd_row_id = parent * r + out_rows - 16
    piv_row_id = parent * k + out_rows
    for c in range(16):
        xs, ss = [], []
        for which, ref in enumerate((mine, other)):
            x = ref[:, c * 256:(c + 1) * 256]
            hi, lo = (x, jnp.zeros_like(x)) if x.dtype == bf16 else split(x)
            pick = lambda y: jnp.dot(sel[which], y, preferred_element_type=f32).astype(bf16)
            xs.append(jnp.concatenate([pick(hi), pick(lo)], axis=0))
            m = map_row[which:which + 1, c * 256:(c + 1) * 256]
            onehots = [
                spread == m - (K + s * (U // 2) + c * 128) for s in sides
            ] + [spread == m - (s * (K // 2) + c // 8 * 128) for s in sides]
            ss.append(jnp.concatenate([o.astype(f32).astype(bf16) for o in onehots], axis=0))
        res = lax.dot_general(
            jnp.concatenate(xs, axis=1), jnp.concatenate(ss, axis=1),
            (((1,), (1,)), ((), ())), preferred_element_type=f32,
        )
        res = res[:height] + res[height:]
        upd_col = side * (U // 2) + c * 128 + lane
        d = diag_row[0:1, pl.ds(pl.multiple_of(K + side * (U // 2) + c * 128, 128), 128)]
        own = res[:, :128] + jnp.where(upd_row_id == upd_col, d, 0.0)
        for at, tile in ((side, own), (1 - side, res[:, 128:256])):
            cols = pl.ds(pl.multiple_of(at * (U // 2) + c * 128, 128), 128)
            value = tile[16:]
            if extra is not None:
                value += extra[:, pl.ds(pl.multiple_of(K + at * (U // 2) + c * 128, 128), 128)]
            upd_out[:, cols] = value
        for n in range(2):
            part = res[:, 256 + n * 128:384 + n * 128]
            piv_acc[n] = part if c % 8 == 0 else piv_acc[n] + part
        if c % 8 == 7:
            half = c // 8
            col = side * (K // 2) + half * 128 + lane
            d = diag_row[0:1, pl.ds(pl.multiple_of(side * (K // 2) + half * 128, 128), 128)]
            piv_acc[0] += jnp.where((piv_row_id == col) & (out_rows < 16), d, 0.0)
            for n, at in enumerate((side, 1 - side)):
                cols = pl.ds(pl.multiple_of(at * (K // 2) + half * 128, 128), 128)
                value = piv_acc[n][16:]
                if extra is not None:
                    value += extra[:, cols]
                coupled_out[:, cols] = value
                piv_out[pl.ds(2 * at + half, k, stride=4), :] = piv_acc[n][:k]


def assemble(level, maps, diag, mine, other, extra):
    r = mine.shape[0]
    k = r // 8
    ins = (maps, diag, mine, other) + ((extra,) if level == 2 else ())
    return pl.pallas_call(
        functools.partial(assemble_kernel, level),
        out_shape=(
            jax.ShapeDtypeStruct((4 * k, 128), f32),
            jax.ShapeDtypeStruct((r, K), f32),
            jax.ShapeDtypeStruct((r, U), f32),
        ),
        in_specs=[VMEM] * len(ins),
        out_specs=(VMEM,) * 3,
        scratch_shapes=[pltpu.VMEM((8, U), i32), pltpu.VMEM((8, U + K), f32)],
        compiler_params=pltpu.CompilerParams(vmem_limit_bytes=40 * 2**20),
        cost_estimate=pl.CostEstimate(flops=2 * 10**9, bytes_accessed=4 * 10**6, transcendentals=0),
        name="assemble%d" % level,
    )(*ins)


def level_kernel(level, *refs):
    last = level == 2
    ysize = 1 << level
    takes_plane, takes_column = level < 2, level > 0
    refs = list(refs)
    take = lambda wanted: refs.pop(0) if wanted else None
    piece, coupled, upd, order = take(True), take(True), take(True), take(last)
    plane_in, column_in = take(takes_plane), take(takes_column)
    own_out, second_out = take(True), take(True)
    sums_out, total_out = take(takes_plane), take(level == 1)
    a, w, fi, fj, prod, got, upd_in, send_sem, recv_sem = refs[:9]
    refs = refs[9:]
    plane_land, column_land = take(takes_plane), take(takes_column)
    r = coupled.shape[0]
    half = prod.shape[2]
    n = K
    cube_at = lax.axis_index("cube")
    zh = lax.axis_index("panel")
    place = lax.rem(cube_at, 8)
    core = lax.rem(cube_at, 2)
    x = lax.rem(cube_at // 2, 4)
    zl = lax.rem(cube_at // 8, 2)
    yfull = cube_at // 16
    y = lax.rem(yfull, ysize)
    ybase = yfull - y
    mine = (y * 2 + zl) * PANELS + zh

    def target(y, zl, w, zh):
        return {"cube": (ybase + y) * 16 + zl * 8 + w, "panel": zh}

    def turned(a, b, c):
        return target(lax.rem(y + a, ysize), lax.rem(zl + b, 2), place, lax.rem(zh + c, 4))

    z_peers = [turned(0, b, c) for b in range(2) for c in range(4) if b + c]
    v_peers = z_peers + [turned(d, b, c) for d in range(1, ysize) for b in range(2) for c in range(4)]
    w_places = [lax.rem(place + d, 8) for d in range(1, 8)]
    w_peers = [target(y, zl, q, zh) for q in w_places]
    cross_places, cross_peers = [], []
    if not last:
        bit = 1 << level
        across = yfull + bit - 2 * bit * lax.rem(yfull // bit, 2)
        cross_places = [place] + w_places
        cross_peers = [{"cube": across * 16 + zl * 8 + q, "panel": zh} for q in cross_places]
    plane_places, plane_peers = [], []
    if takes_plane:
        for turn in PLANE_TURNS:
            to_y, q = lax.rem(yfull + turn // 8, 4), lax.rem(place + turn % 8, 8)
            plane_places.append(to_y * 8 + q)
            plane_peers.append({"cube": to_y * 16 + zl * 8 + q, "panel": zh})
    everyone = v_peers + (plane_peers if takes_plane else w_peers)
    barrier = pltpu.get_barrier_semaphore()
    for peer in everyone:
        pl.semaphore_signal(barrier, inc=1, device_id=peer, device_id_type=pl.DeviceIdType.MESH)
    a[pl.ds(y, 1), pl.ds(zl, 1), pl.ds(x, 1), pl.ds(core, 1), pl.ds(zh, 1)] = piece[...][None, None, None, None, None]
    own = coupled[...]
    if last:
        move = (lax.broadcasted_iota(i32, (n, n), 0) == order[...]).astype(f32).astype(bf16)
        ch, cl = split(own)
        own = jnp.dot(ch, move, preferred_element_type=f32) + jnp.dot(cl, move, preferred_element_type=f32)
    own_rows = own.astype(bf16)[None]
    fi[pl.ds(place, 1)] = own_rows
    fj[pl.ds(mine, 1)] = own_rows
    pl.semaphore_wait(barrier, len(everyone))
    copies = []

    def send(src, dst, peer):
        copy = pltpu.make_async_remote_copy(
            src_ref=src, dst_ref=dst, send_sem=send_sem.at[len(copies)], recv_sem=recv_sem.at[len(copies)],
            device_id=peer, device_id_type=pl.DeviceIdType.MESH,
        )
        copy.start()
        copies.append(copy)
        return copy

    early = None
    stages = [
        (z_peers, a.at[y, zl, x, core, zh]),
        ([target(y, zl, lax.rem(x + d, 4) * 2 + core, zh) for d in range(1, 4)], a.at[y, :, x, core]),
        ([turned(d, 0, 0) for d in range(1, ysize)], a.at[y, :, :, core]),
        ([target(y, zl, x * 2 + 1 - core, zh)], a.at[:, :, :, core]),
    ]
    gathered = []
    for number, (peers, part) in enumerate(stages):
        started = [send(part, part, peer) for peer in peers]
        if number == 0 and not last:
            early = send(upd.at[half:], upd_in, cross_peers[0])
        if number == 1:
            gathered += [send(fj.at[mine], fj.at[mine], peer) for peer in v_peers]
        if number == 2:
            gathered += [send(fi.at[place], fi.at[place], peer) for peer in w_peers]
        for copy in started:
            copy.wait_recv()

    coupling = []
    if takes_column:
        spot = zl * PANELS + zh
        turns = [(b, c) for b in range(2) for c in range(4) if b + c]
        for (b, c), peer in zip(turns, z_peers):
            to_z = lax.rem(zl + b, 2) * PANELS + lax.rem(zh + c, 4)
            coupling.append(send(column_in.at[to_z], column_land.at[spot], peer))
        column_land[pl.ds(spot, 1)] = column_in[pl.ds(spot, 1)]
    if takes_plane:
        spot = yfull * 8 + place
        for q, peer in zip(plane_places, plane_peers):
            coupling.append(send(plane_in.at[q], plane_land.at[spot], peer))
        plane_land[pl.ds(spot, 1)] = plane_in[pl.ds(spot, 1)]
    flat = a.reshape(4 * n, 128)
    if last:
        full = jnp.concatenate([flat[pl.ds(c, n, stride=4), :] for c in range(4)], axis=1)
        for part, source in enumerate(split(full)):
            cols = jnp.dot(source, move, preferred_element_type=f32).astype(bf16)
            both = lax.dot_general(move, cols, (((0,), (0,)), ((), ())), preferred_element_type=f32)
            if part == 0:
                w[:, :n] = both
            else:
                w[:, :n] += both
        w[:, n:] = jnp.concatenate([own, jnp.zeros((128 - r, n), f32)], axis=0).T
    else:
        for c in range(4):
            w[:, c * 128:(c + 1) * 128] = flat[pl.ds(c, n, stride=4), :]
    blocks = n // 128
    width = w.shape[1]
    first, second = ((0,), (0,)), ((1,), (0,))
    for b in range(blocks):
        lo, hi = b * 128, b * 128 + 128
        rows = [w[lo + 8 * p: lo + 8 * p + 8, lo:hi] for p in range(16)]
        inverse = jnp.concatenate(diag_inverse(rows), axis=0)
        if hi < width:
            solved = mm(inverse, w[lo:hi, hi:], second)
        for later in range(b + 1, blocks):
            off = (later - b - 1) * 128
            w[later * 128:later * 128 + 128, later * 128:] -= mm(solved[:, off:off + 128], solved[:, off:], first)
        if last:
            second_out[:, lo:hi] = solved[:, n - hi:].T[:r].astype(bf16)
        done = inverse
        if b:
            done = jnp.concatenate([mm(inverse, w[lo:hi, :lo], second), inverse], axis=1)
            w[lo:hi, :lo] = done[:, :lo]
        w[lo:hi, lo:hi] = inverse
        for later in range(b + 1, blocks):
            off = (later - b - 1) * 128
            part = mm(solved[:, off:off + 128], done, first)
            if b:
                w[later * 128:later * 128 + 128, :lo] -= part[:, :lo]
            w[later * 128:later * 128 + 128, lo:hi] = -part[:, lo:]

    for copy in gathered:
        copy.wait_recv()
    both = jnp.concatenate([fi[...].reshape(8 * r, n), fj[...].reshape(512, n)], axis=0)
    across_rows = ((1,), (1,))
    factors = []
    for b in range(blocks):
        hi = b * 128 + 128
        parts = [
            lax.dot_general(both[:, :hi], part, (across_rows, ((), ())), preferred_element_type=f32)
            for part in split(w[hi - 128:hi, :hi])
        ]
        factors.append((parts[0] + parts[1]).astype(bf16))
    factors = jnp.concatenate(factors, axis=1)
    product = lax.dot_general(
        factors[:8 * r], factors[8 * r:], (across_rows, ((), ())), preferred_element_type=f32
    ).astype(bf16).reshape(8, r, 512)
    for part in range(r // half):
        prod[part] = product[:, part * half:(part + 1) * half]
    back = [send(prod.at[0, q], got.at[0, place], peer) for q, peer in zip(w_places, w_peers)]
    back += [send(prod.at[1, q], got.at[1, place], peer) for q, peer in zip(cross_places, cross_peers)]
    got[0, pl.ds(place, 1)] = prod[0, pl.ds(place, 1)]
    if early is not None:
        early.wait_recv()
    for copy in back:
        copy.wait_recv()
    wide = PANELS * r
    for part in range(r // half):
        source = upd_in if part else upd
        out = second_out if part else own_out
        for block in range(2 * ysize):
            parts = [got[part, q, :, block * wide:(block + 1) * wide].astype(f32) for q in range(8)]
            lo = block * 8 * wide
            out[:, lo:lo + 8 * wide] = source[:half, lo:lo + 8 * wide] - jnp.concatenate(parts, axis=1)
    for copy in coupling:
        copy.wait_recv()
    if takes_plane:
        marks = plane_land[:, :, PART:].reshape(512, 128)
        for c in range(0, PART, 768):
            rows = plane_land[:, :, c:c + 768].reshape(512, 768)
            sums = lax.dot_general(marks, rows, (((0,), (0,)), ((), ())), preferred_element_type=f32)
            sums_out[:, :, c:c + 768] = sums.astype(bf16).reshape(8, 16, 768)
    if takes_column:
        total = column_land[0].astype(f32)
        for q in range(1, 8):
            total = total + column_land[q].astype(f32)
        if last:
            own_out[:, PART - K:] += total
        else:
            total_out[:, :PART] = total
            total_out[:, PART:] = jnp.zeros((16, U + K - PART), f32)
    for copy in copies:
        copy.wait_send()


def eliminate(level, piece, coupled, update_rows, *extra):
    last = level == 2
    ysize = 1 << level
    r = coupled.shape[0]
    half = r if last else r // 2
    ins = (piece, coupled, update_rows) + extra
    second = jax.ShapeDtypeStruct((r, K), bf16) if last else jax.ShapeDtypeStruct((half, U), f32)
    v = 8 * ysize
    count = 7 + 3 + ysize - 1 + 1 + (v - 1 + 7) + 7 + (31 + 9, 31 + 7 + 9, 7)[level]
    outs = (jax.ShapeDtypeStruct((half, U), f32), second)
    sums = jax.ShapeDtypeStruct((8, 16, PART), bf16)
    lands = []
    if level < 2:
        outs += (sums,)
        lands.append(pltpu.VMEM((32, 16, PART + 128), bf16))
    if level > 0:
        lands.append(pltpu.VMEM(sums.shape, bf16))
    if level == 1:
        outs += (jax.ShapeDtypeStruct((16, U + K), f32),)
    return pl.pallas_call(
        functools.partial(level_kernel, level),
        out_shape=outs,
        in_specs=[VMEM] * len(ins),
        out_specs=(VMEM,) * len(outs),
        scratch_shapes=[
            pltpu.VMEM((ysize, 2, 4, 2, 4) + piece.shape, f32),
            pltpu.VMEM((K, K + (128 if last else 0)), f32),
            pltpu.VMEM((8, r, K), bf16),
            pltpu.VMEM((v, r, K), bf16),
            pltpu.VMEM((r // half, 8, half, 512), bf16),
            pltpu.VMEM((r // half, 8, half, 512), bf16),
            pltpu.VMEM((half, U), f32),
            pltpu.SemaphoreType.DMA((count,)), pltpu.SemaphoreType.DMA((count,)),
        ] + lands,
        compiler_params=pltpu.CompilerParams(
            collective_id=level, has_side_effects=True, vmem_limit_bytes=48 * 2**20
        ),
        cost_estimate=pl.CostEstimate(flops=3 * 10**10, bytes_accessed=150 * 10**6, transcendentals=0),
        name="level%d" % level,
    )(*ins)


def from_partner(shard, stride):
    return lax.ppermute(shard, "cube", [(i, i ^ 1 << stride) for i in range(64)])


def plane_of(owner):
    cube, zh = owner // PANELS, lax.rem(owner, PANELS)
    cls = cube // 16 * 8 + lax.rem(cube, 8)
    return cls, lax.rem(cube // 8, 2) * PANELS + zh


def route_plane(coupling_rows, coupling_owner, coupling_slot):
    cls, z = plane_of(coupling_owner[:, 0])
    m = coupling_rows.shape[0]
    hits = (cls[:, None] == jnp.arange(32, dtype=i32)[None, :]).astype(bf16)
    before = (jnp.arange(m)[:, None] > jnp.arange(m)[None, :]).astype(bf16)
    earlier = jnp.dot(before, hits, preferred_element_type=f32)
    earlier = jnp.sum(earlier * hits.astype(f32), axis=1).astype(i32)
    target = cls * 16 + earlier
    choose = (target[None, :] == jnp.arange(512, dtype=i32)[:, None]).astype(bf16)
    marks = (z * 16 + coupling_slot)[:, None] == jnp.arange(128, dtype=i32)[None, :]
    outgoing = []
    for part in (coupling_rows[:, :PART], coupling_rows[:, PART:]):
        payload = jnp.concatenate([part, marks.astype(bf16)], axis=1)
        chosen = jnp.dot(choose, payload, preferred_element_type=f32).astype(bf16)
        outgoing.append(chosen.reshape(32, 16, PART + 128))
    return outgoing


def body(leaf_updates, extend_maps, front_diagonal, pivot_order, coupling_rows, coupling_owner, coupling_slot):
    r = leaf_updates.shape[0] // 2
    own, incoming = leaf_updates[:r], from_partner(leaf_updates[r:].astype(bf16), 3)
    early_part, late_part = route_plane(coupling_rows, coupling_owner, coupling_slot)
    total = None
    for level in range(3):
        piece, coupled, update_rows = assemble(
            level, extend_maps, front_diagonal, own, incoming, total
        )
        extra = ((early_part,), (late_part, early_part), (pivot_order.reshape(1, K), late_part))[level]
        results = eliminate(level, piece, coupled, update_rows, *extra)
        own, incoming = results[:2]
        if level == 0:
            early_part = results[2]
        elif level == 1:
            late_part, total = results[2:]
    return (incoming, own)


def solution(mesh):
    return jax.shard_map(
        body,
        mesh=mesh,
        in_specs=(
            P(("cube", "panel"), None), P(), P(), P(),
            P(("cube", "panel"), None), P(("cube", "panel"), None), P(("cube", "panel")),
        ),
        out_specs=(P(("cube", "panel"), None), P(("cube", "panel"), None)),
        check_vma=False,
    )
```

```python
import functools
import jax
import jax.numpy as jnp
from jax import lax
from jax.experimental import pallas as pl
from jax.experimental.pallas import tpu as pltpu
from jax.sharding import PartitionSpec as P

CAP = 2
K = 512
U = 4096
PANELS = 4
f32, bf16, i32 = jnp.float32, jnp.bfloat16, jnp.int32
VMEM = pl.BlockSpec(memory_space=pltpu.VMEM)


def split(x):
    hi = x.astype(bf16)
    return hi, (x - hi.astype(f32)).astype(bf16)

def mm(x, y, dims):
    xh, xl = split(x); yh, yl = split(y)
    d = functools.partial(lax.dot_general, dimension_numbers=(dims, ((), ())), preferred_element_type=f32)
    return d(xh, yh) + (d(xh, yl) + d(xl, yh))

def diag_inverse(V, ahead=2):
    V = list(V)
    lane = lax.broadcasted_iota(jnp.int32, (8, 128), 1)
    sub = lax.broadcasted_iota(jnp.int32, (8, 128), 0)
    below = [sub > i for i in range(8)]
    scale = []
    for g in range(8):
        p0, j0 = 2 * g, 16 * g
        win = [q for q in range(p0, min(p0 + 2 + ahead, 16))]
        B = {(k, q): jnp.broadcast_to(V[q][:, j0+k:j0+k+1], (8, 128)) for k in range(16) for q in win}
        dinv = [None, None]
        for i in range(16):
            s, ii = divmod(i, 8)
            ps = p0 + s
            j = j0 + i
            inv = 1.0 / jnp.broadcast_to(B[i, ps][ii:ii+1, :], (8, 128))
            dinv[s] = inv if ii == 0 else jnp.where(below[ii-1], inv, dinv[s])
            at = lane == j
            row = jnp.where(at, 1.0, jnp.broadcast_to(V[ps][ii:ii+1, :], (8, 128)))
            splats = {k: jnp.broadcast_to(B[k, ps][ii:ii+1, :], (8, 128)) for k in range(i+1, 16)}
            for q in win:
                if q < ps or (q == ps and ii == 7): continue
                m = B[i, q] * inv
                if q == ps:
                    m = jnp.where(below[ii], m, 0.0)
                    z = jnp.where(at & below[ii], 0.0, V[q])
                else:
                    z = jnp.where(at, 0.0, V[q])
                V[q] = z - m * row
                for k in range(i+1, 16):
                    B[k, q] = B[k, q] - m * splats[k]
        scale += dinv
        rest = range(p0 + 2 + ahead, 16)
        if len(rest):
            G, Q = [], []
            for s in range(2):
                r = sub + (j0 + 8 * s)
                v = V[p0 + s]
                Q.append(v * dinv[s])
                inwin = (lane >= j0) & (lane < j0 + 16)
                G.append(jnp.where(inwin, jnp.where(lane < r, v, jnp.where(lane == r, 1.0, 0.0)), v))
            Gc, Qc = jnp.concatenate(G, 0), jnp.concatenate(Q, 0)
            gh, gl = split(Gc); qh, ql = split(Qc)
            upd = lax.dot_general(jnp.concatenate([qh, qh, ql], 0), jnp.concatenate([gh, gl, gh], 0),
                                  (((0,), (0,)), ((), ())), preferred_element_type=f32)
            zw = (lane >= j0) & (lane < j0 + 16)
            for q in rest:
                V[q] = jnp.where(zw, 0.0, V[q]) - upd[8*q:8*q+8]
    out = []
    for p in range(16):
        r = sub + 8 * p
        s = jnp.sqrt(scale[p])
        out.append(jnp.where(lane < r, V[p] * s, jnp.where(lane == r, s, 0.0)))
    return out


PART = 2304
PLANE_TURNS = (
    2, 8, 6, 24, 10, 30, 14, 26, 4, 16, 12, 18, 28, 22, 20, 1, 3, 9, 7, 25, 11, 31, 15, 27, 5, 17, 13, 19, 29, 23, 21,
)


def place(level):
    group = 16 << level
    cube_at = lax.axis_index("cube")
    position = lax.rem(cube_at, group)
    return group, position, cube_at // group, position // (group // 2)


def assemble_kernel(level, *refs):
    maps, diag, mine, other = refs[:4]
    extra = refs[4] if level == 2 else None
    piv_out, coupled_out, upd_out, map_row, diag_row = refs[-5:]
    group, position, front_at, side = place(level)
    panel_at = lax.axis_index("panel")
    r = U // (group * PANELS)
    k = K // (group * PANELS)
    map_base = (0, 8, 12)[level]
    diag_base = (0, 4, 6)[level]
    block = lax.rem(position, group // 2) * PANELS + panel_at
    parent = position * PANELS + panel_at
    map_row[0:1, :] = maps[pl.ds(map_base + 2 * front_at + side, 1), :]
    map_row[1:2, :] = maps[pl.ds(map_base + 2 * front_at + 1 - side, 1), :]
    diag_row[0:1, :] = diag[pl.ds(diag_base + front_at, 1), :]
    lane = lax.broadcasted_iota(i32, (1, 128), 1)
    height = 16 + r

    def row_choice(half):
        start = block * (2 * r)
        tile = map_row[half:half + 1, pl.ds(pl.multiple_of(start // 128 * 128, 128), 128)]
        at = lax.rem(start + half * r, 128) // r
        t = tile[:, :r]
        for case in range(1, 128 // r):
            t = jnp.where(at == case, tile[:, case * r:(case + 1) * r], t)
        slot = jnp.where(t < K, t - parent * k, 16 + t - K - parent * r)
        rows = lax.broadcasted_iota(i32, (height, r), 0)
        return (rows == slot).astype(f32).astype(bf16)

    sel = (row_choice(0), row_choice(1))
    sides = (side, 1 - side)
    spread = lax.broadcasted_iota(i32, (128, 256), 0)
    piv_acc = [None, None]
    out_rows = lax.broadcasted_iota(i32, (height, 128), 0)
    upd_row_id = parent * r + out_rows - 16
    piv_row_id = parent * k + out_rows
    for c in range(16):
        xs, ss = [], []
        for which, ref in enumerate((mine, other)):
            x = ref[:, c * 256:(c + 1) * 256]
            hi, lo = (x, jnp.zeros_like(x)) if x.dtype == bf16 else split(x)
            pick = lambda y: jnp.dot(sel[which], y, preferred_element_type=f32).astype(bf16)
            xs.append(jnp.concatenate([pick(hi), pick(lo)], axis=0))
            m = map_row[which:which + 1, c * 256:(c + 1) * 256]
            onehots = [
                spread == m - (K + s * (U // 2) + c * 128) for s in sides
            ] + [spread == m - (s * (K // 2) + c // 8 * 128) for s in sides]
            ss.append(jnp.concatenate([o.astype(f32).astype(bf16) for o in onehots], axis=0))
        res = lax.dot_general(
            jnp.concatenate(xs, axis=1), jnp.concatenate(ss, axis=1),
            (((1,), (1,)), ((), ())), preferred_element_type=f32,
        )
        res = res[:height] + res[height:]
        upd_col = side * (U // 2) + c * 128 + lane
        d = diag_row[0:1, pl.ds(pl.multiple_of(K + side * (U // 2) + c * 128, 128), 128)]
        own = res[:, :128] + jnp.where(upd_row_id == upd_col, d, 0.0)
        for at, tile in ((side, own), (1 - side, res[:, 128:256])):
            cols = pl.ds(pl.multiple_of(at * (U // 2) + c * 128, 128), 128)
            value = tile[16:]
            if extra is not None:
                value += extra[:, pl.ds(pl.multiple_of(K + at * (U // 2) + c * 128, 128), 128)]
            upd_out[:, cols] = value
        for n in range(2):
            part = res[:, 256 + n * 128:384 + n * 128]
            piv_acc[n] = part if c % 8 == 0 else piv_acc[n] + part
        if c % 8 == 7:
            half = c // 8
            col = side * (K // 2) + half * 128 + lane
            d = diag_row[0:1, pl.ds(pl.multiple_of(side * (K // 2) + half * 128, 128), 128)]
            piv_acc[0] += jnp.where((piv_row_id == col) & (out_rows < 16), d, 0.0)
            for n, at in enumerate((side, 1 - side)):
                cols = pl.ds(pl.multiple_of(at * (K // 2) + half * 128, 128), 128)
                value = piv_acc[n][16:]
                if extra is not None:
                    value += extra[:, cols]
                coupled_out[:, cols] = value
                piv_out[pl.ds(2 * at + half, k, stride=4), :] = piv_acc[n][:k]


def level_kernel(level, *refs):
    last = level == 2
    ysize = 1 << level
    takes_plane, takes_column = level < 2, level > 0
    refs = list(refs)
    take = lambda wanted: refs.pop(0) if wanted else None
    parts_in = [take(True) for _ in range(4 + last)]
    order = take(last)
    plane_in, column_in = take(takes_plane), take(takes_column)
    own_out, second_out = take(True), take(True)
    sums_out, total_out = take(takes_plane), take(level == 1)
    a, w, fi, fj, prod, got, upd_in, send_sem, recv_sem = refs[:9]
    refs = refs[9:]
    piece, coupled, upd, map_row, diag_row = refs[:5]
    refs = refs[5:]
    plane_land, column_land = take(takes_plane), take(takes_column)
    r = coupled.shape[0]
    half = prod.shape[2]
    n = K
    cube_at = lax.axis_index("cube")
    zh = lax.axis_index("panel")
    place = lax.rem(cube_at, 8)
    core = lax.rem(cube_at, 2)
    x = lax.rem(cube_at // 2, 4)
    zl = lax.rem(cube_at // 8, 2)
    yfull = cube_at // 16
    y = lax.rem(yfull, ysize)
    ybase = yfull - y
    mine = (y * 2 + zl) * PANELS + zh

    def target(y, zl, w, zh):
        return {"cube": (ybase + y) * 16 + zl * 8 + w, "panel": zh}

    def turned(a, b, c):
        return target(lax.rem(y + a, ysize), lax.rem(zl + b, 2), place, lax.rem(zh + c, 4))

    z_peers = [turned(0, b, c) for b in range(2) for c in range(4) if b + c]
    v_peers = z_peers + [turned(d, b, c) for d in range(1, ysize) for b in range(2) for c in range(4)]
    w_places = [lax.rem(place + d, 8) for d in range(1, 8)]
    w_peers = [target(y, zl, q, zh) for q in w_places]
    cross_places, cross_peers = [], []
    if not last:
        bit = 1 << level
        across = yfull + bit - 2 * bit * lax.rem(yfull // bit, 2)
        cross_places = [place] + w_places
        cross_peers = [{"cube": across * 16 + zl * 8 + q, "panel": zh} for q in cross_places]
    plane_places, plane_peers = [], []
    if takes_plane:
        for turn in PLANE_TURNS:
            to_y, q = lax.rem(yfull + turn // 8, 4), lax.rem(place + turn % 8, 8)
            plane_places.append(to_y * 8 + q)
            plane_peers.append({"cube": to_y * 16 + zl * 8 + q, "panel": zh})
    everyone = v_peers + (plane_peers if takes_plane else w_peers)
    barrier = pltpu.get_barrier_semaphore()
    for peer in everyone:
        pl.semaphore_signal(barrier, inc=1, device_id=peer, device_id_type=pl.DeviceIdType.MESH)
    assemble_kernel(level, *parts_in, piece, coupled, upd, map_row, diag_row)
    a[pl.ds(y, 1), pl.ds(zl, 1), pl.ds(x, 1), pl.ds(core, 1), pl.ds(zh, 1)] = piece[...][None, None, None, None, None]
    own = coupled[...]
    if last:
        move = (lax.broadcasted_iota(i32, (n, n), 0) == order[...]).astype(f32).astype(bf16)
        ch, cl = split(own)
        own = jnp.dot(ch, move, preferred_element_type=f32) + jnp.dot(cl, move, preferred_element_type=f32)
    own_rows = own.astype(bf16)[None]
    fi[pl.ds(place, 1)] = own_rows
    fj[pl.ds(mine, 1)] = own_rows
    pl.semaphore_wait(barrier, len(everyone))
    copies = []

    def send(src, dst, peer):
        copy = pltpu.make_async_remote_copy(
            src_ref=src, dst_ref=dst, send_sem=send_sem.at[len(copies)], recv_sem=recv_sem.at[len(copies)],
            device_id=peer, device_id_type=pl.DeviceIdType.MESH,
        )
        copy.start()
        copies.append(copy)
        return copy

    early = None
    stages = [
        (z_peers, a.at[y, zl, x, core, zh]),
        ([target(y, zl, lax.rem(x + d, 4) * 2 + core, zh) for d in range(1, 4)], a.at[y, :, x, core]),
        ([turned(d, 0, 0) for d in range(1, ysize)], a.at[y, :, :, core]),
        ([target(y, zl, x * 2 + 1 - core, zh)], a.at[:, :, :, core]),
    ]
    gathered, coupling = [], []
    for number, (peers, part) in enumerate(stages):
        started = [send(part, part, peer) for peer in peers]
        if number == 0 and not last:
            early = send(upd.at[half:], upd_in, cross_peers[0])
        if number == 1:
            gathered += [send(fj.at[mine], fj.at[mine], peer) for peer in v_peers]
        if number == 2:
            gathered += [send(fi.at[place], fi.at[place], peer) for peer in w_peers]
        if number == 3:
            if takes_column:
                spot = zl * PANELS + zh
                turns = [(b, c) for b in range(2) for c in range(4) if b + c]
                for (b, c), peer in zip(turns, z_peers):
                    to_z = lax.rem(zl + b, 2) * PANELS + lax.rem(zh + c, 4)
                    coupling.append(send(column_in.at[to_z], column_land.at[spot], peer))
                column_land[pl.ds(spot, 1)] = column_in[pl.ds(spot, 1)]
            if takes_plane:
                spot = yfull * 8 + place
                for q, peer in zip(plane_places, plane_peers):
                    coupling.append(send(plane_in.at[q], plane_land.at[spot], peer))
                plane_land[pl.ds(spot, 1)] = plane_in[pl.ds(spot, 1)]
        for copy in started:
            copy.wait_recv()

    flat = a.reshape(4 * n, 128)
    if last:
        full = jnp.concatenate([flat[pl.ds(c, n, stride=4), :] for c in range(4)], axis=1)
        for part, source in enumerate(split(full)):
            cols = jnp.dot(source, move, preferred_element_type=f32).astype(bf16)
            both = lax.dot_general(move, cols, (((0,), (0,)), ((), ())), preferred_element_type=f32)
            if part == 0:
                w[:, :n] = both
            else:
                w[:, :n] += both
        w[:, n:] = jnp.concatenate([own, jnp.zeros((128 - r, n), f32)], axis=0).T
    else:
        for c in range(4):
            w[:, c * 128:(c + 1) * 128] = flat[pl.ds(c, n, stride=4), :]
    blocks = n // 128
    width = w.shape[1]
    first, second = ((0,), (0,)), ((1,), (0,))
    for b in range(blocks):
        lo, hi = b * 128, b * 128 + 128
        rows = [w[lo + 8 * p: lo + 8 * p + 8, lo:hi] for p in range(16)]
        inverse = jnp.concatenate(diag_inverse(rows), axis=0)
        if hi < width:
            solved = mm(inverse, w[lo:hi, hi:], second)
        for later in range(b + 1, blocks):
            off = (later - b - 1) * 128
            w[later * 128:later * 128 + 128, later * 128:] -= mm(solved[:, off:off + 128], solved[:, off:], first)
        if last:
            second_out[:, lo:hi] = solved[:, n - hi:].T[:r].astype(bf16)
        done = inverse
        if b:
            done = jnp.concatenate([mm(inverse, w[lo:hi, :lo], second), inverse], axis=1)
            w[lo:hi, :lo] = done[:, :lo]
        w[lo:hi, lo:hi] = inverse
        for later in range(b + 1, blocks):
            off = (later - b - 1) * 128
            part = mm(solved[:, off:off + 128], done, first)
            if b:
                w[later * 128:later * 128 + 128, :lo] -= part[:, :lo]
            w[later * 128:later * 128 + 128, lo:hi] = -part[:, lo:]

    for copy in gathered:
        copy.wait_recv()
    both = jnp.concatenate([fi[...].reshape(8 * r, n), fj[...].reshape(512, n)], axis=0)
    across_rows = ((1,), (1,))
    factors = []
    for b in range(blocks):
        hi = b * 128 + 128
        parts = [
            lax.dot_general(both[:, :hi], part, (across_rows, ((), ())), preferred_element_type=f32)
            for part in split(w[hi - 128:hi, :hi])
        ]
        factors.append((parts[0] + parts[1]).astype(bf16))
    factors = jnp.concatenate(factors, axis=1)
    product = lax.dot_general(
        factors[:8 * r], factors[8 * r:], (across_rows, ((), ())), preferred_element_type=f32
    ).astype(bf16).reshape(8, r, 512)
    for part in range(r // half):
        prod[part] = product[:, part * half:(part + 1) * half]
    back = [send(prod.at[0, q], got.at[0, place], peer) for q, peer in zip(w_places, w_peers)]
    back += [send(prod.at[1, q], got.at[1, place], peer) for q, peer in zip(cross_places, cross_peers)]
    got[0, pl.ds(place, 1)] = prod[0, pl.ds(place, 1)]
    if early is not None:
        early.wait_recv()
    for copy in back:
        copy.wait_recv()
    wide = PANELS * r
    for part in range(r // half):
        source = upd_in if part else upd
        out = second_out if part else own_out
        for block in range(2 * ysize):
            parts = [got[part, q, :, block * wide:(block + 1) * wide].astype(f32) for q in range(8)]
            lo = block * 8 * wide
            out[:, lo:lo + 8 * wide] = source[:half, lo:lo + 8 * wide] - jnp.concatenate(parts, axis=1)
    for copy in coupling:
        copy.wait_recv()
    if takes_plane:
        marks = plane_land[:, :, PART:].reshape(512, 128)
        for c in range(0, PART, 768):
            rows = plane_land[:, :, c:c + 768].reshape(512, 768)
            sums = lax.dot_general(marks, rows, (((0,), (0,)), ((), ())), preferred_element_type=f32)
            sums_out[:, :, c:c + 768] = sums.astype(bf16).reshape(8, 16, 768)
    if takes_column:
        total = column_land[0].astype(f32)
        for q in range(1, 8):
            total = total + column_land[q].astype(f32)
        if last:
            own_out[:, PART - K:] += total
        else:
            total_out[:, :PART] = total
            total_out[:, PART:] = jnp.zeros((16, U + K - PART), f32)
    for copy in copies:
        copy.wait_send()


def eliminate(level, maps, diag, own, incoming, *extra):
    last = level == 2
    ysize = 1 << level
    r = own.shape[0]
    half = r if last else r // 2
    ins = (maps, diag, own, incoming) + extra
    second = jax.ShapeDtypeStruct((r, K), bf16) if last else jax.ShapeDtypeStruct((half, U), f32)
    v = 8 * ysize
    count = 7 + 3 + ysize - 1 + 1 + (v - 1 + 7) + 7 + (31 + 9, 31 + 7 + 9, 7)[level]
    outs = (jax.ShapeDtypeStruct((half, U), f32), second)
    sums = jax.ShapeDtypeStruct((8, 16, PART), bf16)
    lands = []
    if level < 2:
        outs += (sums,)
        lands.append(pltpu.VMEM((32, 16, PART + 128), bf16))
    if level > 0:
        lands.append(pltpu.VMEM(sums.shape, bf16))
    if level == 1:
        outs += (jax.ShapeDtypeStruct((16, U + K), f32),)
    return pl.pallas_call(
        functools.partial(level_kernel, level),
        out_shape=outs,
        in_specs=[VMEM] * len(ins),
        out_specs=(VMEM,) * len(outs),
        scratch_shapes=[
            pltpu.VMEM((ysize, 2, 4, 2, 4, r // 2, 128), f32),
            pltpu.VMEM((K, K + (128 if last else 0)), f32),
            pltpu.VMEM((8, r, K), bf16),
            pltpu.VMEM((v, r, K), bf16),
            pltpu.VMEM((r // half, 8, half, 512), bf16),
            pltpu.VMEM((r // half, 8, half, 512), bf16),
            pltpu.VMEM((half, U), f32),
            pltpu.SemaphoreType.DMA((count,)), pltpu.SemaphoreType.DMA((count,)),
            pltpu.VMEM((r // 2, 128), f32), pltpu.VMEM((r, K), f32), pltpu.VMEM((r, U), f32),
            pltpu.VMEM((8, U), i32), pltpu.VMEM((8, U + K), f32),
        ] + lands,
        compiler_params=pltpu.CompilerParams(
            collective_id=level, has_side_effects=True, vmem_limit_bytes=48 * 2**20
        ),
        cost_estimate=pl.CostEstimate(flops=3 * 10**10, bytes_accessed=150 * 10**6, transcendentals=0),
        name="level%d" % level,
    )(*ins)


def from_partner(shard, stride):
    return lax.ppermute(shard, "cube", [(i, i ^ 1 << stride) for i in range(64)])


def plane_of(owner):
    cube, zh = owner // PANELS, lax.rem(owner, PANELS)
    cls = cube // 16 * 8 + lax.rem(cube, 8)
    return cls, lax.rem(cube // 8, 2) * PANELS + zh


def route_plane(coupling_rows, coupling_owner, coupling_slot):
    cls, z = plane_of(coupling_owner[:, 0])
    m = coupling_rows.shape[0]
    hits = (cls[:, None] == jnp.arange(32, dtype=i32)[None, :]).astype(bf16)
    before = (jnp.arange(m)[:, None] > jnp.arange(m)[None, :]).astype(bf16)
    earlier = jnp.dot(before, hits, preferred_element_type=f32)
    earlier = jnp.sum(earlier * hits.astype(f32), axis=1).astype(i32)
    target = cls * 16 + earlier
    choose = (target[None, :] == jnp.arange(512, dtype=i32)[:, None]).astype(bf16)
    marks = (z * 16 + coupling_slot)[:, None] == jnp.arange(128, dtype=i32)[None, :]
    outgoing = []
    for part in (coupling_rows[:, :PART], coupling_rows[:, PART:]):
        payload = jnp.concatenate([part, marks.astype(bf16)], axis=1)
        chosen = jnp.dot(choose, payload, preferred_element_type=f32).astype(bf16)
        outgoing.append(chosen.reshape(32, 16, PART + 128))
    return outgoing


def body(leaf_updates, extend_maps, front_diagonal, pivot_order, coupling_rows, coupling_owner, coupling_slot):
    r = leaf_updates.shape[0] // 2
    own, incoming = leaf_updates[:r], from_partner(leaf_updates[r:].astype(bf16), 3)
    early_part, late_part = route_plane(coupling_rows, coupling_owner, coupling_slot)
    total = None
    for level in range(3):
        extra = ((early_part,), (late_part, early_part), (total, pivot_order.reshape(1, K), late_part))[level]
        results = eliminate(level, extend_maps, front_diagonal, own, incoming, *extra)
        own, incoming = results[:2]
        if level == 0:
            early_part = results[2]
        elif level == 1:
            late_part, total = results[2:]
    return (incoming, own)


def solution(mesh):
    return jax.shard_map(
        body,
        mesh=mesh,
        in_specs=(
            P(("cube", "panel"), None), P(), P(), P(),
            P(("cube", "panel"), None), P(("cube", "panel"), None), P(("cube", "panel")),
        ),
        out_specs=(P(("cube", "panel"), None), P(("cube", "panel"), None)),
        check_vma=False,
    )
```

```python
import functools
import jax
import jax.numpy as jnp
from jax import lax
from jax.experimental import pallas as pl
from jax.experimental.pallas import tpu as pltpu
from jax.sharding import PartitionSpec as P

CAP = 2
K = 512
U = 4096
PANELS = 4
f32, bf16, i32 = jnp.float32, jnp.bfloat16, jnp.int32
VMEM = pl.BlockSpec(memory_space=pltpu.VMEM)


def split(x):
    hi = x.astype(bf16)
    return hi, (x - hi.astype(f32)).astype(bf16)

def mm(x, y, dims):
    xh, xl = split(x); yh, yl = split(y)
    d = functools.partial(lax.dot_general, dimension_numbers=(dims, ((), ())), preferred_element_type=f32)
    return d(xh, yh) + (d(xh, yl) + d(xl, yh))

def diag_inverse(V, ahead=2):
    V = list(V)
    lane = lax.broadcasted_iota(jnp.int32, (8, 128), 1)
    sub = lax.broadcasted_iota(jnp.int32, (8, 128), 0)
    below = [sub > i for i in range(8)]
    scale = []
    for g in range(8):
        p0, j0 = 2 * g, 16 * g
        win = [q for q in range(p0, min(p0 + 2 + ahead, 16))]
        B = {(k, q): jnp.broadcast_to(V[q][:, j0+k:j0+k+1], (8, 128)) for k in range(16) for q in win}
        dinv = [None, None]
        for i in range(16):
            s, ii = divmod(i, 8)
            ps = p0 + s
            j = j0 + i
            inv = 1.0 / jnp.broadcast_to(B[i, ps][ii:ii+1, :], (8, 128))
            dinv[s] = inv if ii == 0 else jnp.where(below[ii-1], inv, dinv[s])
            at = lane == j
            row = jnp.where(at, 1.0, jnp.broadcast_to(V[ps][ii:ii+1, :], (8, 128)))
            splats = {k: jnp.broadcast_to(B[k, ps][ii:ii+1, :], (8, 128)) for k in range(i+1, 16)}
            for q in win:
                if q < ps or (q == ps and ii == 7): continue
                m = B[i, q] * inv
                if q == ps:
                    m = jnp.where(below[ii], m, 0.0)
                    z = jnp.where(at & below[ii], 0.0, V[q])
                else:
                    z = jnp.where(at, 0.0, V[q])
                V[q] = z - m * row
                for k in range(i+1, 16):
                    B[k, q] = B[k, q] - m * splats[k]
        scale += dinv
        rest = range(p0 + 2 + ahead, 16)
        if len(rest):
            G, Q = [], []
            for s in range(2):
                r = sub + (j0 + 8 * s)
                v = V[p0 + s]
                Q.append(v * dinv[s])
                inwin = (lane >= j0) & (lane < j0 + 16)
                G.append(jnp.where(inwin, jnp.where(lane < r, v, jnp.where(lane == r, 1.0, 0.0)), v))
            Gc, Qc = jnp.concatenate(G, 0), jnp.concatenate(Q, 0)
            gh, gl = split(Gc); qh, ql = split(Qc)
            upd = lax.dot_general(jnp.concatenate([qh, qh, ql], 0), jnp.concatenate([gh, gl, gh], 0),
                                  (((0,), (0,)), ((), ())), preferred_element_type=f32)
            zw = (lane >= j0) & (lane < j0 + 16)
            for q in rest:
                V[q] = jnp.where(zw, 0.0, V[q]) - upd[8*q:8*q+8]
    out = []
    for p in range(16):
        r = sub + 8 * p
        s = jnp.sqrt(scale[p])
        out.append(jnp.where(lane < r, V[p] * s, jnp.where(lane == r, s, 0.0)))
    return out


PART = 2304
PLANE_TURNS = (
    4, 2, 16, 8, 12, 6, 18, 24, 28, 10, 22, 30, 20, 14, 5, 26, 17, 1, 13, 3, 19, 9, 29, 7, 23, 25, 21, 11, 31, 15, 27,
)


def place(level):
    group = 16 << level
    cube_at = lax.axis_index("cube")
    position = lax.rem(cube_at, group)
    return group, position, cube_at // group, position // (group // 2)


def assemble_kernel(level, *refs):
    maps, diag, mine, other = refs[:4]
    extra = refs[4] if level == 2 else None
    piv_out, coupled_out, upd_out, map_row, diag_row = refs[-5:]
    group, position, front_at, side = place(level)
    panel_at = lax.axis_index("panel")
    r = U // (group * PANELS)
    k = K // (group * PANELS)
    map_base = (0, 8, 12)[level]
    diag_base = (0, 4, 6)[level]
    block = lax.rem(position, group // 2) * PANELS + panel_at
    parent = position * PANELS + panel_at
    map_row[0:1, :] = maps[pl.ds(map_base + 2 * front_at + side, 1), :]
    map_row[1:2, :] = maps[pl.ds(map_base + 2 * front_at + 1 - side, 1), :]
    diag_row[0:1, :] = diag[pl.ds(diag_base + front_at, 1), :]
    lane = lax.broadcasted_iota(i32, (1, 128), 1)
    height = 16 + r

    def row_choice(half):
        start = block * (2 * r)
        tile = map_row[half:half + 1, pl.ds(pl.multiple_of(start // 128 * 128, 128), 128)]
        at = lax.rem(start + half * r, 128) // r
        t = tile[:, :r]
        for case in range(1, 128 // r):
            t = jnp.where(at == case, tile[:, case * r:(case + 1) * r], t)
        slot = jnp.where(t < K, t - parent * k, 16 + t - K - parent * r)
        rows = lax.broadcasted_iota(i32, (height, r), 0)
        return (rows == slot).astype(f32).astype(bf16)

    sel = (row_choice(0), row_choice(1))
    sides = (side, 1 - side)
    spread = lax.broadcasted_iota(i32, (128, 256), 0)
    piv_acc = [None, None]
    out_rows = lax.broadcasted_iota(i32, (height, 128), 0)
    upd_row_id = parent * r + out_rows - 16
    piv_row_id = parent * k + out_rows
    for c in range(16):
        xs, ss = [], []
        for which, ref in enumerate((mine, other)):
            x = ref[:, c * 256:(c + 1) * 256]
            hi, lo = (x, jnp.zeros_like(x)) if x.dtype == bf16 else split(x)
            pick = lambda y: jnp.dot(sel[which], y, preferred_element_type=f32).astype(bf16)
            xs.append(jnp.concatenate([pick(hi), pick(lo)], axis=0))
            m = map_row[which:which + 1, c * 256:(c + 1) * 256]
            onehots = [
                spread == m - (K + s * (U // 2) + c * 128) for s in sides
            ] + [spread == m - (s * (K // 2) + c // 8 * 128) for s in sides]
            ss.append(jnp.concatenate([o.astype(f32).astype(bf16) for o in onehots], axis=0))
        res = lax.dot_general(
            jnp.concatenate(xs, axis=1), jnp.concatenate(ss, axis=1),
            (((1,), (1,)), ((), ())), preferred_element_type=f32,
        )
        res = res[:height] + res[height:]
        upd_col = side * (U // 2) + c * 128 + lane
        d = diag_row[0:1, pl.ds(pl.multiple_of(K + side * (U // 2) + c * 128, 128), 128)]
        own = res[:, :128] + jnp.where(upd_row_id == upd_col, d, 0.0)
        for at, tile in ((side, own), (1 - side, res[:, 128:256])):
            cols = pl.ds(pl.multiple_of(at * (U // 2) + c * 128, 128), 128)
            value = tile[16:]
            if extra is not None:
                value += extra[:, pl.ds(pl.multiple_of(K + at * (U // 2) + c * 128, 128), 128)]
            upd_out[:, cols] = value
        for n in range(2):
            part = res[:, 256 + n * 128:384 + n * 128]
            piv_acc[n] = part if c % 8 == 0 else piv_acc[n] + part
        if c % 8 == 7:
            half = c // 8
            col = side * (K // 2) + half * 128 + lane
            d = diag_row[0:1, pl.ds(pl.multiple_of(side * (K // 2) + half * 128, 128), 128)]
            piv_acc[0] += jnp.where((piv_row_id == col) & (out_rows < 16), d, 0.0)
            for n, at in enumerate((side, 1 - side)):
                cols = pl.ds(pl.multiple_of(at * (K // 2) + half * 128, 128), 128)
                value = piv_acc[n][16:]
                if extra is not None:
                    value += extra[:, cols]
                coupled_out[:, cols] = value
                piv_out[pl.ds(2 * at + half, k, stride=4), :] = piv_acc[n][:k]


def level_kernel(level, *refs):
    last = level == 2
    ysize = 1 << level
    takes_plane, takes_column = level < 2, level > 0
    refs = list(refs)
    take = lambda wanted: refs.pop(0) if wanted else None
    parts_in = [take(True) for _ in range(4 + last)]
    order = take(last)
    plane_in, column_in = take(takes_plane), take(takes_column)
    own_out, second_out = take(True), take(True)
    sums_out, total_out = take(takes_plane), take(level == 1)
    a, w, fi, fj, prod, got, upd_in, send_sem, recv_sem = refs[:9]
    refs = refs[9:]
    piece, coupled, upd, map_row, diag_row = refs[:5]
    refs = refs[5:]
    plane_land, column_land = take(takes_plane), take(takes_column)
    r = coupled.shape[0]
    half = prod.shape[2]
    n = K
    cube_at = lax.axis_index("cube")
    zh = lax.axis_index("panel")
    place = lax.rem(cube_at, 8)
    core = lax.rem(cube_at, 2)
    x = lax.rem(cube_at // 2, 4)
    zl = lax.rem(cube_at // 8, 2)
    yfull = cube_at // 16
    y = lax.rem(yfull, ysize)
    ybase = yfull - y
    mine = (y * 2 + zl) * PANELS + zh

    def target(y, zl, w, zh):
        return {"cube": (ybase + y) * 16 + zl * 8 + w, "panel": zh}

    def turned(a, b, c):
        return target(lax.rem(y + a, ysize), lax.rem(zl + b, 2), place, lax.rem(zh + c, 4))

    z_peers = [turned(0, b, c) for b in range(2) for c in range(4) if b + c]
    v_peers = z_peers + [turned(d, b, c) for d in range(1, ysize) for b in range(2) for c in range(4)]
    w_places = [lax.rem(place + d, 8) for d in range(1, 8)]
    w_peers = [target(y, zl, q, zh) for q in w_places]
    cross_places, cross_peers = [], []
    if not last:
        bit = 1 << level
        across = yfull + bit - 2 * bit * lax.rem(yfull // bit, 2)
        cross_places = [place] + w_places
        cross_peers = [{"cube": across * 16 + zl * 8 + q, "panel": zh} for q in cross_places]
    plane_places, plane_peers = [], []
    if takes_plane:
        for turn in PLANE_TURNS:
            to_y, q = lax.rem(yfull + turn // 8, 4), lax.rem(place + turn % 8, 8)
            plane_places.append(to_y * 8 + q)
            plane_peers.append({"cube": to_y * 16 + zl * 8 + q, "panel": zh})
    everyone = v_peers + (plane_peers if takes_plane else w_peers)
    barrier = pltpu.get_barrier_semaphore()
    for peer in everyone:
        pl.semaphore_signal(barrier, inc=1, device_id=peer, device_id_type=pl.DeviceIdType.MESH)
    assemble_kernel(level, *parts_in, piece, coupled, upd, map_row, diag_row)
    a[pl.ds(y, 1), pl.ds(zl, 1), pl.ds(x, 1), pl.ds(core, 1), pl.ds(zh, 1)] = piece[...][None, None, None, None, None]
    own = coupled[...]
    if last:
        move = (lax.broadcasted_iota(i32, (n, n), 0) == order[...]).astype(f32).astype(bf16)
        ch, cl = split(own)
        own = jnp.dot(ch, move, preferred_element_type=f32) + jnp.dot(cl, move, preferred_element_type=f32)
    own_rows = own.astype(bf16)[None]
    fi[pl.ds(place, 1)] = own_rows
    fj[pl.ds(mine, 1)] = own_rows
    pl.semaphore_wait(barrier, len(everyone))
    copies = []

    def send(src, dst, peer):
        copy = pltpu.make_async_remote_copy(
            src_ref=src, dst_ref=dst, send_sem=send_sem.at[len(copies)], recv_sem=recv_sem.at[len(copies)],
            device_id=peer, device_id_type=pl.DeviceIdType.MESH,
        )
        copy.start()
        copies.append(copy)
        return copy

    early = None
    stages = [
        (z_peers, a.at[y, zl, x, core, zh]),
        ([target(y, zl, lax.rem(x + d, 4) * 2 + core, zh) for d in range(1, 4)], a.at[y, :, x, core]),
        ([turned(d, 0, 0) for d in range(1, ysize)], a.at[y, :, :, core]),
        ([target(y, zl, x * 2 + 1 - core, zh)], a.at[:, :, :, core]),
    ]
    gathered, coupling = [], []
    for number, (peers, part) in enumerate(stages):
        started = [send(part, part, peer) for peer in peers]
        if number == 0 and not last:
            early = send(upd.at[half:], upd_in, cross_peers[0])
        if number == 1:
            gathered += [send(fj.at[mine], fj.at[mine], peer) for peer in v_peers]
        if number == 2:
            gathered += [send(fi.at[place], fi.at[place], peer) for peer in w_peers]
        if number == 3:
            if takes_column:
                spot = zl * PANELS + zh
                turns = [(b, c) for b in range(2) for c in range(4) if b + c]
                for (b, c), peer in zip(turns, z_peers):
                    to_z = lax.rem(zl + b, 2) * PANELS + lax.rem(zh + c, 4)
                    coupling.append(send(column_in.at[to_z], column_land.at[spot], peer))
                column_land[pl.ds(spot, 1)] = column_in[pl.ds(spot, 1)]
            if takes_plane:
                spot = yfull * 8 + place
                for q, peer in zip(plane_places, plane_peers):
                    coupling.append(send(plane_in.at[q], plane_land.at[spot], peer))
                plane_land[pl.ds(spot, 1)] = plane_in[pl.ds(spot, 1)]
        for copy in started:
            copy.wait_recv()

    flat = a.reshape(4 * n, 128)
    if last:
        full = jnp.concatenate([flat[pl.ds(c, n, stride=4), :] for c in range(4)], axis=1)
        for part, source in enumerate(split(full)):
            cols = jnp.dot(source, move, preferred_element_type=f32).astype(bf16)
            both = lax.dot_general(move, cols, (((0,), (0,)), ((), ())), preferred_element_type=f32)
            if part == 0:
                w[:, :n] = both
            else:
                w[:, :n] += both
        w[:, n:] = jnp.concatenate([own, jnp.zeros((128 - r, n), f32)], axis=0).T
    else:
        for c in range(4):
            w[:, c * 128:(c + 1) * 128] = flat[pl.ds(c, n, stride=4), :]
    blocks = n // 128
    width = w.shape[1]
    first, second = ((0,), (0,)), ((1,), (0,))
    for b in range(blocks):
        lo, hi = b * 128, b * 128 + 128
        rows = [w[lo + 8 * p: lo + 8 * p + 8, lo:hi] for p in range(16)]
        inverse = jnp.concatenate(diag_inverse(rows), axis=0)
        if hi < width:
            solved = mm(inverse, w[lo:hi, hi:], second)
        for later in range(b + 1, blocks):
            off = (later - b - 1) * 128
            w[later * 128:later * 128 + 128, later * 128:] -= mm(solved[:, off:off + 128], solved[:, off:], first)
        if last:
            second_out[:, lo:hi] = solved[:, n - hi:].T[:r].astype(bf16)
        done = inverse
        if b:
            done = jnp.concatenate([mm(inverse, w[lo:hi, :lo], second), inverse], axis=1)
            w[lo:hi, :lo] = done[:, :lo]
        w[lo:hi, lo:hi] = inverse
        for later in range(b + 1, blocks):
            off = (later - b - 1) * 128
            part = mm(solved[:, off:off + 128], done, first)
            if b:
                w[later * 128:later * 128 + 128, :lo] -= part[:, :lo]
            w[later * 128:later * 128 + 128, lo:hi] = -part[:, lo:]

    for copy in gathered:
        copy.wait_recv()
    both = jnp.concatenate([fi[...].reshape(8 * r, n), fj[...].reshape(512, n)], axis=0)
    across_rows = ((1,), (1,))
    factors = []
    for b in range(blocks):
        hi = b * 128 + 128
        parts = [
            lax.dot_general(both[:, :hi], part, (across_rows, ((), ())), preferred_element_type=f32)
            for part in split(w[hi - 128:hi, :hi])
        ]
        factors.append((parts[0] + parts[1]).astype(bf16))
    factors = jnp.concatenate(factors, axis=1)
    product = lax.dot_general(
        factors[:8 * r], factors[8 * r:], (across_rows, ((), ())), preferred_element_type=f32
    ).astype(bf16).reshape(8, r, 512)
    for part in range(r // half):
        prod[part] = product[:, part * half:(part + 1) * half]
    back = [send(prod.at[0, q], got.at[0, place], peer) for q, peer in zip(w_places, w_peers)]
    back += [send(prod.at[1, q], got.at[1, place], peer) for q, peer in zip(cross_places, cross_peers)]
    got[0, pl.ds(place, 1)] = prod[0, pl.ds(place, 1)]
    if early is not None:
        early.wait_recv()
    for copy in back:
        copy.wait_recv()
    wide = PANELS * r
    for part in range(r // half):
        source = upd_in if part else upd
        out = second_out if part else own_out
        for block in range(2 * ysize):
            parts = [got[part, q, :, block * wide:(block + 1) * wide].astype(f32) for q in range(8)]
            lo = block * 8 * wide
            out[:, lo:lo + 8 * wide] = source[:half, lo:lo + 8 * wide] - jnp.concatenate(parts, axis=1)
    for copy in coupling:
        copy.wait_recv()
    if takes_plane:
        marks = plane_land[:, :, PART:].reshape(512, 128)
        for c in range(0, PART, 768):
            rows = plane_land[:, :, c:c + 768].reshape(512, 768)
            sums = lax.dot_general(marks, rows, (((0,), (0,)), ((), ())), preferred_element_type=f32)
            sums_out[:, :, c:c + 768] = sums.astype(bf16).reshape(8, 16, 768)
    if takes_column:
        total = column_land[0].astype(f32)
        for q in range(1, 8):
            total = total + column_land[q].astype(f32)
        if last:
            own_out[:, PART - K:] += total
        else:
            total_out[:, :PART] = total
            total_out[:, PART:] = jnp.zeros((16, U + K - PART), f32)
    for copy in copies:
        copy.wait_send()


def eliminate(level, maps, diag, own, incoming, *extra):
    last = level == 2
    ysize = 1 << level
    r = own.shape[0]
    half = r if last else r // 2
    ins = (maps, diag, own, incoming) + extra
    second = jax.ShapeDtypeStruct((r, K), bf16) if last else jax.ShapeDtypeStruct((half, U), f32)
    v = 8 * ysize
    count = 7 + 3 + ysize - 1 + 1 + (v - 1 + 7) + 7 + (31 + 9, 31 + 7 + 9, 7)[level]
    outs = (jax.ShapeDtypeStruct((half, U), f32), second)
    sums = jax.ShapeDtypeStruct((8, 16, PART), bf16)
    lands = []
    if level < 2:
        outs += (sums,)
        lands.append(pltpu.VMEM((32, 16, PART + 128), bf16))
    if level > 0:
        lands.append(pltpu.VMEM(sums.shape, bf16))
    if level == 1:
        outs += (jax.ShapeDtypeStruct((16, U + K), f32),)
    return pl.pallas_call(
        functools.partial(level_kernel, level),
        out_shape=outs,
        in_specs=[VMEM] * len(ins),
        out_specs=(VMEM,) * len(outs),
        scratch_shapes=[
            pltpu.VMEM((ysize, 2, 4, 2, 4, r // 2, 128), f32),
            pltpu.VMEM((K, K + (128 if last else 0)), f32),
            pltpu.VMEM((8, r, K), bf16),
            pltpu.VMEM((v, r, K), bf16),
            pltpu.VMEM((r // half, 8, half, 512), bf16),
            pltpu.VMEM((r // half, 8, half, 512), bf16),
            pltpu.VMEM((half, U), f32),
            pltpu.SemaphoreType.DMA((count,)), pltpu.SemaphoreType.DMA((count,)),
            pltpu.VMEM((r // 2, 128), f32), pltpu.VMEM((r, K), f32), pltpu.VMEM((r, U), f32),
            pltpu.VMEM((8, U), i32), pltpu.VMEM((8, U + K), f32),
        ] + lands,
        compiler_params=pltpu.CompilerParams(
            collective_id=level, has_side_effects=True, vmem_limit_bytes=48 * 2**20
        ),
        cost_estimate=pl.CostEstimate(flops=3 * 10**10, bytes_accessed=150 * 10**6, transcendentals=0),
        name="level%d" % level,
    )(*ins)


def from_partner(shard, stride):
    return lax.ppermute(shard, "cube", [(i, i ^ 1 << stride) for i in range(64)])


def plane_of(owner):
    cube, zh = owner // PANELS, lax.rem(owner, PANELS)
    cls = cube // 16 * 8 + lax.rem(cube, 8)
    return cls, lax.rem(cube // 8, 2) * PANELS + zh


def route_plane(coupling_rows, coupling_owner, coupling_slot):
    cls, z = plane_of(coupling_owner[:, 0])
    m = coupling_rows.shape[0]
    hits = (cls[:, None] == jnp.arange(32, dtype=i32)[None, :]).astype(bf16)
    before = (jnp.arange(m)[:, None] > jnp.arange(m)[None, :]).astype(bf16)
    earlier = jnp.dot(before, hits, preferred_element_type=f32)
    earlier = jnp.sum(earlier * hits.astype(f32), axis=1).astype(i32)
    target = cls * 16 + earlier
    choose = (target[None, :] == jnp.arange(512, dtype=i32)[:, None]).astype(bf16)
    marks = (z * 16 + coupling_slot)[:, None] == jnp.arange(128, dtype=i32)[None, :]
    outgoing = []
    for part in (coupling_rows[:, :PART], coupling_rows[:, PART:]):
        payload = jnp.concatenate([part, marks.astype(bf16)], axis=1)
        chosen = jnp.dot(choose, payload, preferred_element_type=f32).astype(bf16)
        outgoing.append(chosen.reshape(32, 16, PART + 128))
    return outgoing


def body(leaf_updates, extend_maps, front_diagonal, pivot_order, coupling_rows, coupling_owner, coupling_slot):
    r = leaf_updates.shape[0] // 2
    own, incoming = leaf_updates[:r], from_partner(leaf_updates[r:].astype(bf16), 3)
    early_part, late_part = route_plane(coupling_rows, coupling_owner, coupling_slot)
    total = None
    for level in range(3):
        extra = ((early_part,), (late_part, early_part), (total, pivot_order.reshape(1, K), late_part))[level]
        results = eliminate(level, extend_maps, front_diagonal, own, incoming, *extra)
        own, incoming = results[:2]
        if level == 0:
            early_part = results[2]
        elif level == 1:
            late_part, total = results[2:]
    return (incoming, own)


def solution(mesh):
    return jax.shard_map(
        body,
        mesh=mesh,
        in_specs=(
            P(("cube", "panel"), None), P(), P(), P(),
            P(("cube", "panel"), None), P(("cube", "panel"), None), P(("cube", "panel")),
        ),
        out_specs=(P(("cube", "panel"), None), P(("cube", "panel"), None)),
        check_vma=False,
    )
```
